32 devices in a mesh: loop: 8 (over z, core), chan: 4 (over y, x).
Axes of the slice: x: 2, y: 2, z: 4, core: 2. Of those that a mesh axis runs over, the one named last changes fastest.
Arguments:
- features: bfloat16 [32768, 256], P('loop', 'chan'), may hold values from -6 to 6
- kernel_tap_rows: float32 [9, 256], P(None, 'chan'), may hold values from -2 to 2
- in_weight: bfloat16 [256, 1024], replicated, may hold values from -0.375 to 0.375
- out_weight: bfloat16 [1024, 256], replicated, may hold values from -0.1875 to 0.1875
- cotangent: bfloat16 [32768, 256], P('loop', 'chan'), may hold values from -6 to 6
Outputs:
- block_out: bfloat16 [32768, 256], P('loop', 'chan')
- grad_features: bfloat16 [32768, 256], P('loop', 'chan')
- grad_in_weight: float32 [256, 1024], P('chan', 'loop')
- grad_out_weight: float32 [1024, 256], P('loop', 'chan')
- grad_kernel: float32 [9, 256], P(None, 'chan')
The draws below stay inside these ranges and needn't reach their ends.
All inputs are finite; a program needn't handle non-finite values.
Results may differ from the reference program's by a relative error of at most 0.017.
Values may be sent and summed in bfloat16 or wider, within the bound.
A program may use at most 64 MiB of HBM per device.

```python
import math
import jax
import jax.numpy as jnp
from jax import lax

C = 256
F = 1024
TAPS = 9
DILATION_STEP = 512
BASES = 32768


def strengthened(array, rng, source, target, blocks, factor):
    def block_of(position):
        return (jnp.arange(array.shape[position]) // (array.shape[position] // blocks)).reshape((-1,) + (1,) * (array.ndim - 1 - position))

    one_side = jax.random.permutation(rng, blocks)[block_of(target)]
    far = (block_of(target) + blocks // 2) % blocks
    return jnp.where((block_of(source) == one_side) | (block_of(source) == far), factor * array, array)


def levels(stream_key, extent, pieces, smallest, largest):
    def one(position, blocks):
        draws = jax.random.uniform(jax.random.fold_in(jax.random.fold_in(stream_key, 6), position), (blocks,), jnp.float32, smallest / len(pieces), largest / len(pieces))
        return jnp.repeat(jnp.exp(draws), extent[position] // blocks).reshape((-1,) + (1,) * (len(extent) - position - 1))

    gain = one(*pieces[0])
    for cut in pieces[1:]:
        gain = gain * one(*cut)
    return gain


def scatter_about(rng, dims, deviation, bound, cuts=(), dtype=jnp.bfloat16):
    result = jax.random.normal(rng, dims, jnp.float32) * deviation
    if len(cuts) > 0:
        result = levels(rng, dims, cuts, -0.22, 0.18) * result
    return jnp.clip(result, min=-bound, max=bound).astype(dtype)


def gaussian_with(own_key, extent, width, reach, shards, heavy, held_as=jnp.bfloat16):
    entries = width * jax.random.normal(own_key, extent, jnp.float32)
    if shards:
        entries = entries * levels(own_key, extent, shards, -0.22, 0.18)
    return jnp.clip(strengthened(entries, jax.random.fold_in(own_key, 3), *heavy), -reach, reach).astype(held_as)


def setup_inputs(seed: int = 0) -> dict:
    key_of = jax.random.split(jax.random.key(seed), 6)
    return {
        "features": scatter_about(key_of[0], (BASES, C), 1.0, 6.0, ((0, 8), (1, 4))),
        "kernel_tap_rows": scatter_about(key_of[1], (TAPS, C), TAPS ** -0.5, 2.0, ((1, 4),), jnp.float32),
        "in_weight": scatter_about(key_of[2], (C, F), C ** -0.5, 0.375),
        "out_weight": scatter_about(key_of[3], (F, C), F ** -0.5, 0.1875),
        "cotangent": gaussian_with(key_of[4], (BASES, C), 1.0, 6.0, ((0, 8), (1, 4)), (0, 1, 8, 2.0)),
    }


gelu_scale = math.sqrt(2.0 / math.pi)
cubic_coef = 0.044715
epsilon = 1e-05

def gelu_pair(inputs):
    inner_arg = gelu_scale * (inputs + cubic_coef * inputs * inputs * inputs)
    tangent = jnp.tanh(inner_arg)
    act_value = 0.5 * inputs * (1.0 + tangent)
    act_slope = 0.5 * (1.0 + tangent) + 0.5 * inputs * (1.0 - tangent * tangent) * gelu_scale * (1.0 + 3.0 * cubic_coef * inputs * inputs)
    return (act_value, act_slope)

def reference(features, kernel_tap_rows, in_weight, out_weight, cotangent):
    length = features.shape[0]
    middle_position = (TAPS - 1) // 2
    widened_bases = features.astype(jnp.float32)
    blended_sum = jnp.zeros_like(widened_bases)
    for kernel_tap_index in range(TAPS):
        blended_sum = blended_sum + kernel_tap_rows[kernel_tap_index] * jnp.roll(widened_bases, -(kernel_tap_index - middle_position) * DILATION_STEP, axis=0)
    filtered = blended_sum.astype(jnp.bfloat16)
    block_rows = math.gcd(length, 16384)
    block_count = length // block_rows
    filtered_blocks = filtered.reshape(block_count, block_rows, C)
    upstream_blocks = cotangent.reshape(block_count, block_rows, C)

    def step_block(running, row_pair):
        grad_in_sum, grad_out_sum = running
        row_block, upstream = row_pair
        values = row_block.astype(jnp.float32)
        mean_value = lax.optimization_barrier(jnp.mean(values, axis=-1, keepdims=True))
        centred = values - mean_value
        variance = lax.optimization_barrier(jnp.mean(centred * centred, axis=-1, keepdims=True))
        inv_std = lax.rsqrt(variance + epsilon)
        normed = centred * inv_std
        normed_b = normed.astype(jnp.bfloat16)
        hidden_pre = jnp.dot(normed_b, in_weight, preferred_element_type=jnp.float32)
        act_value, act_slope = gelu_pair(hidden_pre)
        act_b = act_value.astype(jnp.bfloat16)
        branch = jnp.dot(act_b, out_weight, preferred_element_type=jnp.float32).astype(jnp.bfloat16)
        grad_act = jnp.dot(upstream, out_weight.T, preferred_element_type=jnp.float32)
        grad_pre = (grad_act * act_slope).astype(jnp.bfloat16)
        grad_normed = jnp.dot(grad_pre, in_weight.T, preferred_element_type=jnp.float32)
        grad_filtered = inv_std * (grad_normed - lax.optimization_barrier(jnp.mean(grad_normed, axis=-1, keepdims=True)) - normed * lax.optimization_barrier(jnp.mean(grad_normed * normed, axis=-1, keepdims=True)))
        back_rows = grad_filtered.astype(jnp.bfloat16)
        grad_in_sum = grad_in_sum + jnp.dot(normed_b.T, grad_pre, preferred_element_type=jnp.float32)
        grad_out_sum = grad_out_sum + jnp.dot(act_b.T, upstream, preferred_element_type=jnp.float32)
        return ((grad_in_sum, grad_out_sum), (branch, back_rows))
    start_sums = (jnp.zeros((C, F), jnp.float32), jnp.zeros((F, C), jnp.float32))
    (grad_in_sum, grad_out_sum), (branch, back_rows) = lax.scan(step_block, start_sums, (filtered_blocks, upstream_blocks))
    branch = branch.reshape(length, C)
    block_out = (widened_bases + branch.astype(jnp.float32)).astype(jnp.bfloat16)
    back_wide = back_rows.reshape(length, C).astype(jnp.float32)
    grad_sum_rows = cotangent.astype(jnp.float32)
    kernel_rows = []
    for kernel_tap_index in range(TAPS):
        shift_positions = (kernel_tap_index - middle_position) * DILATION_STEP
        grad_sum_rows = grad_sum_rows + kernel_tap_rows[kernel_tap_index] * jnp.roll(back_wide, shift_positions, axis=0)
        kernel_rows.append(lax.optimization_barrier(jnp.sum(back_wide * jnp.roll(widened_bases, -shift_positions, axis=0), axis=0)))
    grad_scale = 1.0 / math.sqrt(length)
    grad_kernel = jnp.stack(kernel_rows) * grad_scale
    return (block_out, grad_sum_rows.astype(jnp.bfloat16), grad_in_sum * grad_scale, grad_out_sum * grad_scale, grad_kernel)
```

```python
import functools
import math

import jax
import jax.numpy as jnp
from jax import lax
from jax.experimental import pallas as pl
from jax.experimental.pallas import tpu as pltpu
from jax.sharding import PartitionSpec as P

TAPS = 9
DILATION_STEP = 512


gelu_scale = math.sqrt(2.0 / math.pi)
cubic_coef = 0.044715
epsilon = 1e-05


def with_halo(cells, sides, width):
    for axis, dim in sides:
        count = lax.axis_size(axis)
        head = lax.slice_in_dim(cells, 0, width, axis=dim)
        tail = lax.slice_in_dim(cells, cells.shape[dim] - width, cells.shape[dim], axis=dim)
        cells = jnp.concatenate(
            [
                lax.ppermute(tail, axis, [(i, (i + 1) % count) for i in range(count)]),
                cells,
                lax.ppermute(head, axis, [((i + 1) % count, i) for i in range(count)]),
            ],
            axis=dim,
        )
    return cells


def gelu_pair(inputs):
    inner_arg = gelu_scale * (inputs + cubic_coef * inputs * inputs * inputs)
    tangent = jnp.tanh(inner_arg)
    act_value = 0.5 * inputs * (1.0 + tangent)
    act_slope = 0.5 * (1.0 + tangent) + 0.5 * inputs * (1.0 - tangent * tangent) * gelu_scale * (
        1.0 + 3.0 * cubic_coef * inputs * inputs
    )
    return (act_value, act_slope)


def widen_rows(field_rows, reach_positions):
    return with_halo(field_rows, (("loop", 0),), reach_positions)


def shards(features, kernel_tap_rows, in_weight, out_weight, cotangent):
    middle_position = (TAPS - 1) // 2
    reach_positions = middle_position * DILATION_STEP
    loop_size = lax.axis_size("loop")
    chan_size = lax.axis_size("chan")
    rows_here = features.shape[0]
    grad_scale = 1.0 / math.sqrt(rows_here * loop_size)
    padded_in = widen_rows(features, reach_positions)
    blended_sum = jnp.zeros(features.shape, jnp.float32)
    for kernel_tap_index in range(TAPS):
        leading_row = reach_positions + (kernel_tap_index - middle_position) * DILATION_STEP
        blended_sum = blended_sum + kernel_tap_rows[kernel_tap_index] * padded_in[
            leading_row : leading_row + rows_here
        ].astype(jnp.float32)
    filtered = blended_sum.astype(jnp.bfloat16)
    row_block, upstream = (
        lax.all_to_all(filtered, "chan", split_axis=0, concat_axis=1, tiled=True),
        lax.all_to_all(cotangent, "chan", split_axis=0, concat_axis=1, tiled=True),
    )
    values = row_block.astype(jnp.float32)
    mean_value = jnp.mean(values, axis=-1, keepdims=True)
    centred = values - mean_value
    variance = jnp.mean(centred * centred, axis=-1, keepdims=True)
    inv_std = lax.rsqrt(variance + epsilon)
    normed = centred * inv_std
    normed_b = normed.astype(jnp.bfloat16)
    hidden_pre = jnp.dot(normed_b, in_weight, preferred_element_type=jnp.float32)
    act_value, act_slope = gelu_pair(hidden_pre)
    act_b = act_value.astype(jnp.bfloat16)
    branch = jnp.dot(act_b, out_weight, preferred_element_type=jnp.float32).astype(jnp.bfloat16)
    grad_act = jnp.einsum("pc,fc->pf", upstream, out_weight, preferred_element_type=jnp.float32)
    grad_pre = (grad_act * act_slope).astype(jnp.bfloat16)
    grad_normed = jnp.einsum("pf,cf->pc", grad_pre, in_weight, preferred_element_type=jnp.float32)
    grad_filtered = inv_std * (
        grad_normed
        - jnp.mean(grad_normed, axis=-1, keepdims=True)
        - normed * jnp.mean(grad_normed * normed, axis=-1, keepdims=True)
    )
    back_rows = grad_filtered.astype(jnp.bfloat16)
    local_rows = row_block.shape[0]
    width_c = row_block.shape[1]
    width_f = hidden_pre.shape[1]
    chan_part = width_c // chan_size
    loop_part = width_f // loop_size
    normed_parts = normed_b.reshape(local_rows, chan_size, chan_part)
    upstream_parts = upstream.reshape(local_rows, chan_size, chan_part)
    grad_parts = grad_pre.reshape(local_rows, loop_size, loop_part)
    act_parts = act_b.reshape(local_rows, loop_size, loop_part)
    term_in = (
        jnp.einsum("pai,pbj->baij", normed_parts, grad_parts, preferred_element_type=jnp.float32)
        * grad_scale
    )
    term_out = (
        jnp.einsum("pbj,pai->baji", act_parts, upstream_parts, preferred_element_type=jnp.float32)
        * grad_scale
    )
    branch_cols, back_cols = (
        lax.all_to_all(branch, "chan", split_axis=1, concat_axis=0, tiled=True),
        lax.all_to_all(back_rows, "chan", split_axis=1, concat_axis=0, tiled=True),
    )
    block_out = (features.astype(jnp.float32) + branch_cols.astype(jnp.float32)).astype(
        jnp.bfloat16
    )
    first_in, first_out = (
        lax.psum_scatter(
            term_in.astype(jnp.bfloat16), "chan", scatter_dimension=1, tiled=True
        ).astype(jnp.float32),
        lax.psum_scatter(
            term_out.astype(jnp.bfloat16), "chan", scatter_dimension=1, tiled=True
        ).astype(jnp.float32),
    )
    summed_in, summed_out = (
        lax.psum_scatter(first_in, "loop", scatter_dimension=0, tiled=True),
        lax.psum_scatter(first_out, "loop", scatter_dimension=0, tiled=True),
    )
    grad_in_weight = summed_in.reshape(chan_part, loop_part)
    grad_out_weight = summed_out.reshape(loop_part, chan_part)
    padded_back = widen_rows(back_cols, reach_positions)
    grad_sum_rows = cotangent.astype(jnp.float32)
    back_wide = back_cols.astype(jnp.float32)
    kernel_rows = []
    for kernel_tap_index in range(TAPS):
        shift_positions = (kernel_tap_index - middle_position) * DILATION_STEP
        first_back = reach_positions - shift_positions
        grad_sum_rows = grad_sum_rows + kernel_tap_rows[kernel_tap_index] * padded_back[
            first_back : first_back + rows_here
        ].astype(jnp.float32)
        first_in_row = reach_positions + shift_positions
        kernel_rows.append(
            jnp.sum(
                back_wide * padded_in[first_in_row : first_in_row + rows_here].astype(jnp.float32),
                axis=0,
            )
        )
    kernel_terms = jnp.stack(kernel_rows) * grad_scale
    grad_kernel = lax.psum(kernel_terms, "loop")
    return (
        block_out,
        grad_sum_rows.astype(jnp.bfloat16),
        grad_in_weight,
        grad_out_weight,
        grad_kernel,
    )


MESH = pl.DeviceIdType.MESH
MIDDLE = (TAPS - 1) // 2
HBM = pltpu.MemorySpace.HBM


def fused_kernel(
    L, J, grad_scale,
    x_hbm, ct_hbm, taps_hbm, win_hbm, wout_hbm,
    bo_out, gx_out, gw_in_out, gw_out_out, gk_out,
    xp, ctv, tapv, win, wout, wint, woutt, tf, fb, fr, ctf, nb, nrm, istd, act, gp,
    geb, brb, gep, brv, gfull, gsend, grecv, hf, hs, hr, sf, sb, tr, gka, kt,
    load, send, recv,
):
    cl, rows = ctv.shape
    C, F = win.shape
    B = DILATION_STEP
    K = rows // B
    S = K // 2
    W = 2 * B // J
    Z = L // 2
    own = MIDDLE * B
    bf, f32 = jnp.bfloat16, jnp.float32
    me_l, me_j = lax.axis_index("loop"), lax.axis_index("chan")
    core, z = lax.rem(me_l, 2), me_l // 2
    used = [0]

    def take(n=1):
        used[0] += n
        return used[0] - n

    def rcopy(src, dst, idx, l, j):
        return pltpu.make_async_remote_copy(
            src_ref=src, dst_ref=dst, send_sem=send.at[idx], recv_sem=recv.at[idx],
            device_id=(l, j), device_id_type=MESH)

    def lanes(at, n):
        return pl.ds(pl.multiple_of(at, 128), n)

    loads = [pltpu.make_async_copy(a, b, load.at[i]) for i, (a, b) in enumerate((
        (x_hbm, xp.at[:, own:own + rows]), (ct_hbm, ctv), (taps_hbm, tapv), (win_hbm, win), (wout_hbm, wout)))]
    for c in loads:
        c.start()

    chan_peers = [lax.rem(me_j + d, J) for d in range(1, J)]
    loop_peers = [lax.rem(me_l + e, L) for e in range(1, L)]
    right, left = loop_peers[0], loop_peers[-1]

    barrier = pltpu.get_barrier_semaphore()
    for j in chan_peers:
        pl.semaphore_signal(barrier, inc=1, device_id=(me_l, j), device_id_type=MESH)
    for l in loop_peers:
        pl.semaphore_signal(barrier, inc=1, device_id=(l, me_j), device_id_type=MESH)

    half = J // 2
    mine = pl.ds(pl.multiple_of(me_j * cl, cl), cl)

    def col(s, j):
        return lanes((S - 1 - s + (j // half) * (1 + 2 * s)) * B + lax.rem(j, half) * W, W)

    def own_col(s, j):
        return lanes(own + (S - 1 - s + (j // half) * (1 + 2 * s)) * B + lax.rem(j, half) * W, W)

    def block(k):
        return lanes(k * B, B)

    def chan_rows(j):
        return pl.ds(pl.multiple_of(j * cl, cl), cl)

    ct_base, f_base = take(S * (J - 1)), take(S * (J - 1))
    ge_base, br_base = take(S * (J - 1)), take(S * (J - 1))
    xh_base, gh_base = take(S * 2), take(S * 2)
    core_base = take(Z)

    def ct_copies(s):
        return [rcopy(ctv.at[:, col(s, j)], ctf.at[s, mine, :], ct_base + s * (J - 1) + d, me_l, j)
                for d, j in enumerate(chan_peers)]

    def f_copies(s):
        return [rcopy(fb.at[:, col(s, j)], fr.at[s, mine, :], f_base + s * (J - 1) + d, me_l, j)
                for d, j in enumerate(chan_peers)]

    def ge_copies(s):
        return [rcopy(geb.at[s, chan_rows(j), :], gep.at[:, own_col(s, me_j)], ge_base + s * (J - 1) + d, me_l, j)
                for d, j in enumerate(chan_peers)]

    def br_copies(s):
        return [rcopy(brb.at[s, chan_rows(j), :], brv.at[:, col(s, me_j)], br_base + s * (J - 1) + d, me_l, j)
                for d, j in enumerate(chan_peers)]

    def halo_copies(buf, right_block, left_block, base):
        return [rcopy(buf.at[:, block(right_block + S)], buf.at[:, block(right_block - S)], base, right, me_j),
                rcopy(buf.at[:, block(left_block + S)], buf.at[:, block(left_block + K + S)], base + 1, left, me_j)]

    def xh_copies(s):
        return halo_copies(xp, K - 1 - s, s, xh_base + 2 * s)

    def gh_copies(s):
        return halo_copies(gep, S + s, S - 1 - s, gh_base + 2 * s)

    def start(copies):
        for c in copies:
            c.start()

    def arrive(copies):
        for c in copies:
            c.wait_recv()

    loads[0].wait()
    loads[1].wait()
    pl.semaphore_wait(barrier, J - 1 + L - 1)
    for s in range(S):
        start(xh_copies(s))
    for s in range(S - 1):
        start(ct_copies(s))

    for c in loads[2:]:
        c.wait()
    padded = jnp.concatenate([tapv[...], jnp.zeros((128 - TAPS, cl), f32)], axis=0)
    columns = jnp.concatenate([padded, jnp.zeros((128, 128 - cl), f32)], axis=1).T
    for t in range(TAPS):
        tf[t] = jnp.broadcast_to(columns[0:cl, t:t + 1], (cl, 128))
    wint[...] = win[...].T
    woutt[...] = wout[...].T
    gka[...] = jnp.zeros(gka.shape, f32)
    for s in range(S):
        ctf[s, mine, :] = ctv[:, col(s, me_j)]

    def conv_body(s, carry):
        arrive(xh_copies(s))
        for g in range(cl // 16):
            ch = slice(g * 16, (g + 1) * 16)
            w = [tf[t, ch, :] for t in range(TAPS)]
            for k in (S - 1 - s, S + s):
                for q in range(B // 128):
                    acc = jnp.zeros((16, 128), f32)
                    for t in range(TAPS):
                        acc = acc + w[t] * xp[ch, lanes((k + t) * B + q * 128, 128)].astype(f32)
                    fb[ch, lanes(k * B + q * 128, 128)] = acc.astype(bf)
        start(f_copies(s))
        fr[s, mine, :] = fb[:, col(s, me_j)]

        @pl.when(s == 0)
        def _():
            start(ct_copies(S - 1))
        return carry

    lax.fori_loop(0, S, conv_body, 0)

    def mlp_body(s, carry):
        arrive(ct_copies(s))
        arrive(f_copies(s))
        here = lanes(s * W, W)
        for b in range(W // 128):
            part = slice(b * 128, (b + 1) * 128)
            v = fr[s, :, part].astype(f32)
            centred = v - jnp.mean(v, axis=0, keepdims=True)
            inv = lax.rsqrt(jnp.mean(centred * centred, axis=0, keepdims=True) + epsilon)
            normed = centred * inv
            nrm[:, part] = normed
            istd[:, part] = inv
            nb[:, lanes(s * W + b * 128, 128)] = normed.astype(bf)
        normed_b = nb[:, here]
        up = ctf[s]
        FC = 256
        for f in range(F // FC):
            part = slice(f * FC, (f + 1) * FC)
            pre = jnp.dot(wint[part, :], normed_b, preferred_element_type=f32)
            ga = jnp.dot(wout[part, :], up, preferred_element_type=f32)
            sq = pre * pre
            tangent = jnp.tanh(pre * (gelu_scale + (gelu_scale * cubic_coef) * sq))
            gate = 0.5 + 0.5 * tangent
            slope = gate + pre * (gate * (1.0 - tangent)) * (gelu_scale + (3.0 * gelu_scale * cubic_coef) * sq)
            act[part, here] = (pre * gate).astype(bf)
            gp[part, here] = (ga * slope).astype(bf)
        gn = jnp.dot(win[...], gp[:, here], preferred_element_type=f32)
        for b in range(W // 128):
            part = slice(b * 128, (b + 1) * 128)
            g, normed = gn[:, part], nrm[:, part]
            out = istd[:, part] * (g - jnp.mean(g, axis=0, keepdims=True)
                                   - normed * jnp.mean(g * normed, axis=0, keepdims=True))
            geb[s, :, part] = out.astype(bf)
        start(ge_copies(s))
        gep[:, own_col(s, me_j)] = geb[s, mine, :]
        brb[s] = jnp.dot(woutt[...], act[:, here], preferred_element_type=f32).astype(bf)
        brv[:, col(s, me_j)] = brb[s, mine, :]

        @pl.when(s == 1)
        def _():
            start(br_copies(0))
        return carry

    lax.fori_loop(0, S, mlp_body, 0)

    def forward(s):
        arrive(ge_copies(s))
        start(gh_copies(s))

    def kernel_terms(s):
        for g in range(cl // 16):
            ch = slice(g * 16, (g + 1) * 16)
            sums = [gka[t, ch, :] for t in range(TAPS)]
            for k in (S - 1 - s, S + s):
                for q in range(B // 128):
                    e = gep[ch, lanes(own + k * B + q * 128, 128)].astype(f32)
                    for t in range(TAPS):
                        sums[t] = sums[t] + e * xp[ch, lanes((k + t) * B + q * 128, 128)].astype(f32)
            for t in range(TAPS):
                gka[t, ch, :] = sums[t]

    forward(0)

    def term_body(zz, carry):
        cols = lanes(zz * 256, 256)
        both = jnp.concatenate([ctf[s] for s in range(S)], axis=1)
        for i, (a, b) in enumerate(((nb[...], gp), (both, act))):
            term = lax.dot_general(a, b[cols, :], (((1,), (1,)), ((), ())), preferred_element_type=f32) * grad_scale
            for h in range(2):
                part = term[:, h * 128:(h + 1) * 128]
                gfull[h, zz, i] = part
                gsend[h, zz, i] = part.astype(bf)
        rcopy(gsend.at[1 - core, zz], grecv.at[zz], core_base + zz, z * 2 + 1 - core, me_j).start()
        return carry

    lax.fori_loop(0, Z, term_body, 0)
    forward(1)
    start(br_copies(1))

    CR = C // J

    def core_sum(zz, carry):
        c = rcopy(gsend.at[1 - core, zz], grecv.at[zz], core_base + zz, z * 2 + 1 - core, me_j)
        c.wait_recv()
        c.wait_send()
        for i in range(2):
            h = gfull[core, zz, i] + grecv[zz, i].astype(f32)
            for j in range(J):
                hf[j, zz, i] = h[j * CR:(j + 1) * CR]
                hs[j, zz, i] = h[j * CR:(j + 1) * CR].astype(bf)
        return carry

    lax.fori_loop(0, Z, core_sum, 0)
    h_in = [rcopy(hs.at[j], hr.at[me_j], take(), me_l, j) for j in chan_peers]
    start(h_in)
    start(br_copies(2))
    start(br_copies(3))

    def early_terms(s, carry):
        kernel_terms(s)
        return carry

    def late_terms(s, carry):
        forward(s)
        kernel_terms(s)
        return carry

    lax.fori_loop(0, 2, early_terms, 0)
    lax.fori_loop(2, S, late_terms, 0)
    sums = [jnp.sum(gka[t], axis=1, keepdims=True) * grad_scale for t in range(TAPS)]
    total = jnp.concatenate(sums + [jnp.zeros((cl, 128 - TAPS), f32)], axis=1)
    total = jnp.concatenate([total, jnp.zeros((128 - cl, 128), f32)], axis=0).T
    kt[me_l] = total[0:16]
    kt_in = [rcopy(kt.at[me_l], kt.at[me_l], take(), l, me_j) for l in loop_peers]
    start(kt_in)

    for s in range(S):
        arrive(gh_copies(s))

    def back_body(k, carry):
        for g in range(cl // 16):
            ch = slice(g * 16, (g + 1) * 16)
            w = [tf[t, ch, :] for t in range(TAPS)]
            for q in range(B // 128):
                at = lanes(k * B + q * 128, 128)
                acc = ctv[ch, at].astype(f32)
                for t in range(TAPS):
                    acc = acc + w[t] * gep[ch, lanes((k + TAPS - 1 - t) * B + q * 128, 128)].astype(f32)
                gx_out[ch, at] = acc.astype(bf)
        return carry

    lax.fori_loop(0, K, back_body, 0)

    arrive(h_in)
    for zz in range(Z):
        total = hf[me_j, zz]
        for d in range(1, J):
            total = total + hr[lax.rem(me_j + J - d, J), zz].astype(f32)
        sf[zz] = total
        sb[zz] = total.astype(bf)
    z_in = []
    for e in range(1, Z):
        zz = lax.rem(z + e, Z)
        z_in.append(rcopy(sb.at[zz], tr.at[z], take(), zz * 2 + core, me_j))
    start(z_in)

    def finish(s, carry):
        arrive(br_copies(s))
        for k in (S - 1 - s, S + s):
            bo_out[:, block(k)] = (xp[:, block(k + S)].astype(f32) + brv[:, block(k)].astype(f32)).astype(bf)
        return carry

    lax.fori_loop(0, S, finish, 0)
    arrive(kt_in)
    total = kt[0]
    for l in range(1, L):
        total = total + kt[l]
    gk_out[...] = total[0:TAPS, 0:cl]
    arrive(z_in)
    total = sf[z]
    for e in range(1, Z):
        total = total + tr[lax.rem(z + Z - e, Z)].astype(f32)
    gw_in_out[...] = total[0]
    gw_out_out[...] = total[1]

    def sent(s, carry):
        for copies in (ct_copies(s), f_copies(s), ge_copies(s), br_copies(s), xh_copies(s), gh_copies(s)):
            for c in copies:
                c.wait_send()
        return carry

    lax.fori_loop(0, S, sent, 0)
    for c in h_in + kt_in + z_in:
        c.wait_send()


def flush_kernel(*refs):
    n = len(refs) // 2
    sems = refs[2 * n]
    copies = [pltpu.make_async_copy(refs[i], refs[n + i], sems.at[i]) for i in range(n)]
    for c in copies:
        c.start()
    for c in copies:
        c.wait()


def fits(L, J, rows, cl, F):
    return (cl * 2 == 128 and rows == 2 * MIDDLE * DILATION_STEP and L % 2 == 0 and L > 2 and J == 4
            and F == L * 128)


def fused_shards(features, kernel_tap_rows, in_weight, out_weight, cotangent):
    L, J = lax.axis_size("loop"), lax.axis_size("chan")
    rows, cl = features.shape
    C, F = in_weight.shape
    if not fits(L, J, rows, cl, F):
        return shards(features, kernel_tap_rows, in_weight, out_weight, cotangent)
    N = rows // J
    K = rows // DILATION_STEP
    S = K // 2
    W = N // S
    Z = L // 2
    CR = C // J
    bf, f32 = jnp.bfloat16, jnp.float32
    ext = rows + 2 * MIDDLE * DILATION_STEP
    scratch = [
        pltpu.VMEM((cl, ext), bf),
        pltpu.VMEM((cl, rows), bf),
        pltpu.VMEM((TAPS, cl), f32),
        pltpu.VMEM((C, F), bf),
        pltpu.VMEM((F, C), bf),
        pltpu.VMEM((F, C), bf),
        pltpu.VMEM((C, F), bf),
        pltpu.VMEM((TAPS, cl, 128), f32),
        pltpu.VMEM((cl, rows), bf),
        pltpu.VMEM((S, C, W), bf),
        pltpu.VMEM((S, C, W), bf),
        pltpu.VMEM((C, N), bf),
        pltpu.VMEM((C, W), f32),
        pltpu.VMEM((1, W), f32),
        pltpu.VMEM((F, N), bf),
        pltpu.VMEM((F, N), bf),
        pltpu.VMEM((S, C, W), bf),
        pltpu.VMEM((S, C, W), bf),
        pltpu.VMEM((cl, ext), bf),
        pltpu.VMEM((cl, rows), bf),
        pltpu.VMEM((2, Z, 2, C, 128), f32),
        pltpu.VMEM((2, Z, 2, C, 128), bf),
        pltpu.VMEM((Z, 2, C, 128), bf),
        pltpu.VMEM((J, Z, 2, CR, 128), f32),
        pltpu.VMEM((J, Z, 2, CR, 128), bf),
        pltpu.VMEM((J, Z, 2, CR, 128), bf),
        pltpu.VMEM((Z, 2, CR, 128), f32),
        pltpu.VMEM((Z, 2, CR, 128), bf),
        pltpu.VMEM((Z, 2, CR, 128), bf),
        pltpu.VMEM((TAPS, cl, 128), f32),
        pltpu.VMEM((L, 16, 128), f32),
    ]
    copies = 4 * S * (J - 1) + 4 * S + Z + (J - 1) + (L - 1) + (Z - 1)
    scratch += [pltpu.SemaphoreType.DMA((5,)), pltpu.SemaphoreType.DMA((copies,)), pltpu.SemaphoreType.DMA((copies,))]
    vmem = pl.BlockSpec(memory_space=pltpu.VMEM)
    hbm = pl.BlockSpec(memory_space=HBM)
    shapes = (
        jax.ShapeDtypeStruct((cl, rows), bf),
        jax.ShapeDtypeStruct((cl, rows), bf),
        jax.ShapeDtypeStruct((CR, F // L), f32),
        jax.ShapeDtypeStruct((CR, F // L), f32),
        jax.ShapeDtypeStruct((TAPS, cl), f32),
    )
    results = pl.pallas_call(
        functools.partial(fused_kernel, L, J, 1.0 / math.sqrt(rows * L)),
        out_shape=shapes,
        in_specs=[hbm] * 5,
        out_specs=(vmem,) * 5,
        scratch_shapes=scratch,
        compiler_params=pltpu.CompilerParams(
            collective_id=0, has_side_effects=True, vmem_limit_bytes=62 * 1024 * 1024),
        cost_estimate=pl.CostEstimate(flops=12 * N * C * F, bytes_accessed=8 * rows * cl * 2, transcendentals=N * F),
    )(features.T, cotangent.T, kernel_tap_rows, in_weight, out_weight)
    bo, gx, gw_in, gw_out, gk = pl.pallas_call(
        flush_kernel,
        out_shape=shapes,
        in_specs=[pl.BlockSpec(memory_space=pl.ANY)] * 5,
        out_specs=(hbm,) * 5,
        scratch_shapes=[pltpu.SemaphoreType.DMA((5,))],
    )(*results)
    return bo.T, gx.T, gw_in, gw_out.T, gk


def solution(mesh):
    placed = (P("loop", "chan"), P(None, "chan"), P(), P(), P("loop", "chan"))
    return jax.shard_map(
        fused_shards,
        mesh=mesh,
        in_specs=placed,
        out_specs=(
            P("loop", "chan"),
            P("loop", "chan"),
            P("chan", "loop"),
            P("loop", "chan"),
            P(None, "chan"),
        ),
        check_vma=False,
    )
```

```python
import functools
import math

import jax
import jax.numpy as jnp
from jax import lax
from jax.experimental import pallas as pl
from jax.experimental.pallas import tpu as pltpu
from jax.sharding import PartitionSpec as P

TAPS = 9
DILATION_STEP = 512


gelu_scale = math.sqrt(2.0 / math.pi)
cubic_coef = 0.044715
epsilon = 1e-05


def with_halo(cells, sides, width):
    for axis, dim in sides:
        count = lax.axis_size(axis)
        head = lax.slice_in_dim(cells, 0, width, axis=dim)
        tail = lax.slice_in_dim(cells, cells.shape[dim] - width, cells.shape[dim], axis=dim)
        cells = jnp.concatenate(
            [
                lax.ppermute(tail, axis, [(i, (i + 1) % count) for i in range(count)]),
                cells,
                lax.ppermute(head, axis, [((i + 1) % count, i) for i in range(count)]),
            ],
            axis=dim,
        )
    return cells


def gelu_pair(inputs):
    inner_arg = gelu_scale * (inputs + cubic_coef * inputs * inputs * inputs)
    tangent = jnp.tanh(inner_arg)
    act_value = 0.5 * inputs * (1.0 + tangent)
    act_slope = 0.5 * (1.0 + tangent) + 0.5 * inputs * (1.0 - tangent * tangent) * gelu_scale * (
        1.0 + 3.0 * cubic_coef * inputs * inputs
    )
    return (act_value, act_slope)


def widen_rows(field_rows, reach_positions):
    return with_halo(field_rows, (("loop", 0),), reach_positions)


def shards(features, kernel_tap_rows, in_weight, out_weight, cotangent):
    middle_position = (TAPS - 1) // 2
    reach_positions = middle_position * DILATION_STEP
    loop_size = lax.axis_size("loop")
    chan_size = lax.axis_size("chan")
    rows_here = features.shape[0]
    grad_scale = 1.0 / math.sqrt(rows_here * loop_size)
    padded_in = widen_rows(features, reach_positions)
    blended_sum = jnp.zeros(features.shape, jnp.float32)
    for kernel_tap_index in range(TAPS):
        leading_row = reach_positions + (kernel_tap_index - middle_position) * DILATION_STEP
        blended_sum = blended_sum + kernel_tap_rows[kernel_tap_index] * padded_in[
            leading_row : leading_row + rows_here
        ].astype(jnp.float32)
    filtered = blended_sum.astype(jnp.bfloat16)
    row_block, upstream = (
        lax.all_to_all(filtered, "chan", split_axis=0, concat_axis=1, tiled=True),
        lax.all_to_all(cotangent, "chan", split_axis=0, concat_axis=1, tiled=True),
    )
    values = row_block.astype(jnp.float32)
    mean_value = jnp.mean(values, axis=-1, keepdims=True)
    centred = values - mean_value
    variance = jnp.mean(centred * centred, axis=-1, keepdims=True)
    inv_std = lax.rsqrt(variance + epsilon)
    normed = centred * inv_std
    normed_b = normed.astype(jnp.bfloat16)
    hidden_pre = jnp.dot(normed_b, in_weight, preferred_element_type=jnp.float32)
    act_value, act_slope = gelu_pair(hidden_pre)
    act_b = act_value.astype(jnp.bfloat16)
    branch = jnp.dot(act_b, out_weight, preferred_element_type=jnp.float32).astype(jnp.bfloat16)
    grad_act = jnp.einsum("pc,fc->pf", upstream, out_weight, preferred_element_type=jnp.float32)
    grad_pre = (grad_act * act_slope).astype(jnp.bfloat16)
    grad_normed = jnp.einsum("pf,cf->pc", grad_pre, in_weight, preferred_element_type=jnp.float32)
    grad_filtered = inv_std * (
        grad_normed
        - jnp.mean(grad_normed, axis=-1, keepdims=True)
        - normed * jnp.mean(grad_normed * normed, axis=-1, keepdims=True)
    )
    back_rows = grad_filtered.astype(jnp.bfloat16)
    local_rows = row_block.shape[0]
    width_c = row_block.shape[1]
    width_f = hidden_pre.shape[1]
    chan_part = width_c // chan_size
    loop_part = width_f // loop_size
    normed_parts = normed_b.reshape(local_rows, chan_size, chan_part)
    upstream_parts = upstream.reshape(local_rows, chan_size, chan_part)
    grad_parts = grad_pre.reshape(local_rows, loop_size, loop_part)
    act_parts = act_b.reshape(local_rows, loop_size, loop_part)
    term_in = (
        jnp.einsum("pai,pbj->baij", normed_parts, grad_parts, preferred_element_type=jnp.float32)
        * grad_scale
    )
    term_out = (
        jnp.einsum("pbj,pai->baji", act_parts, upstream_parts, preferred_element_type=jnp.float32)
        * grad_scale
    )
    branch_cols, back_cols = (
        lax.all_to_all(branch, "chan", split_axis=1, concat_axis=0, tiled=True),
        lax.all_to_all(back_rows, "chan", split_axis=1, concat_axis=0, tiled=True),
    )
    block_out = (features.astype(jnp.float32) + branch_cols.astype(jnp.float32)).astype(
        jnp.bfloat16
    )
    first_in, first_out = (
        lax.psum_scatter(
            term_in.astype(jnp.bfloat16), "chan", scatter_dimension=1, tiled=True
        ).astype(jnp.float32),
        lax.psum_scatter(
            term_out.astype(jnp.bfloat16), "chan", scatter_dimension=1, tiled=True
        ).astype(jnp.float32),
    )
    summed_in, summed_out = (
        lax.psum_scatter(first_in, "loop", scatter_dimension=0, tiled=True),
        lax.psum_scatter(first_out, "loop", scatter_dimension=0, tiled=True),
    )
    grad_in_weight = summed_in.reshape(chan_part, loop_part)
    grad_out_weight = summed_out.reshape(loop_part, chan_part)
    padded_back = widen_rows(back_cols, reach_positions)
    grad_sum_rows = cotangent.astype(jnp.float32)
    back_wide = back_cols.astype(jnp.float32)
    kernel_rows = []
    for kernel_tap_index in range(TAPS):
        shift_positions = (kernel_tap_index - middle_position) * DILATION_STEP
        first_back = reach_positions - shift_positions
        grad_sum_rows = grad_sum_rows + kernel_tap_rows[kernel_tap_index] * padded_back[
            first_back : first_back + rows_here
        ].astype(jnp.float32)
        first_in_row = reach_positions + shift_positions
        kernel_rows.append(
            jnp.sum(
                back_wide * padded_in[first_in_row : first_in_row + rows_here].astype(jnp.float32),
                axis=0,
            )
        )
    kernel_terms = jnp.stack(kernel_rows) * grad_scale
    grad_kernel = lax.psum(kernel_terms, "loop")
    return (
        block_out,
        grad_sum_rows.astype(jnp.bfloat16),
        grad_in_weight,
        grad_out_weight,
        grad_kernel,
    )


MESH = pl.DeviceIdType.MESH
MIDDLE = (TAPS - 1) // 2
HBM = pltpu.MemorySpace.HBM


def fused_kernel(
    L, J, grad_scale,
    x_hbm, ct_hbm, taps_hbm, win_hbm, wout_hbm,
    bo_out, gx_out, gw_in_out, gw_out_out, gk_out,
    xp, ctv, tapv, win, wout, wint, woutt, tf, fb, fr, ctf, nb, nrm, istd, act, gp,
    geb, brb, gep, brv, gfull, gsend, grecv, hf, hs, hr, sf, sb, tr, gka, kt,
    load, send, recv,
):
    cl, rows = ctv.shape
    C, F = win.shape
    B = DILATION_STEP
    K = rows // B
    S = K // 2
    W = 2 * B // J
    Z = L // 2
    own = MIDDLE * B
    bf, f32 = jnp.bfloat16, jnp.float32
    me_l, me_j = lax.axis_index("loop"), lax.axis_index("chan")
    core, z = lax.rem(me_l, 2), me_l // 2
    used = [0]

    def take(n=1):
        used[0] += n
        return used[0] - n

    def rcopy(src, dst, idx, l, j):
        return pltpu.make_async_remote_copy(
            src_ref=src, dst_ref=dst, send_sem=send.at[idx], recv_sem=recv.at[idx],
            device_id=(l, j), device_id_type=MESH)

    def lanes(at, n):
        return pl.ds(pl.multiple_of(at, 128), n)

    loads = [pltpu.make_async_copy(a, b, load.at[i]) for i, (a, b) in enumerate((
        (x_hbm, xp.at[:, own:own + rows]), (ct_hbm, ctv), (taps_hbm, tapv), (win_hbm, win), (wout_hbm, wout)))]
    for c in loads:
        c.start()

    chan_peers = [lax.rem(me_j + d, J) for d in range(1, J)]
    loop_peers = [lax.rem(me_l + e, L) for e in range(1, L)]
    right, left = loop_peers[0], loop_peers[-1]

    barrier = pltpu.get_barrier_semaphore()
    for j in chan_peers:
        pl.semaphore_signal(barrier, inc=1, device_id=(me_l, j), device_id_type=MESH)
    for l in loop_peers:
        pl.semaphore_signal(barrier, inc=1, device_id=(l, me_j), device_id_type=MESH)

    half = J // 2
    mine = pl.ds(pl.multiple_of(me_j * cl, cl), cl)

    def col(s, j):
        return lanes((S - 1 - s + (j // half) * (1 + 2 * s)) * B + lax.rem(j, half) * W, W)

    def own_col(s, j):
        return lanes(own + (S - 1 - s + (j // half) * (1 + 2 * s)) * B + lax.rem(j, half) * W, W)

    def block(k):
        return lanes(k * B, B)

    def chan_rows(j):
        return pl.ds(pl.multiple_of(j * cl, cl), cl)

    ct_base, f_base = take(S * (J - 1)), take(S * (J - 1))
    ge_base, br_base = take(S * (J - 1)), take(S * (J - 1))
    xh_base, gh_base = take(S * 2), take(S * 2)
    core_base = take(Z)

    def ct_copies(s):
        return [rcopy(ctv.at[:, col(s, j)], ctf.at[s, mine, :], ct_base + s * (J - 1) + d, me_l, j)
                for d, j in enumerate(chan_peers)]

    def f_copies(s):
        return [rcopy(fb.at[:, col(s, j)], fr.at[s, mine, :], f_base + s * (J - 1) + d, me_l, j)
                for d, j in enumerate(chan_peers)]

    def ge_copies(s):
        return [rcopy(geb.at[s, chan_rows(j), :], gep.at[:, own_col(s, me_j)], ge_base + s * (J - 1) + d, me_l, j)
                for d, j in enumerate(chan_peers)]

    def br_copies(s):
        return [rcopy(brb.at[s, chan_rows(j), :], brv.at[:, col(s, me_j)], br_base + s * (J - 1) + d, me_l, j)
                for d, j in enumerate(chan_peers)]

    def halo_copies(buf, right_block, left_block, base):
        return [rcopy(buf.at[:, block(right_block + S)], buf.at[:, block(right_block - S)], base, right, me_j),
                rcopy(buf.at[:, block(left_block + S)], buf.at[:, block(left_block + K + S)], base + 1, left, me_j)]

    def xh_copies(s):
        return halo_copies(xp, K - 1 - s, s, xh_base + 2 * s)

    def gh_copies(s):
        return halo_copies(gep, S + s, S - 1 - s, gh_base + 2 * s)

    def start(copies):
        for c in copies:
            c.start()

    def arrive(copies):
        for c in copies:
            c.wait_recv()

    loads[0].wait()
    loads[1].wait()
    pl.semaphore_wait(barrier, J - 1 + L - 1)
    for s in range(S):
        start(xh_copies(s))
    for s in range(S - 1):
        start(ct_copies(s))

    for c in loads[2:]:
        c.wait()
    padded = jnp.concatenate([tapv[...], jnp.zeros((128 - TAPS, cl), f32)], axis=0)
    columns = jnp.concatenate([padded, jnp.zeros((128, 128 - cl), f32)], axis=1).T
    for t in range(TAPS):
        tf[t] = jnp.broadcast_to(columns[0:cl, t:t + 1], (cl, 128))
    wint[...] = win[...].T
    woutt[...] = wout[...].T
    gka[...] = jnp.zeros(gka.shape, f32)
    for s in range(S):
        ctf[s, mine, :] = ctv[:, col(s, me_j)]

    def conv_body(s, carry):
        arrive(xh_copies(s))
        for g in range(cl // 16):
            ch = slice(g * 16, (g + 1) * 16)
            w = [tf[t, ch, :] for t in range(TAPS)]
            for k in (S - 1 - s, S + s):
                for q in range(B // 128):
                    acc = jnp.zeros((16, 128), f32)
                    for t in range(TAPS):
                        acc = acc + w[t] * xp[ch, lanes((k + t) * B + q * 128, 128)].astype(f32)
                    fb[ch, lanes(k * B + q * 128, 128)] = acc.astype(bf)
        start(f_copies(s))
        fr[s, mine, :] = fb[:, col(s, me_j)]

        @pl.when(s == 0)
        def _():
            start(ct_copies(S - 1))
        return carry

    lax.fori_loop(0, S, conv_body, 0)

    def mlp_body(s, carry):
        arrive(ct_copies(s))
        arrive(f_copies(s))
        here = lanes(s * W, W)
        for b in range(W // 128):
            part = slice(b * 128, (b + 1) * 128)
            v = fr[s, :, part].astype(f32)
            centred = v - jnp.mean(v, axis=0, keepdims=True)
            inv = lax.rsqrt(jnp.mean(centred * centred, axis=0, keepdims=True) + epsilon)
            normed = centred * inv
            nrm[:, part] = normed
            istd[:, part] = inv
            nb[:, lanes(s * W + b * 128, 128)] = normed.astype(bf)
        normed_b = nb[:, here]
        up = ctf[s]
        FC = 256
        for f in range(F // FC):
            part = slice(f * FC, (f + 1) * FC)
            pre = jnp.dot(wint[part, :], normed_b, preferred_element_type=f32)
            ga = jnp.dot(wout[part, :], up, preferred_element_type=f32)
            sq = pre * pre
            tangent = jnp.tanh(pre * (gelu_scale + (gelu_scale * cubic_coef) * sq))
            gate = 0.5 + 0.5 * tangent
            slope = gate + pre * (gate * (1.0 - tangent)) * (gelu_scale + (3.0 * gelu_scale * cubic_coef) * sq)
            act[part, here] = (pre * gate).astype(bf)
            gp[part, here] = (ga * slope).astype(bf)
        gn = jnp.dot(win[...], gp[:, here], preferred_element_type=f32)
        for b in range(W // 128):
            part = slice(b * 128, (b + 1) * 128)
            g, normed = gn[:, part], nrm[:, part]
            out = istd[:, part] * (g - jnp.mean(g, axis=0, keepdims=True)
                                   - normed * jnp.mean(g * normed, axis=0, keepdims=True))
            geb[s, :, part] = out.astype(bf)
        start(ge_copies(s))
        gep[:, own_col(s, me_j)] = geb[s, mine, :]
        brb[s] = jnp.dot(woutt[...], act[:, here], preferred_element_type=f32).astype(bf)
        brv[:, col(s, me_j)] = brb[s, mine, :]

        @pl.when(s == 1)
        def _():
            start(br_copies(0))
        return carry

    lax.fori_loop(0, S, mlp_body, 0)

    def forward(s):
        arrive(ge_copies(s))
        start(gh_copies(s))

    def kernel_terms(s):
        for g in range(cl // 16):
            ch = slice(g * 16, (g + 1) * 16)
            sums = [gka[t, ch, :] for t in range(TAPS)]
            for k in (S - 1 - s, S + s):
                for q in range(B // 128):
                    e = gep[ch, lanes(own + k * B + q * 128, 128)].astype(f32)
                    for t in range(TAPS):
                        sums[t] = sums[t] + e * xp[ch, lanes((k + t) * B + q * 128, 128)].astype(f32)
            for t in range(TAPS):
                gka[t, ch, :] = sums[t]

    forward(0)

    def term_body(zz, carry):
        cols = lanes(zz * 256, 256)
        both = jnp.concatenate([ctf[s] for s in range(S)], axis=1)
        for i, (a, b) in enumerate(((nb[...], gp), (both, act))):
            term = lax.dot_general(a, b[cols, :], (((1,), (1,)), ((), ())), preferred_element_type=f32) * grad_scale
            for h in range(2):
                part = term[:, h * 128:(h + 1) * 128]
                gfull[h, zz, i] = part
                gsend[h, zz, i] = part.astype(bf)
        rcopy(gsend.at[1 - core, zz], grecv.at[zz], core_base + zz, z * 2 + 1 - core, me_j).start()
        return carry

    lax.fori_loop(0, Z, term_body, 0)
    forward(1)
    start(br_copies(1))

    CR = C // J

    def core_sum(zz, carry):
        c = rcopy(gsend.at[1 - core, zz], grecv.at[zz], core_base + zz, z * 2 + 1 - core, me_j)
        c.wait_recv()
        c.wait_send()
        for i in range(2):
            h = gfull[core, zz, i] + grecv[zz, i].astype(f32)
            for j in range(J):
                hf[j, zz, i] = h[j * CR:(j + 1) * CR]
                hs[j, zz, i] = h[j * CR:(j + 1) * CR].astype(bf)
        return carry

    lax.fori_loop(0, Z, core_sum, 0)
    h_in = [rcopy(hs.at[j], hr.at[me_j], take(), me_l, j) for j in chan_peers]
    start(h_in)
    start(br_copies(2))
    start(br_copies(3))

    def early_terms(s, carry):
        kernel_terms(s)
        return carry

    def late_terms(s, carry):
        forward(s)
        kernel_terms(s)
        return carry

    lax.fori_loop(0, 2, early_terms, 0)
    lax.fori_loop(2, S, late_terms, 0)
    sums = [jnp.sum(gka[t], axis=1, keepdims=True) * grad_scale for t in range(TAPS)]
    total = jnp.concatenate(sums + [jnp.zeros((cl, 128 - TAPS), f32)], axis=1)
    total = jnp.concatenate([total, jnp.zeros((128 - cl, 128), f32)], axis=0).T
    kt[me_l] = total[0:16]
    kt_in = [rcopy(kt.at[me_l], kt.at[me_l], take(), l, me_j) for l in loop_peers]
    start(kt_in)

    for s in range(S):
        arrive(gh_copies(s))

    def back_body(k, carry):
        for g in range(cl // 16):
            ch = slice(g * 16, (g + 1) * 16)
            w = [tf[t, ch, :] for t in range(TAPS)]
            for q in range(B // 128):
                at = lanes(k * B + q * 128, 128)
                acc = ctv[ch, at].astype(f32)
                for t in range(TAPS):
                    acc = acc + w[t] * gep[ch, lanes((k + TAPS - 1 - t) * B + q * 128, 128)].astype(f32)
                gx_out[ch, at] = acc.astype(bf)
        return carry

    lax.fori_loop(0, K, back_body, 0)

    arrive(h_in)
    for zz in range(Z):
        total = hf[me_j, zz]
        for d in range(1, J):
            total = total + hr[lax.rem(me_j + J - d, J), zz].astype(f32)
        sf[zz] = total
        sb[zz] = total.astype(bf)
    z_in = []
    for e in range(1, Z):
        zz = lax.rem(z + e, Z)
        z_in.append(rcopy(sb.at[zz], tr.at[z], take(), zz * 2 + core, me_j))
    start(z_in)

    def finish(s, carry):
        arrive(br_copies(s))
        for k in (S - 1 - s, S + s):
            bo_out[:, block(k)] = (xp[:, block(k + S)].astype(f32) + brv[:, block(k)].astype(f32)).astype(bf)
        return carry

    lax.fori_loop(0, S, finish, 0)
    arrive(kt_in)
    total = kt[0]
    for l in range(1, L):
        total = total + kt[l]
    gk_out[...] = total[0:TAPS, 0:cl]
    arrive(z_in)
    total = sf[z]
    for e in range(1, Z):
        total = total + tr[lax.rem(z + Z - e, Z)].astype(f32)
    gw_in_out[...] = total[0]
    gw_out_out[...] = total[1]

    def sent(s, carry):
        for copies in (ct_copies(s), f_copies(s), ge_copies(s), br_copies(s), xh_copies(s), gh_copies(s)):
            for c in copies:
                c.wait_send()
        return carry

    lax.fori_loop(0, S, sent, 0)
    for c in h_in + kt_in + z_in:
        c.wait_send()


def flush_kernel(*refs):
    n = len(refs) // 2
    sems = refs[2 * n]
    copies = [pltpu.make_async_copy(refs[i], refs[n + i], sems.at[i]) for i in range(n)]
    for c in copies:
        c.start()
    for c in copies:
        c.wait()


def fits(L, J, rows, cl, F):
    return (cl * 2 == 128 and rows == 2 * MIDDLE * DILATION_STEP and L % 2 == 0 and L > 2 and J == 4
            and F == L * 128)


def fused_shards(features, kernel_tap_rows, in_weight, out_weight, cotangent):
    L, J = lax.axis_size("loop"), lax.axis_size("chan")
    rows, cl = features.shape
    C, F = in_weight.shape
    if not fits(L, J, rows, cl, F):
        return shards(features, kernel_tap_rows, in_weight, out_weight, cotangent)
    N = rows // J
    K = rows // DILATION_STEP
    S = K // 2
    W = N // S
    Z = L // 2
    CR = C // J
    bf, f32 = jnp.bfloat16, jnp.float32
    ext = rows + 2 * MIDDLE * DILATION_STEP
    scratch = [
        pltpu.VMEM((cl, ext), bf),
        pltpu.VMEM((cl, rows), bf),
        pltpu.VMEM((TAPS, cl), f32),
        pltpu.VMEM((C, F), bf),
        pltpu.VMEM((F, C), bf),
        pltpu.VMEM((F, C), bf),
        pltpu.VMEM((C, F), bf),
        pltpu.VMEM((TAPS, cl, 128), f32),
        pltpu.VMEM((cl, rows), bf),
        pltpu.VMEM((S, C, W), bf),
        pltpu.VMEM((S, C, W), bf),
        pltpu.VMEM((C, N), bf),
        pltpu.VMEM((C, W), f32),
        pltpu.VMEM((1, W), f32),
        pltpu.VMEM((F, N), bf),
        pltpu.VMEM((F, N), bf),
        pltpu.VMEM((S, C, W), bf),
        pltpu.VMEM((S, C, W), bf),
        pltpu.VMEM((cl, ext), bf),
        pltpu.VMEM((cl, rows), bf),
        pltpu.VMEM((2, Z, 2, C, 128), f32),
        pltpu.VMEM((2, Z, 2, C, 128), bf),
        pltpu.VMEM((Z, 2, C, 128), bf),
        pltpu.VMEM((J, Z, 2, CR, 128), f32),
        pltpu.VMEM((J, Z, 2, CR, 128), bf),
        pltpu.VMEM((J, Z, 2, CR, 128), bf),
        pltpu.VMEM((Z, 2, CR, 128), f32),
        pltpu.VMEM((Z, 2, CR, 128), bf),
        pltpu.VMEM((Z, 2, CR, 128), bf),
        pltpu.VMEM((TAPS, cl, 128), f32),
        pltpu.VMEM((L, 16, 128), f32),
    ]
    copies = 4 * S * (J - 1) + 4 * S + Z + (J - 1) + (L - 1) + (Z - 1)
    scratch += [pltpu.SemaphoreType.DMA((5,)), pltpu.SemaphoreType.DMA((copies,)), pltpu.SemaphoreType.DMA((copies,))]
    vmem = pl.BlockSpec(memory_space=pltpu.VMEM)
    hbm = pl.BlockSpec(memory_space=HBM)
    shapes = (
        jax.ShapeDtypeStruct((cl, rows), bf),
        jax.ShapeDtypeStruct((cl, rows), bf),
        jax.ShapeDtypeStruct((CR, F // L), f32),
        jax.ShapeDtypeStruct((CR, F // L), f32),
        jax.ShapeDtypeStruct((TAPS, cl), f32),
    )
    results = pl.pallas_call(
        functools.partial(fused_kernel, L, J, 1.0 / math.sqrt(rows * L)),
        out_shape=shapes,
        in_specs=[hbm] * 5,
        out_specs=(vmem,) * 5,
        scratch_shapes=scratch,
        compiler_params=pltpu.CompilerParams(
            collective_id=0, has_side_effects=True, vmem_limit_bytes=54000 * 1024),
        cost_estimate=pl.CostEstimate(flops=12 * N * C * F, bytes_accessed=8 * rows * cl * 2, transcendentals=N * F),
    )(features.T, cotangent.T, kernel_tap_rows, in_weight, out_weight)
    bo, gx, gw_in, gw_out, gk = pl.pallas_call(
        flush_kernel,
        out_shape=shapes,
        in_specs=[pl.BlockSpec(memory_space=pl.ANY)] * 5,
        out_specs=(hbm,) * 5,
        scratch_shapes=[pltpu.SemaphoreType.DMA((5,))],
        compiler_params=pltpu.CompilerParams(vmem_limit_bytes=1024 * 1024),
    )(*results)
    return bo.T, gx.T, gw_in, gw_out.T, gk


def solution(mesh):
    placed = (P("loop", "chan"), P(None, "chan"), P(), P(), P("loop", "chan"))
    return jax.shard_map(
        fused_shards,
        mesh=mesh,
        in_specs=placed,
        out_specs=(
            P("loop", "chan"),
            P("loop", "chan"),
            P("chan", "loop"),
            P("loop", "chan"),
            P(None, "chan"),
        ),
        check_vma=False,
    )
```

```python
import functools
import math

import jax
import jax.numpy as jnp
from jax import lax
from jax.experimental import pallas as pl
from jax.experimental.pallas import tpu as pltpu
from jax.sharding import PartitionSpec as P

TAPS = 9
DILATION_STEP = 512


gelu_scale = math.sqrt(2.0 / math.pi)
cubic_coef = 0.044715
epsilon = 1e-05


def with_halo(cells, sides, width):
    for axis, dim in sides:
        count = lax.axis_size(axis)
        head = lax.slice_in_dim(cells, 0, width, axis=dim)
        tail = lax.slice_in_dim(cells, cells.shape[dim] - width, cells.shape[dim], axis=dim)
        cells = jnp.concatenate(
            [
                lax.ppermute(tail, axis, [(i, (i + 1) % count) for i in range(count)]),
                cells,
                lax.ppermute(head, axis, [((i + 1) % count, i) for i in range(count)]),
            ],
            axis=dim,
        )
    return cells


def gelu_pair(inputs):
    inner_arg = gelu_scale * (inputs + cubic_coef * inputs * inputs * inputs)
    tangent = jnp.tanh(inner_arg)
    act_value = 0.5 * inputs * (1.0 + tangent)
    act_slope = 0.5 * (1.0 + tangent) + 0.5 * inputs * (1.0 - tangent * tangent) * gelu_scale * (
        1.0 + 3.0 * cubic_coef * inputs * inputs
    )
    return (act_value, act_slope)


def widen_rows(field_rows, reach_positions):
    return with_halo(field_rows, (("loop", 0),), reach_positions)


def shards(features, kernel_tap_rows, in_weight, out_weight, cotangent):
    middle_position = (TAPS - 1) // 2
    reach_positions = middle_position * DILATION_STEP
    loop_size = lax.axis_size("loop")
    chan_size = lax.axis_size("chan")
    rows_here = features.shape[0]
    grad_scale = 1.0 / math.sqrt(rows_here * loop_size)
    padded_in = widen_rows(features, reach_positions)
    blended_sum = jnp.zeros(features.shape, jnp.float32)
    for kernel_tap_index in range(TAPS):
        leading_row = reach_positions + (kernel_tap_index - middle_position) * DILATION_STEP
        blended_sum = blended_sum + kernel_tap_rows[kernel_tap_index] * padded_in[
            leading_row : leading_row + rows_here
        ].astype(jnp.float32)
    filtered = blended_sum.astype(jnp.bfloat16)
    row_block, upstream = (
        lax.all_to_all(filtered, "chan", split_axis=0, concat_axis=1, tiled=True),
        lax.all_to_all(cotangent, "chan", split_axis=0, concat_axis=1, tiled=True),
    )
    values = row_block.astype(jnp.float32)
    mean_value = jnp.mean(values, axis=-1, keepdims=True)
    centred = values - mean_value
    variance = jnp.mean(centred * centred, axis=-1, keepdims=True)
    inv_std = lax.rsqrt(variance + epsilon)
    normed = centred * inv_std
    normed_b = normed.astype(jnp.bfloat16)
    hidden_pre = jnp.dot(normed_b, in_weight, preferred_element_type=jnp.float32)
    act_value, act_slope = gelu_pair(hidden_pre)
    act_b = act_value.astype(jnp.bfloat16)
    branch = jnp.dot(act_b, out_weight, preferred_element_type=jnp.float32).astype(jnp.bfloat16)
    grad_act = jnp.einsum("pc,fc->pf", upstream, out_weight, preferred_element_type=jnp.float32)
    grad_pre = (grad_act * act_slope).astype(jnp.bfloat16)
    grad_normed = jnp.einsum("pf,cf->pc", grad_pre, in_weight, preferred_element_type=jnp.float32)
    grad_filtered = inv_std * (
        grad_normed
        - jnp.mean(grad_normed, axis=-1, keepdims=True)
        - normed * jnp.mean(grad_normed * normed, axis=-1, keepdims=True)
    )
    back_rows = grad_filtered.astype(jnp.bfloat16)
    local_rows = row_block.shape[0]
    width_c = row_block.shape[1]
    width_f = hidden_pre.shape[1]
    chan_part = width_c // chan_size
    loop_part = width_f // loop_size
    normed_parts = normed_b.reshape(local_rows, chan_size, chan_part)
    upstream_parts = upstream.reshape(local_rows, chan_size, chan_part)
    grad_parts = grad_pre.reshape(local_rows, loop_size, loop_part)
    act_parts = act_b.reshape(local_rows, loop_size, loop_part)
    term_in = (
        jnp.einsum("pai,pbj->baij", normed_parts, grad_parts, preferred_element_type=jnp.float32)
        * grad_scale
    )
    term_out = (
        jnp.einsum("pbj,pai->baji", act_parts, upstream_parts, preferred_element_type=jnp.float32)
        * grad_scale
    )
    branch_cols, back_cols = (
        lax.all_to_all(branch, "chan", split_axis=1, concat_axis=0, tiled=True),
        lax.all_to_all(back_rows, "chan", split_axis=1, concat_axis=0, tiled=True),
    )
    block_out = (features.astype(jnp.float32) + branch_cols.astype(jnp.float32)).astype(
        jnp.bfloat16
    )
    first_in, first_out = (
        lax.psum_scatter(
            term_in.astype(jnp.bfloat16), "chan", scatter_dimension=1, tiled=True
        ).astype(jnp.float32),
        lax.psum_scatter(
            term_out.astype(jnp.bfloat16), "chan", scatter_dimension=1, tiled=True
        ).astype(jnp.float32),
    )
    summed_in, summed_out = (
        lax.psum_scatter(first_in, "loop", scatter_dimension=0, tiled=True),
        lax.psum_scatter(first_out, "loop", scatter_dimension=0, tiled=True),
    )
    grad_in_weight = summed_in.reshape(chan_part, loop_part)
    grad_out_weight = summed_out.reshape(loop_part, chan_part)
    padded_back = widen_rows(back_cols, reach_positions)
    grad_sum_rows = cotangent.astype(jnp.float32)
    back_wide = back_cols.astype(jnp.float32)
    kernel_rows = []
    for kernel_tap_index in range(TAPS):
        shift_positions = (kernel_tap_index - middle_position) * DILATION_STEP
        first_back = reach_positions - shift_positions
        grad_sum_rows = grad_sum_rows + kernel_tap_rows[kernel_tap_index] * padded_back[
            first_back : first_back + rows_here
        ].astype(jnp.float32)
        first_in_row = reach_positions + shift_positions
        kernel_rows.append(
            jnp.sum(
                back_wide * padded_in[first_in_row : first_in_row + rows_here].astype(jnp.float32),
                axis=0,
            )
        )
    kernel_terms = jnp.stack(kernel_rows) * grad_scale
    grad_kernel = lax.psum(kernel_terms, "loop")
    return (
        block_out,
        grad_sum_rows.astype(jnp.bfloat16),
        grad_in_weight,
        grad_out_weight,
        grad_kernel,
    )


MESH = pl.DeviceIdType.MESH
MIDDLE = (TAPS - 1) // 2
HBM = pltpu.MemorySpace.HBM


def fused_kernel(
    L, J, grad_scale,
    x_hbm, ct_hbm, taps_hbm, win_hbm, wout_hbm,
    bo_out, gx_out, gw_in_out, gw_out_out, gk_out,
    xp, ctv, tapv, win, wout, wint, woutt, tf, fb, fr, ctf, nb, nrm, istd, act, gp,
    geb, brb, gep, brv, gfull, gsend, grecv, hf, hs, hr, sf, sb, tr, zs, tz, vf, vs, vr, gka, kt, acc_x,
    load, send, recv,
):
    cl, rows = ctv.shape
    C, F = win.shape
    B = DILATION_STEP
    K = rows // B
    S = K // 2
    W = 2 * B // J
    Z = L // 2
    own = MIDDLE * B
    bf, f32 = jnp.bfloat16, jnp.float32
    me_l, me_j = lax.axis_index("loop"), lax.axis_index("chan")
    core, z = lax.rem(me_l, 2), me_l // 2
    used = [0]

    def take(n=1):
        used[0] += n
        return used[0] - n

    def rcopy(src, dst, idx, l, j):
        return pltpu.make_async_remote_copy(
            src_ref=src, dst_ref=dst, send_sem=send.at[idx], recv_sem=recv.at[idx],
            device_id=(l, j), device_id_type=MESH)

    def lanes(at, n):
        return pl.ds(pl.multiple_of(at, 128), n)

    loads = [pltpu.make_async_copy(a, b, load.at[i]) for i, (a, b) in enumerate((
        (x_hbm, xp.at[:, own:own + rows]), (ct_hbm, ctv), (taps_hbm, tapv), (win_hbm, win), (wout_hbm, wout)))]
    for c in loads:
        c.start()

    chan_peers = [lax.rem(me_j + d, J) for d in range(1, J)]
    loop_peers = [lax.rem(me_l + e, L) for e in range(1, L)]
    right, left = loop_peers[0], loop_peers[-1]

    barrier = pltpu.get_barrier_semaphore()
    for j in chan_peers:
        pl.semaphore_signal(barrier, inc=1, device_id=(me_l, j), device_id_type=MESH)
    for l in loop_peers:
        pl.semaphore_signal(barrier, inc=1, device_id=(l, me_j), device_id_type=MESH)

    half = J // 2
    mine = pl.ds(pl.multiple_of(me_j * cl, cl), cl)

    def col(s, j):
        return lanes((S - 1 - s + (j // half) * (1 + 2 * s)) * B + lax.rem(j, half) * W, W)

    def own_col(s, j):
        return lanes(own + (S - 1 - s + (j // half) * (1 + 2 * s)) * B + lax.rem(j, half) * W, W)

    def block(k):
        return lanes(k * B, B)

    def chan_rows(j):
        return pl.ds(pl.multiple_of(j * cl, cl), cl)

    ct_base, f_base = take(S * (J - 1)), take(S * (J - 1))
    ge_base, br_base = take(S * (J - 1)), take(S * (J - 1))
    xh_base, gh_base = take(S * 2), take(S * 2)
    core_base = take(Z)
    h_base, tz_base = take(Z * (J - 1)), take(Z - 1)

    def ct_copies(s):
        return [rcopy(ctv.at[:, col(s, j)], ctf.at[s, mine, :], ct_base + s * (J - 1) + d, me_l, j)
                for d, j in enumerate(chan_peers)]

    def f_copies(s):
        return [rcopy(fb.at[:, col(s, j)], fr.at[s, mine, :], f_base + s * (J - 1) + d, me_l, j)
                for d, j in enumerate(chan_peers)]

    def ge_copies(s):
        return [rcopy(geb.at[s, chan_rows(j), :], gep.at[:, own_col(s, me_j)], ge_base + s * (J - 1) + d, me_l, j)
                for d, j in enumerate(chan_peers)]

    def br_copies(s):
        return [rcopy(brb.at[s, chan_rows(j), :], brv.at[:, col(s, me_j)], br_base + s * (J - 1) + d, me_l, j)
                for d, j in enumerate(chan_peers)]

    def halo_copies(buf, right_block, left_block, base):
        return [rcopy(buf.at[:, block(right_block + S)], buf.at[:, block(right_block - S)], base, right, me_j),
                rcopy(buf.at[:, block(left_block + S)], buf.at[:, block(left_block + K + S)], base + 1, left, me_j)]

    def xh_copies(s):
        return halo_copies(xp, K - 1 - s, s, xh_base + 2 * s)

    def gh_copies(s):
        return halo_copies(gep, S + s, S - 1 - s, gh_base + 2 * s)

    def start(copies):
        for c in copies:
            c.start()

    def arrive(copies):
        for c in copies:
            c.wait_recv()

    loads[0].wait()
    loads[1].wait()
    pl.semaphore_wait(barrier, J - 1 + L - 1)
    for s in range(S):
        start(xh_copies(s))
    for s in range(S - 1):
        start(ct_copies(s))

    for c in loads[2:]:
        c.wait()
    padded = jnp.concatenate([tapv[...], jnp.zeros((128 - TAPS, cl), f32)], axis=0)
    columns = jnp.concatenate([padded, jnp.zeros((128, 128 - cl), f32)], axis=1).T
    for t in range(TAPS):
        tf[t] = jnp.broadcast_to(columns[0:cl, t:t + 1], (cl, 128))
    wint[...] = win[...].T
    woutt[...] = wout[...].T
    gka[...] = jnp.zeros(gka.shape, f32)
    for s in range(S):
        ctf[s, mine, :] = ctv[:, col(s, me_j)]

    def conv_body(s, carry):
        arrive(xh_copies(s))
        for g in range(cl // 16):
            ch = slice(g * 16, (g + 1) * 16)
            w = [tf[t, ch, :] for t in range(TAPS)]
            for k in (S - 1 - s, S + s):
                for q in range(B // 128):
                    acc = jnp.zeros((16, 128), f32)
                    for t in range(TAPS):
                        acc = acc + w[t] * xp[ch, lanes((k + t) * B + q * 128, 128)].astype(f32)
                    fb[ch, lanes(k * B + q * 128, 128)] = acc.astype(bf)
        start(f_copies(s))
        fr[s, mine, :] = fb[:, col(s, me_j)]

        @pl.when(s == 0)
        def _():
            start(ct_copies(S - 1))
        return carry

    lax.fori_loop(0, S, conv_body, 0)

    def mlp_body(s, carry):
        arrive(ct_copies(s))
        arrive(f_copies(s))
        here = lanes(s * W, W)
        for b in range(W // 128):
            part = slice(b * 128, (b + 1) * 128)
            v = fr[s, :, part].astype(f32)
            centred = v - jnp.mean(v, axis=0, keepdims=True)
            inv = lax.rsqrt(jnp.mean(centred * centred, axis=0, keepdims=True) + epsilon)
            normed = centred * inv
            nrm[:, part] = normed
            istd[:, part] = inv
            nb[:, lanes(s * W + b * 128, 128)] = normed.astype(bf)
        normed_b = nb[:, here]
        up = ctf[s]
        FC = 256
        for f in range(F // FC):
            part = slice(f * FC, (f + 1) * FC)
            pre = jnp.dot(wint[part, :], normed_b, preferred_element_type=f32)
            ga = jnp.dot(wout[part, :], up, preferred_element_type=f32)
            sq = pre * pre
            tangent = jnp.tanh(pre * (gelu_scale + (gelu_scale * cubic_coef) * sq))
            gate = 0.5 + 0.5 * tangent
            slope = gate + pre * (gate * (1.0 - tangent)) * (gelu_scale + (3.0 * gelu_scale * cubic_coef) * sq)
            act[part, here] = (pre * gate).astype(bf)
            gp[part, here] = (ga * slope).astype(bf)
        gn = jnp.dot(win[...], gp[:, here], preferred_element_type=f32)
        for b in range(W // 128):
            part = slice(b * 128, (b + 1) * 128)
            g, normed = gn[:, part], nrm[:, part]
            out = istd[:, part] * (g - jnp.mean(g, axis=0, keepdims=True)
                                   - normed * jnp.mean(g * normed, axis=0, keepdims=True))
            geb[s, :, part] = out.astype(bf)
        start(ge_copies(s))
        gep[:, own_col(s, me_j)] = geb[s, mine, :]
        brb[s] = jnp.dot(woutt[...], act[:, here], preferred_element_type=f32).astype(bf)
        brv[:, col(s, me_j)] = brb[s, mine, :]

        return carry

    lax.fori_loop(0, S, mlp_body, 0)
    start(br_copies(0))

    def forward(s):
        arrive(ge_copies(s))
        start(gh_copies(s))

    def kernel_terms(s):
        for g in range(cl // 16):
            ch = slice(g * 16, (g + 1) * 16)
            sums = [gka[t, ch, :] for t in range(TAPS)]
            for k in (S - 1 - s, S + s):
                for q in range(B // 128):
                    e = gep[ch, lanes(own + k * B + q * 128, 128)].astype(f32)
                    for t in range(TAPS):
                        sums[t] = sums[t] + e * xp[ch, lanes((k + t) * B + q * 128, 128)].astype(f32)
            for t in range(TAPS):
                gka[t, ch, :] = sums[t]

    forward(0)
    CR = C // J

    def core_copy(zz):
        return rcopy(gsend.at[1 - core, zz], grecv.at[zz], core_base + zz, z * 2 + 1 - core, me_j)

    def term_body(e, carry):
        zz = lax.rem(z + 1 + e, Z)
        cols = lanes(zz * 256, 256)
        both = jnp.concatenate([ctf[s] for s in range(S)], axis=1)
        for i, (a, b) in enumerate(((nb[...], gp), (both, act))):
            term = lax.dot_general(a, b[cols, :], (((1,), (1,)), ((), ())), preferred_element_type=f32) * grad_scale
            for h in range(2):
                part = term[:, h * 128:(h + 1) * 128]
                gfull[h, zz, i] = part
                gsend[h, zz, i] = part.astype(bf)
        core_copy(zz).start()

        @pl.when(e == 1)
        def _():
            forward(1)
        return carry

    lax.fori_loop(0, Z, term_body, 0)

    def h_copies(zz):
        return [rcopy(hs.at[j, zz], hr.at[me_j, zz], h_base + zz * (J - 1) + d, me_l, j)
                for d, j in enumerate(chan_peers)]

    def zfirst(e):
        zz = lax.rem(z + 1 + e, Z)
        return rcopy(zs.at[zz], tz.at[z], tz_base + e, zz * 2 + core, me_j)

    def core_sum(e, carry):
        zz = lax.rem(z + 1 + e, Z)
        core_copy(zz).wait_recv()
        h = gfull[core, zz, 1] + grecv[zz, 1].astype(f32)
        gfull[core, zz, 1] = h
        zs[zz] = h.astype(bf)

        @pl.when(e < Z - 1)
        def _():
            zfirst(e).start()
        h = gfull[core, zz, 0] + grecv[zz, 0].astype(f32)
        for j in range(J):
            hf[j, zz] = h[j * CR:(j + 1) * CR]
            hs[j, zz] = h[j * CR:(j + 1) * CR].astype(bf)
        start(h_copies(zz))

        @pl.when(e == 1)
        def _():
            forward(2)
        return carry

    lax.fori_loop(0, Z, core_sum, 0)
    for s in range(1, S):
        start(br_copies(s))

    def early_terms(s, carry):
        kernel_terms(s)
        return carry

    lax.fori_loop(0, S - 1, early_terms, 0)
    forward(S - 1)
    kernel_terms(S - 1)
    sums = [jnp.sum(gka[t], axis=1, keepdims=True) * grad_scale for t in range(TAPS)]
    total = jnp.concatenate(sums + [jnp.zeros((cl, 128 - TAPS), f32)], axis=1)
    total = jnp.concatenate([total, jnp.zeros((128 - cl, 128), f32)], axis=0).T
    kt[me_l] = total[0:16]
    kt_in = [rcopy(kt.at[me_l], kt.at[me_l], take(), l, me_j) for l in loop_peers]
    start(kt_in)

    def back(final):
        late = (S - 1, S, S + K - 1, S + K)

        def part(q, carry):
            for g in range(cl // 16):
                ch = slice(g * 16, (g + 1) * 16)
                w = [tf[t, ch, :] for t in range(TAPS)]
                for k in range(K):
                    at = lanes(k * B + q * 128, 128)
                    acc = acc_x[ch, at] if final else ctv[ch, at].astype(f32)
                    for t in range(TAPS):
                        b = k + TAPS - 1 - t
                        if (b in late) == final:
                            acc = acc + w[t] * gep[ch, lanes(b * B + q * 128, 128)].astype(f32)
                    if final:
                        gx_out[ch, at] = acc.astype(bf)
                    else:
                        acc_x[ch, at] = acc
            return carry

        lax.fori_loop(0, B // 128, part, 0)

    for s in range(S - 1):
        arrive(gh_copies(s))
    back(False)
    arrive(gh_copies(S - 1))
    back(True)

    for zz in range(Z):
        arrive(h_copies(zz))
    for zz in range(Z):
        total = hf[me_j, zz]
        for d in range(1, J):
            total = total + hr[lax.rem(me_j + J - d, J), zz].astype(f32)
        sf[zz] = total
        sb[zz] = total.astype(bf)
    z_in = []
    for e in range(1, Z):
        zz = lax.rem(z + e, Z)
        z_in.append(rcopy(sb.at[zz], tr.at[z], take(), zz * 2 + core, me_j))
    start(z_in)
    for e in range(Z - 1):
        zfirst(e).wait_recv()
    total = gfull[core, z, 1]
    for e in range(1, Z):
        total = total + tz[lax.rem(z + Z - e, Z)].astype(f32)
    for j in range(J):
        vf[j] = total[j * CR:(j + 1) * CR]
        vs[j] = total[j * CR:(j + 1) * CR].astype(bf)
    v_in = [rcopy(vs.at[j], vr.at[me_j], take(), me_l, j) for j in chan_peers]
    start(v_in)

    def finish(s, carry):
        arrive(br_copies(s))
        for k in (S - 1 - s, S + s):
            bo_out[:, block(k)] = (xp[:, block(k + S)].astype(f32) + brv[:, block(k)].astype(f32)).astype(bf)
        return carry

    lax.fori_loop(0, S, finish, 0)
    arrive(kt_in)
    total = kt[0]
    for l in range(1, L):
        total = total + kt[l]
    gk_out[...] = total[0:TAPS, 0:cl]
    arrive(z_in)
    total = sf[z]
    for e in range(1, Z):
        total = total + tr[lax.rem(z + Z - e, Z)].astype(f32)
    gw_in_out[...] = total
    arrive(v_in)
    total = vf[me_j]
    for d in range(1, J):
        total = total + vr[lax.rem(me_j + J - d, J)].astype(f32)
    gw_out_out[...] = total

    def sent(s, carry):
        for copies in (ct_copies(s), f_copies(s), ge_copies(s), br_copies(s), xh_copies(s), gh_copies(s)):
            for c in copies:
                c.wait_send()
        return carry

    lax.fori_loop(0, S, sent, 0)
    for zz in range(Z):
        for c in [core_copy(zz)] + h_copies(zz):
            c.wait_send()
    for c in kt_in + z_in + v_in + [zfirst(e) for e in range(Z - 1)]:
        c.wait_send()


def flush_kernel(*refs):
    n = len(refs) // 2
    sems = refs[2 * n]
    copies = [pltpu.make_async_copy(refs[i], refs[n + i], sems.at[i]) for i in range(n)]
    for c in copies:
        c.start()
    for c in copies:
        c.wait()


def fits(L, J, rows, cl, F):
    return (cl * 2 == 128 and rows == 2 * MIDDLE * DILATION_STEP and L % 2 == 0 and L > 2 and J == 4
            and F == L * 128)


def fused_shards(features, kernel_tap_rows, in_weight, out_weight, cotangent):
    L, J = lax.axis_size("loop"), lax.axis_size("chan")
    rows, cl = features.shape
    C, F = in_weight.shape
    if not fits(L, J, rows, cl, F):
        return shards(features, kernel_tap_rows, in_weight, out_weight, cotangent)
    N = rows // J
    K = rows // DILATION_STEP
    S = K // 2
    W = N // S
    Z = L // 2
    CR = C // J
    bf, f32 = jnp.bfloat16, jnp.float32
    ext = rows + 2 * MIDDLE * DILATION_STEP
    scratch = [
        pltpu.VMEM((cl, ext), bf),
        pltpu.VMEM((cl, rows), bf),
        pltpu.VMEM((TAPS, cl), f32),
        pltpu.VMEM((C, F), bf),
        pltpu.VMEM((F, C), bf),
        pltpu.VMEM((F, C), bf),
        pltpu.VMEM((C, F), bf),
        pltpu.VMEM((TAPS, cl, 128), f32),
        pltpu.VMEM((cl, rows), bf),
        pltpu.VMEM((S, C, W), bf),
        pltpu.VMEM((S, C, W), bf),
        pltpu.VMEM((C, N), bf),
        pltpu.VMEM((C, W), f32),
        pltpu.VMEM((1, W), f32),
        pltpu.VMEM((F, N), bf),
        pltpu.VMEM((F, N), bf),
        pltpu.VMEM((S, C, W), bf),
        pltpu.VMEM((S, C, W), bf),
        pltpu.VMEM((cl, ext), bf),
        pltpu.VMEM((cl, rows), bf),
        pltpu.VMEM((2, Z, 2, C, 128), f32),
        pltpu.VMEM((2, Z, 2, C, 128), bf),
        pltpu.VMEM((Z, 2, C, 128), bf),
        pltpu.VMEM((J, Z, CR, 128), f32),
        pltpu.VMEM((J, Z, CR, 128), bf),
        pltpu.VMEM((J, Z, CR, 128), bf),
        pltpu.VMEM((Z, CR, 128), f32),
        pltpu.VMEM((Z, CR, 128), bf),
        pltpu.VMEM((Z, CR, 128), bf),
        pltpu.VMEM((Z, C, 128), bf),
        pltpu.VMEM((Z, C, 128), bf),
        pltpu.VMEM((J, CR, 128), f32),
        pltpu.VMEM((J, CR, 128), bf),
        pltpu.VMEM((J, CR, 128), bf),
        pltpu.VMEM((TAPS, cl, 128), f32),
        pltpu.VMEM((L, 16, 128), f32),
        pltpu.VMEM((cl, rows), f32),
    ]
    copies = 4 * S * (J - 1) + 4 * S + Z + (Z + 1) * (J - 1) + (L - 1) + 2 * (Z - 1)
    scratch += [pltpu.SemaphoreType.DMA((5,)), pltpu.SemaphoreType.DMA((copies,)), pltpu.SemaphoreType.DMA((copies,))]
    vmem = pl.BlockSpec(memory_space=pltpu.VMEM)
    hbm = pl.BlockSpec(memory_space=HBM)
    shapes = (
        jax.ShapeDtypeStruct((cl, rows), bf),
        jax.ShapeDtypeStruct((cl, rows), bf),
        jax.ShapeDtypeStruct((CR, F // L), f32),
        jax.ShapeDtypeStruct((CR, F // L), f32),
        jax.ShapeDtypeStruct((TAPS, cl), f32),
    )
    results = pl.pallas_call(
        functools.partial(fused_kernel, L, J, 1.0 / math.sqrt(rows * L)),
        out_shape=shapes,
        in_specs=[hbm] * 5,
        out_specs=(vmem,) * 5,
        scratch_shapes=scratch,
        compiler_params=pltpu.CompilerParams(
            collective_id=0, has_side_effects=True, vmem_limit_bytes=50 * 1024 * 1024),
        cost_estimate=pl.CostEstimate(flops=12 * N * C * F, bytes_accessed=8 * rows * cl * 2, transcendentals=N * F),
    )(*[pltpu.with_memory_space_constraint(a, HBM)
        for a in (features.T, cotangent.T, kernel_tap_rows, in_weight, out_weight)])
    bo, gx, gw_in, gw_out, gk = pl.pallas_call(
        flush_kernel,
        out_shape=shapes,
        in_specs=[pl.BlockSpec(memory_space=pl.ANY)] * 5,
        out_specs=(hbm,) * 5,
        scratch_shapes=[pltpu.SemaphoreType.DMA((5,))],
        compiler_params=pltpu.CompilerParams(vmem_limit_bytes=1024 * 1024),
    )(*results)
    return bo.T, gx.T, gw_in, gw_out.T, gk


def solution(mesh):
    placed = (P("loop", "chan"), P(None, "chan"), P(), P(), P("loop", "chan"))
    return jax.shard_map(
        fused_shards,
        mesh=mesh,
        in_specs=placed,
        out_specs=(
            P("loop", "chan"),
            P("loop", "chan"),
            P("chan", "loop"),
            P("loop", "chan"),
            P(None, "chan"),
        ),
        check_vma=False,
    )
```

```python
import functools
import math

import jax
import jax.numpy as jnp
from jax import lax
from jax.experimental import pallas as pl
from jax.experimental.pallas import tpu as pltpu
from jax.sharding import PartitionSpec as P

TAPS = 9
DILATION_STEP = 512


gelu_scale = math.sqrt(2.0 / math.pi)
cubic_coef = 0.044715
epsilon = 1e-05


def with_halo(cells, sides, width):
    for axis, dim in sides:
        count = lax.axis_size(axis)
        head = lax.slice_in_dim(cells, 0, width, axis=dim)
        tail = lax.slice_in_dim(cells, cells.shape[dim] - width, cells.shape[dim], axis=dim)
        cells = jnp.concatenate(
            [
                lax.ppermute(tail, axis, [(i, (i + 1) % count) for i in range(count)]),
                cells,
                lax.ppermute(head, axis, [((i + 1) % count, i) for i in range(count)]),
            ],
            axis=dim,
        )
    return cells


def gelu_pair(inputs):
    inner_arg = gelu_scale * (inputs + cubic_coef * inputs * inputs * inputs)
    tangent = jnp.tanh(inner_arg)
    act_value = 0.5 * inputs * (1.0 + tangent)
    act_slope = 0.5 * (1.0 + tangent) + 0.5 * inputs * (1.0 - tangent * tangent) * gelu_scale * (
        1.0 + 3.0 * cubic_coef * inputs * inputs
    )
    return (act_value, act_slope)


def widen_rows(field_rows, reach_positions):
    return with_halo(field_rows, (("loop", 0),), reach_positions)


def shards(features, kernel_tap_rows, in_weight, out_weight, cotangent):
    middle_position = (TAPS - 1) // 2
    reach_positions = middle_position * DILATION_STEP
    loop_size = lax.axis_size("loop")
    chan_size = lax.axis_size("chan")
    rows_here = features.shape[0]
    grad_scale = 1.0 / math.sqrt(rows_here * loop_size)
    padded_in = widen_rows(features, reach_positions)
    blended_sum = jnp.zeros(features.shape, jnp.float32)
    for kernel_tap_index in range(TAPS):
        leading_row = reach_positions + (kernel_tap_index - middle_position) * DILATION_STEP
        blended_sum = blended_sum + kernel_tap_rows[kernel_tap_index] * padded_in[
            leading_row : leading_row + rows_here
        ].astype(jnp.float32)
    filtered = blended_sum.astype(jnp.bfloat16)
    row_block, upstream = (
        lax.all_to_all(filtered, "chan", split_axis=0, concat_axis=1, tiled=True),
        lax.all_to_all(cotangent, "chan", split_axis=0, concat_axis=1, tiled=True),
    )
    values = row_block.astype(jnp.float32)
    mean_value = jnp.mean(values, axis=-1, keepdims=True)
    centred = values - mean_value
    variance = jnp.mean(centred * centred, axis=-1, keepdims=True)
    inv_std = lax.rsqrt(variance + epsilon)
    normed = centred * inv_std
    normed_b = normed.astype(jnp.bfloat16)
    hidden_pre = jnp.dot(normed_b, in_weight, preferred_element_type=jnp.float32)
    act_value, act_slope = gelu_pair(hidden_pre)
    act_b = act_value.astype(jnp.bfloat16)
    branch = jnp.dot(act_b, out_weight, preferred_element_type=jnp.float32).astype(jnp.bfloat16)
    grad_act = jnp.einsum("pc,fc->pf", upstream, out_weight, preferred_element_type=jnp.float32)
    grad_pre = (grad_act * act_slope).astype(jnp.bfloat16)
    grad_normed = jnp.einsum("pf,cf->pc", grad_pre, in_weight, preferred_element_type=jnp.float32)
    grad_filtered = inv_std * (
        grad_normed
        - jnp.mean(grad_normed, axis=-1, keepdims=True)
        - normed * jnp.mean(grad_normed * normed, axis=-1, keepdims=True)
    )
    back_rows = grad_filtered.astype(jnp.bfloat16)
    local_rows = row_block.shape[0]
    width_c = row_block.shape[1]
    width_f = hidden_pre.shape[1]
    chan_part = width_c // chan_size
    loop_part = width_f // loop_size
    normed_parts = normed_b.reshape(local_rows, chan_size, chan_part)
    upstream_parts = upstream.reshape(local_rows, chan_size, chan_part)
    grad_parts = grad_pre.reshape(local_rows, loop_size, loop_part)
    act_parts = act_b.reshape(local_rows, loop_size, loop_part)
    term_in = (
        jnp.einsum("pai,pbj->baij", normed_parts, grad_parts, preferred_element_type=jnp.float32)
        * grad_scale
    )
    term_out = (
        jnp.einsum("pbj,pai->baji", act_parts, upstream_parts, preferred_element_type=jnp.float32)
        * grad_scale
    )
    branch_cols, back_cols = (
        lax.all_to_all(branch, "chan", split_axis=1, concat_axis=0, tiled=True),
        lax.all_to_all(back_rows, "chan", split_axis=1, concat_axis=0, tiled=True),
    )
    block_out = (features.astype(jnp.float32) + branch_cols.astype(jnp.float32)).astype(
        jnp.bfloat16
    )
    first_in, first_out = (
        lax.psum_scatter(
            term_in.astype(jnp.bfloat16), "chan", scatter_dimension=1, tiled=True
        ).astype(jnp.float32),
        lax.psum_scatter(
            term_out.astype(jnp.bfloat16), "chan", scatter_dimension=1, tiled=True
        ).astype(jnp.float32),
    )
    summed_in, summed_out = (
        lax.psum_scatter(first_in, "loop", scatter_dimension=0, tiled=True),
        lax.psum_scatter(first_out, "loop", scatter_dimension=0, tiled=True),
    )
    grad_in_weight = summed_in.reshape(chan_part, loop_part)
    grad_out_weight = summed_out.reshape(loop_part, chan_part)
    padded_back = widen_rows(back_cols, reach_positions)
    grad_sum_rows = cotangent.astype(jnp.float32)
    back_wide = back_cols.astype(jnp.float32)
    kernel_rows = []
    for kernel_tap_index in range(TAPS):
        shift_positions = (kernel_tap_index - middle_position) * DILATION_STEP
        first_back = reach_positions - shift_positions
        grad_sum_rows = grad_sum_rows + kernel_tap_rows[kernel_tap_index] * padded_back[
            first_back : first_back + rows_here
        ].astype(jnp.float32)
        first_in_row = reach_positions + shift_positions
        kernel_rows.append(
            jnp.sum(
                back_wide * padded_in[first_in_row : first_in_row + rows_here].astype(jnp.float32),
                axis=0,
            )
        )
    kernel_terms = jnp.stack(kernel_rows) * grad_scale
    grad_kernel = lax.psum(kernel_terms, "loop")
    return (
        block_out,
        grad_sum_rows.astype(jnp.bfloat16),
        grad_in_weight,
        grad_out_weight,
        grad_kernel,
    )


MESH = pl.DeviceIdType.MESH
MIDDLE = (TAPS - 1) // 2
HBM = pltpu.MemorySpace.HBM


def fused_kernel(
    L, J, grad_scale,
    x_hbm, ct_hbm, taps_hbm, win_hbm, wout_hbm,
    bo_out, gx_out, gw_in_out, gw_out_out, gk_out,
    xp, ctv, tapv, win, wout, wint, woutt, tf, fb, fr, ctf, nb, nrm, istd, act, gp,
    geb, brb, gep, brv, gfull, gsend, grecv, s1s, s1r, s2s, s2r, uf, sb, tr, gka, kt, acc_x,
    load, send, recv,
):
    cl, rows = ctv.shape
    C, F = win.shape
    B = DILATION_STEP
    K = rows // B
    S = K // 2
    W = 2 * B // J
    Z = L // 2
    own = MIDDLE * B
    bf, f32 = jnp.bfloat16, jnp.float32
    me_l, me_j = lax.axis_index("loop"), lax.axis_index("chan")
    core, z = lax.rem(me_l, 2), me_l // 2
    used = [0]

    def take(n=1):
        used[0] += n
        return used[0] - n

    def rcopy(src, dst, idx, l, j):
        return pltpu.make_async_remote_copy(
            src_ref=src, dst_ref=dst, send_sem=send.at[idx], recv_sem=recv.at[idx],
            device_id=(l, j), device_id_type=MESH)

    def lanes(at, n):
        return pl.ds(pl.multiple_of(at, 128), n)

    loads = [pltpu.make_async_copy(a, b, load.at[i]) for i, (a, b) in enumerate((
        (x_hbm, xp.at[:, own:own + rows]), (ct_hbm, ctv), (taps_hbm, tapv), (win_hbm, win), (wout_hbm, wout)))]
    for c in loads:
        c.start()

    chan_peers = [lax.rem(me_j + d, J) for d in range(1, J)]
    loop_peers = [lax.rem(me_l + e, L) for e in range(1, L)]
    right, left = loop_peers[0], loop_peers[-1]

    barrier = pltpu.get_barrier_semaphore()
    for j in chan_peers:
        pl.semaphore_signal(barrier, inc=1, device_id=(me_l, j), device_id_type=MESH)
    for l in loop_peers:
        pl.semaphore_signal(barrier, inc=1, device_id=(l, me_j), device_id_type=MESH)

    half = J // 2
    mine = pl.ds(pl.multiple_of(me_j * cl, cl), cl)

    def col(s, j):
        return lanes((S - 1 - s + (j // half) * (1 + 2 * s)) * B + lax.rem(j, half) * W, W)

    def own_col(s, j):
        return lanes(own + (S - 1 - s + (j // half) * (1 + 2 * s)) * B + lax.rem(j, half) * W, W)

    def block(k):
        return lanes(k * B, B)

    def chan_rows(j):
        return pl.ds(pl.multiple_of(j * cl, cl), cl)

    ct_base, f_base = take(S * (J - 1)), take(S * (J - 1))
    ge_base, br_base = take(S * (J - 1)), take(S * (J - 1))
    xh_base, gh_base = take(S * 2), take(S * 2)
    core_base = take(Z)
    s1_base, s2_base, z_base = take(2 * Z), take(2 * Z), take(Z - 1)

    def ct_copies(s):
        return [rcopy(ctv.at[:, col(s, j)], ctf.at[s, mine, :], ct_base + s * (J - 1) + d, me_l, j)
                for d, j in enumerate(chan_peers)]

    def f_copies(s):
        return [rcopy(fb.at[:, col(s, j)], fr.at[s, mine, :], f_base + s * (J - 1) + d, me_l, j)
                for d, j in enumerate(chan_peers)]

    def ge_copies(s):
        return [rcopy(geb.at[s, chan_rows(j), :], gep.at[:, own_col(s, me_j)], ge_base + s * (J - 1) + d, me_l, j)
                for d, j in enumerate(chan_peers)]

    def br_copies(s):
        return [rcopy(brb.at[s, chan_rows(j), :], brv.at[:, col(s, me_j)], br_base + s * (J - 1) + d, me_l, j)
                for d, j in enumerate(chan_peers)]

    def halo_copies(buf, right_block, left_block, base):
        return [rcopy(buf.at[:, block(right_block + S)], buf.at[:, block(right_block - S)], base, right, me_j),
                rcopy(buf.at[:, block(left_block + S)], buf.at[:, block(left_block + K + S)], base + 1, left, me_j)]

    def xh_copies(s):
        return halo_copies(xp, K - 1 - s, s, xh_base + 2 * s)

    def gh_copies(s):
        return halo_copies(gep, S + s, S - 1 - s, gh_base + 2 * s)

    def start(copies):
        for c in copies:
            c.start()

    def arrive(copies):
        for c in copies:
            c.wait_recv()

    loads[0].wait()
    loads[1].wait()
    pl.semaphore_wait(barrier, J - 1 + L - 1)
    for s in range(S):
        start(xh_copies(s))
    for s in range(S - 1):
        start(ct_copies(s))

    for c in loads[2:]:
        c.wait()
    padded = jnp.concatenate([tapv[...], jnp.zeros((128 - TAPS, cl), f32)], axis=0)
    columns = jnp.concatenate([padded, jnp.zeros((128, 128 - cl), f32)], axis=1).T
    for t in range(TAPS):
        tf[t] = jnp.broadcast_to(columns[0:cl, t:t + 1], (cl, 128))
    wint[...] = win[...].T
    woutt[...] = wout[...].T
    gka[...] = jnp.zeros(gka.shape, f32)
    for s in range(S):
        ctf[s, mine, :] = ctv[:, col(s, me_j)]

    def conv_body(s, carry):
        arrive(xh_copies(s))
        for g in range(cl // 16):
            ch = slice(g * 16, (g + 1) * 16)
            w = [tf[t, ch, :] for t in range(TAPS)]
            for k in (S - 1 - s, S + s):
                for q in range(B // 128):
                    acc = jnp.zeros((16, 128), f32)
                    for t in range(TAPS):
                        acc = acc + w[t] * xp[ch, lanes((k + t) * B + q * 128, 128)].astype(f32)
                    fb[ch, lanes(k * B + q * 128, 128)] = acc.astype(bf)
        start(f_copies(s))
        fr[s, mine, :] = fb[:, col(s, me_j)]

        @pl.when(s == 0)
        def _():
            start(ct_copies(S - 1))
        return carry

    lax.fori_loop(0, S, conv_body, 0)

    def mlp_body(s, carry):
        arrive(ct_copies(s))
        arrive(f_copies(s))
        here = lanes(s * W, W)
        for b in range(W // 128):
            part = slice(b * 128, (b + 1) * 128)
            v = fr[s, :, part].astype(f32)
            centred = v - jnp.mean(v, axis=0, keepdims=True)
            inv = lax.rsqrt(jnp.mean(centred * centred, axis=0, keepdims=True) + epsilon)
            normed = centred * inv
            nrm[:, part] = normed
            istd[:, part] = inv
            nb[:, lanes(s * W + b * 128, 128)] = normed.astype(bf)
        normed_b = nb[:, here]
        up = ctf[s]
        FC = 256
        for f in range(F // FC):
            part = slice(f * FC, (f + 1) * FC)
            pre = jnp.dot(wint[part, :], normed_b, preferred_element_type=f32)
            ga = jnp.dot(wout[part, :], up, preferred_element_type=f32)
            sq = pre * pre
            tangent = jnp.tanh(pre * (gelu_scale + (gelu_scale * cubic_coef) * sq))
            gate = 0.5 + 0.5 * tangent
            slope = gate + pre * (gate * (1.0 - tangent)) * (gelu_scale + (3.0 * gelu_scale * cubic_coef) * sq)
            act[part, here] = (pre * gate).astype(bf)
            gp[part, here] = (ga * slope).astype(bf)
        gn = jnp.dot(win[...], gp[:, here], preferred_element_type=f32)
        for b in range(W // 128):
            part = slice(b * 128, (b + 1) * 128)
            g, normed = gn[:, part], nrm[:, part]
            out = istd[:, part] * (g - jnp.mean(g, axis=0, keepdims=True)
                                   - normed * jnp.mean(g * normed, axis=0, keepdims=True))
            geb[s, :, part] = out.astype(bf)
        start(ge_copies(s))
        gep[:, own_col(s, me_j)] = geb[s, mine, :]
        brb[s] = jnp.dot(woutt[...], act[:, here], preferred_element_type=f32).astype(bf)
        brv[:, col(s, me_j)] = brb[s, mine, :]

        return carry

    lax.fori_loop(0, S, mlp_body, 0)
    start(br_copies(0))

    def forward(s):
        arrive(ge_copies(s))
        start(gh_copies(s))

    def kernel_terms(s):
        for g in range(cl // 16):
            ch = slice(g * 16, (g + 1) * 16)
            sums = [gka[t, ch, :] for t in range(TAPS)]
            for k in (S - 1 - s, S + s):
                for q in range(B // 128):
                    e = gep[ch, lanes(own + k * B + q * 128, 128)].astype(f32)
                    for t in range(TAPS):
                        sums[t] = sums[t] + e * xp[ch, lanes((k + t) * B + q * 128, 128)].astype(f32)
            for t in range(TAPS):
                gka[t, ch, :] = sums[t]

    forward(0)
    CR = C // J

    def core_copy(zz):
        return rcopy(gsend.at[1 - core, zz], grecv.at[zz], core_base + zz, z * 2 + 1 - core, me_j)

    def term_body(e, carry):
        zz = lax.rem(z + 1 + e, Z)
        cols = lanes(zz * 256, 256)
        both = jnp.concatenate([ctf[s] for s in range(S)], axis=1)
        for i, (a, b) in enumerate(((nb[...], gp), (both, act))):
            term = lax.dot_general(a, b[cols, :], (((1,), (1,)), ((), ())), preferred_element_type=f32) * grad_scale
            for h in range(2):
                part = term[:, h * 128:(h + 1) * 128]
                gfull[h, zz, i] = part
                gsend[h, zz, i] = part.astype(bf)
        core_copy(zz).start()

        @pl.when(e == 1)
        def _():
            forward(1)
        return carry

    lax.fori_loop(0, Z, term_body, 0)

    jx = me_j + 1 - 2 * lax.rem(me_j, 2)
    jy = lax.rem(me_j + 2, J)
    jd = lax.rem(jx + 2, J)

    def piece(j):
        return pl.ds(pl.multiple_of(j * CR, CR), CR)

    def s1_copies(zz):
        return [rcopy(s1s.at[zz, i], s1r.at[zz, i], s1_base + 2 * zz + i, me_l, j) for i, j in enumerate((jx, jy))]

    def s2_copies(zz):
        return [rcopy(s2s.at[zz, i], s2r.at[zz, i], s2_base + 2 * zz + i, me_l, j) for i, j in enumerate((jy, jx))]

    def z_copy(e):
        zz = lax.rem(z + 1 + e, Z)
        return rcopy(sb.at[zz], tr.at[z], z_base + e, zz * 2 + core, me_j)

    def core_sum(e, carry):
        zz = lax.rem(z + 1 + e, Z)
        core_copy(zz).wait_recv()
        for i, j in enumerate((jx, jy)):
            gfull[core, zz, i] = gfull[core, zz, i] + grecv[zz, i].astype(f32)
            s1s[zz, i, 0] = gfull[core, zz, i, piece(j), :].astype(bf)
            s1s[zz, i, 1] = gfull[core, zz, i, piece(jd), :].astype(bf)
        start(s1_copies(zz))

        @pl.when(e == 1)
        def _():
            forward(2)
        return carry

    lax.fori_loop(0, Z, core_sum, 0)
    start(br_copies(1))

    def halving(e, carry):
        zz = lax.rem(z + 1 + e, Z)
        arrive(s1_copies(zz))
        for i, j in enumerate((jy, jx)):
            s2s[zz, i] = (gfull[core, zz, i, piece(j), :] + s1r[zz, i, 1].astype(f32)).astype(bf)
            uf[zz, i] = gfull[core, zz, i, piece(me_j), :] + s1r[zz, i, 0].astype(f32)
        start(s2_copies(zz))

        @pl.when(e == Z - 2)
        def _():
            start(br_copies(2))
        return carry

    def z_stage(e, carry):
        zz = lax.rem(z + 1 + e, Z)
        arrive(s2_copies(zz))
        total = uf[zz] + s2r[zz].astype(f32)
        uf[zz] = total
        sb[zz] = total.astype(bf)

        @pl.when(e < Z - 1)
        def _():
            z_copy(e).start()
        return carry

    def early_terms(s, carry):
        kernel_terms(s)
        return carry

    lax.fori_loop(0, S - 1, early_terms, 0)
    forward(S - 1)
    kernel_terms(S - 1)
    sums = [jnp.sum(gka[t], axis=1, keepdims=True) * grad_scale for t in range(TAPS)]
    total = jnp.concatenate(sums + [jnp.zeros((cl, 128 - TAPS), f32)], axis=1)
    total = jnp.concatenate([total, jnp.zeros((128 - cl, 128), f32)], axis=0).T
    kt[me_l] = total[0:16]
    kt_in = [rcopy(kt.at[me_l], kt.at[me_l], take(), l, me_j) for l in loop_peers]
    start(kt_in)

    def back(final):
        late = (S - 1, S, S + K - 1, S + K)

        def part(q, carry):
            for g in range(cl // 16):
                ch = slice(g * 16, (g + 1) * 16)
                w = [tf[t, ch, :] for t in range(TAPS)]
                for k in range(K):
                    at = lanes(k * B + q * 128, 128)
                    acc = acc_x[ch, at] if final else ctv[ch, at].astype(f32)
                    for t in range(TAPS):
                        b = k + TAPS - 1 - t
                        if (b in late) == final:
                            acc = acc + w[t] * gep[ch, lanes(b * B + q * 128, 128)].astype(f32)
                    if final:
                        gx_out[ch, at] = acc.astype(bf)
                    else:
                        acc_x[ch, at] = acc
            return carry

        lax.fori_loop(0, B // 128, part, 0)

    for s in range(S - 1):
        arrive(gh_copies(s))
    back(False)
    lax.fori_loop(0, Z, halving, 0)
    start(br_copies(3))
    arrive(gh_copies(S - 1))
    back(True)
    lax.fori_loop(0, Z, z_stage, 0)

    def finish(s, carry):
        arrive(br_copies(s))
        for k in (S - 1 - s, S + s):
            bo_out[:, block(k)] = (xp[:, block(k + S)].astype(f32) + brv[:, block(k)].astype(f32)).astype(bf)
        return carry

    lax.fori_loop(0, S, finish, 0)
    arrive(kt_in)
    total = kt[0]
    for l in range(1, L):
        total = total + kt[l]
    gk_out[...] = total[0:TAPS, 0:cl]
    for e in range(Z - 1):
        z_copy(e).wait_recv()
    total = uf[z]
    for e in range(1, Z):
        total = total + tr[lax.rem(z + Z - e, Z)].astype(f32)
    gw_in_out[...] = total[0]
    gw_out_out[...] = total[1]

    def sent(s, carry):
        for copies in (ct_copies(s), f_copies(s), ge_copies(s), br_copies(s), xh_copies(s), gh_copies(s)):
            for c in copies:
                c.wait_send()
        return carry

    lax.fori_loop(0, S, sent, 0)
    for zz in range(Z):
        for c in [core_copy(zz)] + s1_copies(zz) + s2_copies(zz):
            c.wait_send()
    for c in kt_in + [z_copy(e) for e in range(Z - 1)]:
        c.wait_send()


def flush_kernel(*refs):
    n = len(refs) // 2
    sems = refs[2 * n]
    copies = [pltpu.make_async_copy(refs[i], refs[n + i], sems.at[i]) for i in range(n)]
    for c in copies:
        c.start()
    for c in copies:
        c.wait()


def fits(L, J, rows, cl, F):
    return (cl * 2 == 128 and rows == 2 * MIDDLE * DILATION_STEP and L % 2 == 0 and L > 2 and J == 4
            and F == L * 128)


def fused_shards(features, kernel_tap_rows, in_weight, out_weight, cotangent):
    L, J = lax.axis_size("loop"), lax.axis_size("chan")
    rows, cl = features.shape
    C, F = in_weight.shape
    if not fits(L, J, rows, cl, F):
        return shards(features, kernel_tap_rows, in_weight, out_weight, cotangent)
    N = rows // J
    K = rows // DILATION_STEP
    S = K // 2
    W = N // S
    Z = L // 2
    CR = C // J
    bf, f32 = jnp.bfloat16, jnp.float32
    ext = rows + 2 * MIDDLE * DILATION_STEP
    scratch = [
        pltpu.VMEM((cl, ext), bf),
        pltpu.VMEM((cl, rows), bf),
        pltpu.VMEM((TAPS, cl), f32),
        pltpu.VMEM((C, F), bf),
        pltpu.VMEM((F, C), bf),
        pltpu.VMEM((F, C), bf),
        pltpu.VMEM((C, F), bf),
        pltpu.VMEM((TAPS, cl, 128), f32),
        pltpu.VMEM((cl, rows), bf),
        pltpu.VMEM((S, C, W), bf),
        pltpu.VMEM((S, C, W), bf),
        pltpu.VMEM((C, N), bf),
        pltpu.VMEM((C, W), f32),
        pltpu.VMEM((1, W), f32),
        pltpu.VMEM((F, N), bf),
        pltpu.VMEM((F, N), bf),
        pltpu.VMEM((S, C, W), bf),
        pltpu.VMEM((S, C, W), bf),
        pltpu.VMEM((cl, ext), bf),
        pltpu.VMEM((cl, rows), bf),
        pltpu.VMEM((2, Z, 2, C, 128), f32),
        pltpu.VMEM((2, Z, 2, C, 128), bf),
        pltpu.VMEM((Z, 2, C, 128), bf),
        pltpu.VMEM((Z, 2, 2, CR, 128), bf),
        pltpu.VMEM((Z, 2, 2, CR, 128), bf),
        pltpu.VMEM((Z, 2, CR, 128), bf),
        pltpu.VMEM((Z, 2, CR, 128), bf),
        pltpu.VMEM((Z, 2, CR, 128), f32),
        pltpu.VMEM((Z, 2, CR, 128), bf),
        pltpu.VMEM((Z, 2, CR, 128), bf),
        pltpu.VMEM((TAPS, cl, 128), f32),
        pltpu.VMEM((L, 16, 128), f32),
        pltpu.VMEM((cl, rows), f32),
    ]
    copies = 4 * S * (J - 1) + 4 * S + 5 * Z + (L - 1) + (Z - 1)
    scratch += [pltpu.SemaphoreType.DMA((5,)), pltpu.SemaphoreType.DMA((copies,)), pltpu.SemaphoreType.DMA((copies,))]
    vmem = pl.BlockSpec(memory_space=pltpu.VMEM)
    hbm = pl.BlockSpec(memory_space=HBM)
    shapes = (
        jax.ShapeDtypeStruct((cl, rows), bf),
        jax.ShapeDtypeStruct((cl, rows), bf),
        jax.ShapeDtypeStruct((CR, F // L), f32),
        jax.ShapeDtypeStruct((CR, F // L), f32),
        jax.ShapeDtypeStruct((TAPS, cl), f32),
    )
    results = pl.pallas_call(
        functools.partial(fused_kernel, L, J, 1.0 / math.sqrt(rows * L)),
        out_shape=shapes,
        in_specs=[hbm] * 5,
        out_specs=(vmem,) * 5,
        scratch_shapes=scratch,
        compiler_params=pltpu.CompilerParams(
            collective_id=0, has_side_effects=True, vmem_limit_bytes=50 * 1024 * 1024),
        cost_estimate=pl.CostEstimate(flops=12 * N * C * F, bytes_accessed=8 * rows * cl * 2, transcendentals=N * F),
    )(*[pltpu.with_memory_space_constraint(a, HBM)
        for a in (features.T, cotangent.T, kernel_tap_rows, in_weight, out_weight)])
    bo, gx, gw_in, gw_out, gk = pl.pallas_call(
        flush_kernel,
        out_shape=shapes,
        in_specs=[pl.BlockSpec(memory_space=pl.ANY)] * 5,
        out_specs=(hbm,) * 5,
        scratch_shapes=[pltpu.SemaphoreType.DMA((5,))],
        compiler_params=pltpu.CompilerParams(vmem_limit_bytes=1024 * 1024),
    )(*results)
    return bo.T, gx.T, gw_in, gw_out.T, gk


def solution(mesh):
    placed = (P("loop", "chan"), P(None, "chan"), P(), P(), P("loop", "chan"))
    return jax.shard_map(
        fused_shards,
        mesh=mesh,
        in_specs=placed,
        out_specs=(
            P("loop", "chan"),
            P("loop", "chan"),
            P("chan", "loop"),
            P("loop", "chan"),
            P(None, "chan"),
        ),
        check_vma=False,
    )
```

```python
import functools
import math

import jax
import jax.numpy as jnp
from jax import lax
from jax.experimental import pallas as pl
from jax.experimental.pallas import tpu as pltpu
from jax.sharding import PartitionSpec as P

TAPS = 9
DILATION_STEP = 512


gelu_scale = math.sqrt(2.0 / math.pi)
cubic_coef = 0.044715
epsilon = 1e-05


def with_halo(cells, sides, width):
    for axis, dim in sides:
        count = lax.axis_size(axis)
        head = lax.slice_in_dim(cells, 0, width, axis=dim)
        tail = lax.slice_in_dim(cells, cells.shape[dim] - width, cells.shape[dim], axis=dim)
        cells = jnp.concatenate(
            [
                lax.ppermute(tail, axis, [(i, (i + 1) % count) for i in range(count)]),
                cells,
                lax.ppermute(head, axis, [((i + 1) % count, i) for i in range(count)]),
            ],
            axis=dim,
        )
    return cells


def gelu_pair(inputs):
    inner_arg = gelu_scale * (inputs + cubic_coef * inputs * inputs * inputs)
    tangent = jnp.tanh(inner_arg)
    act_value = 0.5 * inputs * (1.0 + tangent)
    act_slope = 0.5 * (1.0 + tangent) + 0.5 * inputs * (1.0 - tangent * tangent) * gelu_scale * (
        1.0 + 3.0 * cubic_coef * inputs * inputs
    )
    return (act_value, act_slope)


def widen_rows(field_rows, reach_positions):
    return with_halo(field_rows, (("loop", 0),), reach_positions)


def shards(features, kernel_tap_rows, in_weight, out_weight, cotangent):
    middle_position = (TAPS - 1) // 2
    reach_positions = middle_position * DILATION_STEP
    loop_size = lax.axis_size("loop")
    chan_size = lax.axis_size("chan")
    rows_here = features.shape[0]
    grad_scale = 1.0 / math.sqrt(rows_here * loop_size)
    padded_in = widen_rows(features, reach_positions)
    blended_sum = jnp.zeros(features.shape, jnp.float32)
    for kernel_tap_index in range(TAPS):
        leading_row = reach_positions + (kernel_tap_index - middle_position) * DILATION_STEP
        blended_sum = blended_sum + kernel_tap_rows[kernel_tap_index] * padded_in[
            leading_row : leading_row + rows_here
        ].astype(jnp.float32)
    filtered = blended_sum.astype(jnp.bfloat16)
    row_block, upstream = (
        lax.all_to_all(filtered, "chan", split_axis=0, concat_axis=1, tiled=True),
        lax.all_to_all(cotangent, "chan", split_axis=0, concat_axis=1, tiled=True),
    )
    values = row_block.astype(jnp.float32)
    mean_value = jnp.mean(values, axis=-1, keepdims=True)
    centred = values - mean_value
    variance = jnp.mean(centred * centred, axis=-1, keepdims=True)
    inv_std = lax.rsqrt(variance + epsilon)
    normed = centred * inv_std
    normed_b = normed.astype(jnp.bfloat16)
    hidden_pre = jnp.dot(normed_b, in_weight, preferred_element_type=jnp.float32)
    act_value, act_slope = gelu_pair(hidden_pre)
    act_b = act_value.astype(jnp.bfloat16)
    branch = jnp.dot(act_b, out_weight, preferred_element_type=jnp.float32).astype(jnp.bfloat16)
    grad_act = jnp.einsum("pc,fc->pf", upstream, out_weight, preferred_element_type=jnp.float32)
    grad_pre = (grad_act * act_slope).astype(jnp.bfloat16)
    grad_normed = jnp.einsum("pf,cf->pc", grad_pre, in_weight, preferred_element_type=jnp.float32)
    grad_filtered = inv_std * (
        grad_normed
        - jnp.mean(grad_normed, axis=-1, keepdims=True)
        - normed * jnp.mean(grad_normed * normed, axis=-1, keepdims=True)
    )
    back_rows = grad_filtered.astype(jnp.bfloat16)
    local_rows = row_block.shape[0]
    width_c = row_block.shape[1]
    width_f = hidden_pre.shape[1]
    chan_part = width_c // chan_size
    loop_part = width_f // loop_size
    normed_parts = normed_b.reshape(local_rows, chan_size, chan_part)
    upstream_parts = upstream.reshape(local_rows, chan_size, chan_part)
    grad_parts = grad_pre.reshape(local_rows, loop_size, loop_part)
    act_parts = act_b.reshape(local_rows, loop_size, loop_part)
    term_in = (
        jnp.einsum("pai,pbj->baij", normed_parts, grad_parts, preferred_element_type=jnp.float32)
        * grad_scale
    )
    term_out = (
        jnp.einsum("pbj,pai->baji", act_parts, upstream_parts, preferred_element_type=jnp.float32)
        * grad_scale
    )
    branch_cols, back_cols = (
        lax.all_to_all(branch, "chan", split_axis=1, concat_axis=0, tiled=True),
        lax.all_to_all(back_rows, "chan", split_axis=1, concat_axis=0, tiled=True),
    )
    block_out = (features.astype(jnp.float32) + branch_cols.astype(jnp.float32)).astype(
        jnp.bfloat16
    )
    first_in, first_out = (
        lax.psum_scatter(
            term_in.astype(jnp.bfloat16), "chan", scatter_dimension=1, tiled=True
        ).astype(jnp.float32),
        lax.psum_scatter(
            term_out.astype(jnp.bfloat16), "chan", scatter_dimension=1, tiled=True
        ).astype(jnp.float32),
    )
    summed_in, summed_out = (
        lax.psum_scatter(first_in, "loop", scatter_dimension=0, tiled=True),
        lax.psum_scatter(first_out, "loop", scatter_dimension=0, tiled=True),
    )
    grad_in_weight = summed_in.reshape(chan_part, loop_part)
    grad_out_weight = summed_out.reshape(loop_part, chan_part)
    padded_back = widen_rows(back_cols, reach_positions)
    grad_sum_rows = cotangent.astype(jnp.float32)
    back_wide = back_cols.astype(jnp.float32)
    kernel_rows = []
    for kernel_tap_index in range(TAPS):
        shift_positions = (kernel_tap_index - middle_position) * DILATION_STEP
        first_back = reach_positions - shift_positions
        grad_sum_rows = grad_sum_rows + kernel_tap_rows[kernel_tap_index] * padded_back[
            first_back : first_back + rows_here
        ].astype(jnp.float32)
        first_in_row = reach_positions + shift_positions
        kernel_rows.append(
            jnp.sum(
                back_wide * padded_in[first_in_row : first_in_row + rows_here].astype(jnp.float32),
                axis=0,
            )
        )
    kernel_terms = jnp.stack(kernel_rows) * grad_scale
    grad_kernel = lax.psum(kernel_terms, "loop")
    return (
        block_out,
        grad_sum_rows.astype(jnp.bfloat16),
        grad_in_weight,
        grad_out_weight,
        grad_kernel,
    )


MESH = pl.DeviceIdType.MESH
MIDDLE = (TAPS - 1) // 2
HBM = pltpu.MemorySpace.HBM


def fused_kernel(
    L, J, grad_scale,
    x_hbm, ct_hbm, taps_hbm, win_hbm, wout_hbm,
    bo_out, gx_out, gw_in_out, gw_out_out, gk_out,
    xp, ctv, tapv, win, wout, wint, woutt, tf, fb, fr, ctf, nb, nrm, istd, act, gp,
    geb, brb, gep, brv, gfull, gsend, grecv, s1s, s1r, s2s, s2r, uf, sb, tr, gka, kt, kr, acc_x,
    load, send, recv,
):
    cl, rows = ctv.shape
    C, F = win.shape
    B = DILATION_STEP
    K = rows // B
    S = K // 2
    W = 2 * B // J
    V = (J - 1) * cl
    Z = L // 2
    own = MIDDLE * B
    bf, f32 = jnp.bfloat16, jnp.float32
    me_l, me_j = lax.axis_index("loop"), lax.axis_index("chan")
    core, z = lax.rem(me_l, 2), me_l // 2
    ct_r, f_r, ge_r, xh_r, core_r, s1_r, s2_r = [S * i for i in range(7)]
    br_r = 7 * S
    gh_r, z_r, kt_r = br_r + 2, br_r + 4, br_r + 5
    ct_s, f_s, ge_s, br_s, xh_s, gh_s, core_s, s1_s, s2_s, z_s, kt_s = range(11)

    def rcopy(src, dst, out, into, l, j):
        return pltpu.make_async_remote_copy(
            src_ref=src, dst_ref=dst, send_sem=send.at[out], recv_sem=recv.at[into],
            device_id=(l, j), device_id_type=MESH)

    def await_all(like, sem):
        pltpu.make_async_copy(like, like, sem).wait()

    def got(like, into):
        await_all(like, recv.at[into])

    def lanes(at, n):
        return pl.ds(pl.multiple_of(at, 128), n)

    jx = me_j + 1 - 2 * lax.rem(me_j, 2)
    jy = lax.rem(me_j + 2, J)
    jd = lax.rem(jx + 2, J)
    chan_peers = [jd, jx, jy]
    loop_peers = [lax.rem(me_l + e, L) for e in range(1, L)]
    right, left = loop_peers[0], loop_peers[-1]

    barrier = pltpu.get_barrier_semaphore()
    for j in chan_peers:
        pl.semaphore_signal(barrier, inc=1, device_id=(me_l, j), device_id_type=MESH)
    for l in loop_peers:
        pl.semaphore_signal(barrier, inc=1, device_id=(l, me_j), device_id_type=MESH)

    loads = [pltpu.make_async_copy(a, b, load.at[i]) for i, (a, b) in enumerate((
        (x_hbm, xp.at[:, own:own + rows]), (ct_hbm, ctv), (taps_hbm, tapv), (win_hbm, win), (wout_hbm, wout)))]
    for c in loads[:3]:
        c.start()

    half = J // 2
    mine = pl.ds(pl.multiple_of(me_j * cl, cl), cl)

    def col(s, j):
        return lanes((S - 1 - s + (j // half) * (1 + 2 * s)) * B + lax.rem(j, half) * W, W)

    def own_col(s, j):
        return lanes(own + (S - 1 - s + (j // half) * (1 + 2 * s)) * B + lax.rem(j, half) * W, W)

    def block(k):
        return lanes(k * B, B)

    def chan_rows(j):
        return pl.ds(pl.multiple_of(j * cl, cl), cl)

    def ct_copies(s):
        return [rcopy(ct_hbm.at[:, col(s, j)], ctf.at[s, mine, :], ct_s, ct_r + s, me_l, j) for j in chan_peers]

    def f_copies(s):
        return [rcopy(fb.at[:, col(s, j)], fr.at[s, mine, :], f_s, f_r + s, me_l, j) for j in chan_peers]

    def ge_copies(s):
        return [rcopy(geb.at[s, chan_rows(j), :], gep.at[:, own_col(s, me_j)], ge_s, ge_r + s, me_l, j)
                for j in chan_peers]

    def br_copies(s):
        return [rcopy(brb.at[s, chan_rows(j), :], brv.at[:, col(s, me_j)], br_s, br_r + s // (S - 1), me_l, j)
                for j in chan_peers]

    def xh_copies(s):
        return [rcopy(x_hbm.at[:, block(K - 1 - s)], xp.at[:, block(S - 1 - s)], xh_s, xh_r + s, right, me_j),
                rcopy(x_hbm.at[:, block(s)], xp.at[:, block(K + S + s)], xh_s, xh_r + s, left, me_j)]

    def gh_copies(s):
        near, far, into = S - 1 - s, S + s, gh_r + s // (S - 1)
        return [rcopy(gep.at[:, block(far + S)], gep.at[:, block(far - S)], gh_s, into, right, me_j),
                rcopy(gep.at[:, block(near + S)], gep.at[:, block(near + K + S)], gh_s, into, left, me_j)]

    def start(copies):
        for c in copies:
            c.start()

    pl.semaphore_wait(barrier, J - 1 + L - 1)
    start(xh_copies(0))
    start(ct_copies(0))
    for s in range(1, S):
        start(xh_copies(s))
        start(ct_copies(s))
    for c in loads[3:]:
        c.start()
    for c in loads:
        c.wait()
    padded = jnp.concatenate([tapv[...], jnp.zeros((128 - TAPS, cl), f32)], axis=0)
    columns = jnp.concatenate([padded, jnp.zeros((128, 128 - cl), f32)], axis=1).T
    for t in range(TAPS):
        tf[t] = jnp.broadcast_to(columns[0:cl, t:t + 1], (cl, 128))
    wint[...] = win[...].T
    woutt[...] = wout[...].T
    gka[...] = jnp.zeros(gka.shape, f32)
    for s in range(S):
        ctf[s, mine, :] = ctv[:, col(s, me_j)]

    def conv(s):
        near, far = S - 1 - s, S + s

        def part(q, carry):
            done = []
            for g in range(cl // 16):
                ch = slice(g * 16, (g + 1) * 16)
                w = [tf[t, ch, :] for t in range(TAPS)]
                sums = [jnp.zeros((16, 128), f32) for _ in range(2)]
                for b in range(near, far + TAPS):
                    v = xp[ch, lanes(b * B + q * 128, 128)].astype(f32)
                    for i, k in enumerate((near, far)):
                        if 0 <= b - k < TAPS:
                            sums[i] = sums[i] + w[b - k] * v
                done.append([a.astype(bf) for a in sums])
            for g in range(cl // 16):
                for i, k in enumerate((near, far)):
                    fb[g * 16:(g + 1) * 16, lanes(k * B + q * 128, 128)] = done[g][i]
            return carry

        lax.fori_loop(0, B // 128, part, 0)

    for s in range(S):
        got(xp.at[:, 0:2 * B], xh_r + s)
        conv(s)
        start(f_copies(s))
        fr[s, mine, :] = fb[:, col(s, me_j)]

    def mlp_body(s, carry):
        got(ctf.at[s, 0:V, :], ct_r + s)
        got(fr.at[s, 0:V, :], f_r + s)
        here = lanes(s * W, W)
        for b in range(W // 128):
            part = slice(b * 128, (b + 1) * 128)
            v = fr[s, :, part].astype(f32)
            centred = v - jnp.mean(v, axis=0, keepdims=True)
            inv = lax.rsqrt(jnp.mean(centred * centred, axis=0, keepdims=True) + epsilon)
            normed = centred * inv
            nrm[:, part] = normed
            istd[:, part] = inv
            nb[:, lanes(s * W + b * 128, 128)] = normed.astype(bf)
        normed_b = nb[:, here]
        up = ctf[s]
        FC = 256
        for f in range(F // FC):
            part = slice(f * FC, (f + 1) * FC)
            pre = jnp.dot(wint[part, :], normed_b, preferred_element_type=f32)
            ga = jnp.dot(wout[part, :], up, preferred_element_type=f32)
            sq = pre * pre
            tangent = jnp.tanh(pre * (gelu_scale + (gelu_scale * cubic_coef) * sq))
            gate = 0.5 + 0.5 * tangent
            slope = gate + pre * (gate * (1.0 - tangent)) * (gelu_scale + (3.0 * gelu_scale * cubic_coef) * sq)
            act[part, here] = (pre * gate).astype(bf)
            gp[part, here] = (ga * slope).astype(bf)
        gn = jnp.dot(win[...], gp[:, here], preferred_element_type=f32)
        for b in range(W // 128):
            part = slice(b * 128, (b + 1) * 128)
            g, normed = gn[:, part], nrm[:, part]
            out = istd[:, part] * (g - jnp.mean(g, axis=0, keepdims=True)
                                   - normed * jnp.mean(g * normed, axis=0, keepdims=True))
            geb[s, :, part] = out.astype(bf)
        start(ge_copies(s))
        gep[:, own_col(s, me_j)] = geb[s, mine, :]
        brb[s] = jnp.dot(woutt[...], act[:, here], preferred_element_type=f32).astype(bf)
        brv[:, col(s, me_j)] = brb[s, mine, :]

        return carry

    lax.fori_loop(0, S, mlp_body, 0)

    def forward(s):
        got(gep.at[:, 0:(J - 1) * W], ge_r + s)
        start(gh_copies(s))

    def kernel_terms(s):
        near, far = S - 1 - s, S + s
        for g in range(cl // 16):
            ch = slice(g * 16, (g + 1) * 16)
            sums = [gka[t, ch, :] for t in range(TAPS)]
            for q in range(B // 128):
                e = [gep[ch, lanes(own + k * B + q * 128, 128)].astype(f32) for k in (near, far)]
                for b in range(near, far + TAPS):
                    v = xp[ch, lanes(b * B + q * 128, 128)].astype(f32)
                    for i, k in enumerate((near, far)):
                        if 0 <= b - k < TAPS:
                            sums[b - k] = sums[b - k] + e[i] * v
            for t in range(TAPS):
                gka[t, ch, :] = sums[t]

    CR = C // J

    def core_copy(zz):
        return rcopy(gsend.at[1 - core, zz], grecv.at[zz], core_s, core_r + zz, z * 2 + 1 - core, me_j)

    def term_body(e, carry):
        zz = lax.rem(z + 1 + e, Z)
        cols = lanes(zz * 256, 256)
        both = jnp.concatenate([ctf[s] for s in range(S)], axis=1)
        for i, (a, b) in enumerate(((nb[...], gp), (both, act))):
            term = lax.dot_general(a, b[cols, :], (((1,), (1,)), ((), ())), preferred_element_type=f32) * grad_scale
            for h in range(2):
                part = term[:, h * 128:(h + 1) * 128]
                gfull[h, zz, i] = part
                gsend[h, zz, i] = part.astype(bf)
        core_copy(zz).start()

        @pl.when(e == 2)
        def _():
            forward(1)

        @pl.when(e >= 2)
        def _():
            core_sum(e - 2)
        return carry

    def piece(j):
        return pl.ds(pl.multiple_of(j * CR, CR), CR)

    def s1_copies(zz):
        return [rcopy(s1s.at[zz, i], s1r.at[zz, i], s1_s, s1_r + zz, me_l, j) for i, j in enumerate((jx, jy))]

    def s2_copies(zz):
        return [rcopy(s2s.at[zz, i], s2r.at[zz, i], s2_s, s2_r + zz, me_l, j) for i, j in enumerate((jy, jx))]

    def z_copy(e):
        zz = lax.rem(z + 1 + e, Z)
        return rcopy(sb.at[zz], tr.at[z - (z > zz).astype(jnp.int32)], z_s, z_r, zz * 2 + core, me_j)

    def core_sum(e):
        zz = lax.rem(z + 1 + e, Z)
        got(grecv.at[zz], core_r + zz)
        for i, j in enumerate((jx, jy)):
            gfull[core, zz, i] = gfull[core, zz, i] + grecv[zz, i].astype(f32)
            s1s[zz, i, 0] = gfull[core, zz, i, piece(j), :].astype(bf)
            s1s[zz, i, 1] = gfull[core, zz, i, piece(jd), :].astype(bf)
        start(s1_copies(zz))

    def halving(e):
        zz = lax.rem(z + 1 + e, Z)
        got(s1r.at[zz], s1_r + zz)
        for i, j in enumerate((jy, jx)):
            s2s[zz, i] = (gfull[core, zz, i, piece(j), :] + s1r[zz, i, 1].astype(f32)).astype(bf)
            uf[zz, i] = gfull[core, zz, i, piece(me_j), :] + s1r[zz, i, 0].astype(f32)
        start(s2_copies(zz))

    def z_stage(e):
        zz = lax.rem(z + 1 + e, Z)
        got(s2r.at[zz], s2_r + zz)
        total = uf[zz] + s2r[zz].astype(f32)
        uf[zz] = total
        sb[zz] = total.astype(bf)

        if e < Z - 1:
            z_copy(e).start()

    def back(final):
        late = (S - 1, S, S + K - 1, S + K)

        def part(q, carry):
            for g in range(cl // 16):
                ch = slice(g * 16, (g + 1) * 16)
                w = [tf[t, ch, :] for t in range(TAPS)]
                at = [lanes(k * B + q * 128, 128) for k in range(K)]
                sums = [acc_x[ch, a] if final else ctv[ch, a].astype(f32) for a in at]
                for b in range(K + 2 * S):
                    if (b in late) == final:
                        v = gep[ch, lanes(b * B + q * 128, 128)].astype(f32)
                        for t in range(TAPS):
                            k = b - (TAPS - 1 - t)
                            if 0 <= k < K:
                                sums[k] = sums[k] + w[t] * v
                for k in range(K):
                    if final:
                        gx_out[ch, at[k]] = sums[k].astype(bf)
                    else:
                        acc_x[ch, at[k]] = sums[k]
            return carry

        lax.fori_loop(0, B // 128, part, 0)

    forward(0)
    lax.fori_loop(0, Z, term_body, 0)
    core_sum(Z - 2)
    kernel_terms(0)
    core_sum(Z - 1)
    start(br_copies(0))
    start(br_copies(1))
    kernel_terms(1)
    forward(2)
    kernel_terms(2)
    forward(3)
    halving(0)
    kernel_terms(3)
    halving(1)
    sums = [jnp.sum(gka[t], axis=1, keepdims=True) * grad_scale for t in range(TAPS)]
    total = jnp.concatenate(sums + [jnp.zeros((cl, 128 - TAPS), f32)], axis=1)
    total = jnp.concatenate([total, jnp.zeros((128 - cl, 128), f32)], axis=0).T
    kt[me_l] = total[0:16]
    start([rcopy(kt.at[me_l], kr.at[me_l - (me_l > l).astype(jnp.int32)], kt_s, kt_r, l, me_j) for l in loop_peers])

    halving(2)
    start(br_copies(2))
    halving(3)
    start(br_copies(3))
    z_stage(0)
    got(gep.at[:, 0:(S - 1) * 2 * B], gh_r)
    back(False)
    z_stage(1)
    z_stage(2)
    got(gep.at[:, 0:2 * B], gh_r + 1)
    back(True)
    z_stage(3)

    def finish(k, carry):
        bo_out[:, block(k)] = (xp[:, block(k + S)].astype(f32) + brv[:, block(k)].astype(f32)).astype(bf)
        return carry

    got(brv.at[:, 0:(S - 1) * (J - 1) * W], br_r)
    lax.fori_loop(1, K - 1, finish, 0)
    got(kr, kt_r)
    total = kt[me_l]
    for l in range(L - 1):
        total = total + kr[l]
    gk_out[...] = total[0:TAPS, 0:cl]
    got(brv.at[:, 0:(J - 1) * W], br_r + 1)
    finish(0, 0)
    finish(K - 1, 0)
    got(tr, z_r)
    total = uf[z]
    for e in range(Z - 1):
        total = total + tr[e].astype(f32)
    gw_in_out[...] = total[0]
    gw_out_out[...] = total[1]
    for like, out in ((ctv.at[:, 0:S * (J - 1) * W], ct_s), (fb.at[:, 0:S * (J - 1) * W], f_s), (geb.at[:, 0:V, :], ge_s),
                      (brb.at[:, 0:V, :], br_s), (xp.at[:, 0:2 * S * B], xh_s), (gep.at[:, 0:2 * S * B], gh_s),
                      (gsend.at[0], core_s), (s1s, s1_s), (s2s, s2_s), (sb.at[0:Z - 1], z_s), (kt.at[0:L - 1], kt_s)):
        await_all(like, send.at[out])


def flush_kernel(*refs):
    n = len(refs) // 2
    sems = refs[2 * n]
    copies = [pltpu.make_async_copy(refs[i], refs[n + i], sems.at[i]) for i in range(n)]
    for c in copies:
        c.start()
    for c in copies:
        c.wait()


def fits(L, J, rows, cl, F):
    return (cl * 2 == 128 and rows == 2 * MIDDLE * DILATION_STEP and L % 2 == 0 and L > 2 and J == 4
            and F == L * 128 and L == 2 * MIDDLE)


def fused_shards(features, kernel_tap_rows, in_weight, out_weight, cotangent):
    L, J = lax.axis_size("loop"), lax.axis_size("chan")
    rows, cl = features.shape
    C, F = in_weight.shape
    if not fits(L, J, rows, cl, F):
        return shards(features, kernel_tap_rows, in_weight, out_weight, cotangent)
    N = rows // J
    K = rows // DILATION_STEP
    S = K // 2
    W = N // S
    Z = L // 2
    CR = C // J
    bf, f32 = jnp.bfloat16, jnp.float32
    ext = rows + 2 * MIDDLE * DILATION_STEP
    scratch = [
        pltpu.VMEM((cl, ext), bf),
        pltpu.VMEM((cl, rows), bf),
        pltpu.VMEM((TAPS, cl), f32),
        pltpu.VMEM((C, F), bf),
        pltpu.VMEM((F, C), bf),
        pltpu.VMEM((F, C), bf),
        pltpu.VMEM((C, F), bf),
        pltpu.VMEM((TAPS, cl, 128), f32),
        pltpu.VMEM((cl, rows), bf),
        pltpu.VMEM((S, C, W), bf),
        pltpu.VMEM((S, C, W), bf),
        pltpu.VMEM((C, N), bf),
        pltpu.VMEM((C, W), f32),
        pltpu.VMEM((1, W), f32),
        pltpu.VMEM((F, N), bf),
        pltpu.VMEM((F, N), bf),
        pltpu.VMEM((S, C, W), bf),
        pltpu.VMEM((S, C, W), bf),
        pltpu.VMEM((cl, ext), bf),
        pltpu.VMEM((cl, rows), bf),
        pltpu.VMEM((2, Z, 2, C, 128), f32),
        pltpu.VMEM((2, Z, 2, C, 128), bf),
        pltpu.VMEM((Z, 2, C, 128), bf),
        pltpu.VMEM((Z, 2, 2, CR, 128), bf),
        pltpu.VMEM((Z, 2, 2, CR, 128), bf),
        pltpu.VMEM((Z, 2, CR, 128), bf),
        pltpu.VMEM((Z, 2, CR, 128), bf),
        pltpu.VMEM((Z, 2, CR, 128), f32),
        pltpu.VMEM((Z, 2, CR, 128), bf),
        pltpu.VMEM((Z - 1, 2, CR, 128), bf),
        pltpu.VMEM((TAPS, cl, 128), f32),
        pltpu.VMEM((L, 16, 128), f32),
        pltpu.VMEM((L - 1, 16, 128), f32),
        pltpu.VMEM((cl, rows), f32),
    ]
    scratch += [pltpu.SemaphoreType.DMA((5,)), pltpu.SemaphoreType.DMA((11,)), pltpu.SemaphoreType.DMA((7 * S + 6,))]
    vmem = pl.BlockSpec(memory_space=pltpu.VMEM)
    hbm = pl.BlockSpec(memory_space=HBM)
    shapes = (
        jax.ShapeDtypeStruct((cl, rows), bf),
        jax.ShapeDtypeStruct((cl, rows), bf),
        jax.ShapeDtypeStruct((CR, F // L), f32),
        jax.ShapeDtypeStruct((CR, F // L), f32),
        jax.ShapeDtypeStruct((TAPS, cl), f32),
    )
    results = pl.pallas_call(
        functools.partial(fused_kernel, L, J, 1.0 / math.sqrt(rows * L)),
        out_shape=shapes,
        in_specs=[hbm] * 5,
        out_specs=(vmem,) * 5,
        scratch_shapes=scratch,
        compiler_params=pltpu.CompilerParams(
            collective_id=0, has_side_effects=True, vmem_limit_bytes=50 * 1024 * 1024),
        cost_estimate=pl.CostEstimate(flops=12 * N * C * F, bytes_accessed=8 * rows * cl * 2, transcendentals=N * F),
    )(*[pltpu.with_memory_space_constraint(a, HBM)
        for a in (features.T, cotangent.T, kernel_tap_rows, in_weight, out_weight)])
    bo, gx, gw_in, gw_out, gk = pl.pallas_call(
        flush_kernel,
        out_shape=shapes,
        in_specs=[pl.BlockSpec(memory_space=pl.ANY)] * 5,
        out_specs=(hbm,) * 5,
        scratch_shapes=[pltpu.SemaphoreType.DMA((5,))],
        compiler_params=pltpu.CompilerParams(vmem_limit_bytes=1024 * 1024),
    )(*results)
    return bo.T, gx.T, gw_in, gw_out.T, gk


def solution(mesh):
    placed = (P("loop", "chan"), P(None, "chan"), P(), P(), P("loop", "chan"))
    return jax.shard_map(
        fused_shards,
        mesh=mesh,
        in_specs=placed,
        out_specs=(
            P("loop", "chan"),
            P("loop", "chan"),
            P("chan", "loop"),
            P("loop", "chan"),
            P(None, "chan"),
        ),
        check_vma=False,
    )
```

```python
import functools
import math

import jax
import jax.numpy as jnp
from jax import lax
from jax.experimental import pallas as pl
from jax.experimental.pallas import tpu as pltpu
from jax.sharding import PartitionSpec as P

TAPS = 9
DILATION_STEP = 512


gelu_scale = math.sqrt(2.0 / math.pi)
cubic_coef = 0.044715
epsilon = 1e-05


def with_halo(cells, sides, width):
    for axis, dim in sides:
        count = lax.axis_size(axis)
        head = lax.slice_in_dim(cells, 0, width, axis=dim)
        tail = lax.slice_in_dim(cells, cells.shape[dim] - width, cells.shape[dim], axis=dim)
        cells = jnp.concatenate(
            [
                lax.ppermute(tail, axis, [(i, (i + 1) % count) for i in range(count)]),
                cells,
                lax.ppermute(head, axis, [((i + 1) % count, i) for i in range(count)]),
            ],
            axis=dim,
        )
    return cells


def gelu_pair(inputs):
    inner_arg = gelu_scale * (inputs + cubic_coef * inputs * inputs * inputs)
    tangent = jnp.tanh(inner_arg)
    act_value = 0.5 * inputs * (1.0 + tangent)
    act_slope = 0.5 * (1.0 + tangent) + 0.5 * inputs * (1.0 - tangent * tangent) * gelu_scale * (
        1.0 + 3.0 * cubic_coef * inputs * inputs
    )
    return (act_value, act_slope)


def widen_rows(field_rows, reach_positions):
    return with_halo(field_rows, (("loop", 0),), reach_positions)


def shards(features, kernel_tap_rows, in_weight, out_weight, cotangent):
    middle_position = (TAPS - 1) // 2
    reach_positions = middle_position * DILATION_STEP
    loop_size = lax.axis_size("loop")
    chan_size = lax.axis_size("chan")
    rows_here = features.shape[0]
    grad_scale = 1.0 / math.sqrt(rows_here * loop_size)
    padded_in = widen_rows(features, reach_positions)
    blended_sum = jnp.zeros(features.shape, jnp.float32)
    for kernel_tap_index in range(TAPS):
        leading_row = reach_positions + (kernel_tap_index - middle_position) * DILATION_STEP
        blended_sum = blended_sum + kernel_tap_rows[kernel_tap_index] * padded_in[
            leading_row : leading_row + rows_here
        ].astype(jnp.float32)
    filtered = blended_sum.astype(jnp.bfloat16)
    row_block, upstream = (
        lax.all_to_all(filtered, "chan", split_axis=0, concat_axis=1, tiled=True),
        lax.all_to_all(cotangent, "chan", split_axis=0, concat_axis=1, tiled=True),
    )
    values = row_block.astype(jnp.float32)
    mean_value = jnp.mean(values, axis=-1, keepdims=True)
    centred = values - mean_value
    variance = jnp.mean(centred * centred, axis=-1, keepdims=True)
    inv_std = lax.rsqrt(variance + epsilon)
    normed = centred * inv_std
    normed_b = normed.astype(jnp.bfloat16)
    hidden_pre = jnp.dot(normed_b, in_weight, preferred_element_type=jnp.float32)
    act_value, act_slope = gelu_pair(hidden_pre)
    act_b = act_value.astype(jnp.bfloat16)
    branch = jnp.dot(act_b, out_weight, preferred_element_type=jnp.float32).astype(jnp.bfloat16)
    grad_act = jnp.einsum("pc,fc->pf", upstream, out_weight, preferred_element_type=jnp.float32)
    grad_pre = (grad_act * act_slope).astype(jnp.bfloat16)
    grad_normed = jnp.einsum("pf,cf->pc", grad_pre, in_weight, preferred_element_type=jnp.float32)
    grad_filtered = inv_std * (
        grad_normed
        - jnp.mean(grad_normed, axis=-1, keepdims=True)
        - normed * jnp.mean(grad_normed * normed, axis=-1, keepdims=True)
    )
    back_rows = grad_filtered.astype(jnp.bfloat16)
    local_rows = row_block.shape[0]
    width_c = row_block.shape[1]
    width_f = hidden_pre.shape[1]
    chan_part = width_c // chan_size
    loop_part = width_f // loop_size
    normed_parts = normed_b.reshape(local_rows, chan_size, chan_part)
    upstream_parts = upstream.reshape(local_rows, chan_size, chan_part)
    grad_parts = grad_pre.reshape(local_rows, loop_size, loop_part)
    act_parts = act_b.reshape(local_rows, loop_size, loop_part)
    term_in = (
        jnp.einsum("pai,pbj->baij", normed_parts, grad_parts, preferred_element_type=jnp.float32)
        * grad_scale
    )
    term_out = (
        jnp.einsum("pbj,pai->baji", act_parts, upstream_parts, preferred_element_type=jnp.float32)
        * grad_scale
    )
    branch_cols, back_cols = (
        lax.all_to_all(branch, "chan", split_axis=1, concat_axis=0, tiled=True),
        lax.all_to_all(back_rows, "chan", split_axis=1, concat_axis=0, tiled=True),
    )
    block_out = (features.astype(jnp.float32) + branch_cols.astype(jnp.float32)).astype(
        jnp.bfloat16
    )
    first_in, first_out = (
        lax.psum_scatter(
            term_in.astype(jnp.bfloat16), "chan", scatter_dimension=1, tiled=True
        ).astype(jnp.float32),
        lax.psum_scatter(
            term_out.astype(jnp.bfloat16), "chan", scatter_dimension=1, tiled=True
        ).astype(jnp.float32),
    )
    summed_in, summed_out = (
        lax.psum_scatter(first_in, "loop", scatter_dimension=0, tiled=True),
        lax.psum_scatter(first_out, "loop", scatter_dimension=0, tiled=True),
    )
    grad_in_weight = summed_in.reshape(chan_part, loop_part)
    grad_out_weight = summed_out.reshape(loop_part, chan_part)
    padded_back = widen_rows(back_cols, reach_positions)
    grad_sum_rows = cotangent.astype(jnp.float32)
    back_wide = back_cols.astype(jnp.float32)
    kernel_rows = []
    for kernel_tap_index in range(TAPS):
        shift_positions = (kernel_tap_index - middle_position) * DILATION_STEP
        first_back = reach_positions - shift_positions
        grad_sum_rows = grad_sum_rows + kernel_tap_rows[kernel_tap_index] * padded_back[
            first_back : first_back + rows_here
        ].astype(jnp.float32)
        first_in_row = reach_positions + shift_positions
        kernel_rows.append(
            jnp.sum(
                back_wide * padded_in[first_in_row : first_in_row + rows_here].astype(jnp.float32),
                axis=0,
            )
        )
    kernel_terms = jnp.stack(kernel_rows) * grad_scale
    grad_kernel = lax.psum(kernel_terms, "loop")
    return (
        block_out,
        grad_sum_rows.astype(jnp.bfloat16),
        grad_in_weight,
        grad_out_weight,
        grad_kernel,
    )


MESH = pl.DeviceIdType.MESH
MIDDLE = (TAPS - 1) // 2
HBM = pltpu.MemorySpace.HBM


def fused_kernel(
    L, J, grad_scale,
    x_hbm, ct_hbm, taps_hbm, win_hbm, wout_hbm,
    bo_out, gx_out, gw_in_out, gw_out_out, gk_out,
    xp, ctv, tapv, win, wout, wint, woutt, tf, fb, fr, ctf, nb, nrm, istd, act, gp,
    geb, brb, gep, brv, gfull, gsend, grecv, s1s, s1r, s2s, s2r, uf, sb, tr, gka, kt, kr, acc_x,
    load, send, recv,
):
    cl, rows = ctv.shape
    C, F = win.shape
    B = DILATION_STEP
    K = rows // B
    S = K // 2
    W = 2 * B // J
    V = (J - 1) * cl
    Z = L // 2
    own = MIDDLE * B
    bf, f32 = jnp.bfloat16, jnp.float32
    me_l, me_j = lax.axis_index("loop"), lax.axis_index("chan")
    core, z = lax.rem(me_l, 2), me_l // 2
    ct_r, f_r, ge_r, xh_r, core_r, s1_r, s2_r = [S * i for i in range(7)]
    br_r = 7 * S
    gh_r, z_r, kt_r = br_r + 2, br_r + 4, br_r + 5
    ct_s, f_s, ge_s, br_s, xh_s, gh_s, core_s, s1_s, s2_s, z_s, kt_s = range(11)

    def rcopy(src, dst, out, into, l, j):
        return pltpu.make_async_remote_copy(
            src_ref=src, dst_ref=dst, send_sem=send.at[out], recv_sem=recv.at[into],
            device_id=(l, j), device_id_type=MESH)

    def await_all(like, sem):
        pltpu.make_async_copy(like, like, sem).wait()

    def got(like, into):
        await_all(like, recv.at[into])

    def lanes(at, n):
        return pl.ds(pl.multiple_of(at, 128), n)

    jx = me_j + 1 - 2 * lax.rem(me_j, 2)
    jy = lax.rem(me_j + 2, J)
    jd = lax.rem(jx + 2, J)
    chan_peers = [jd, jx, jy]
    loop_peers = [lax.rem(me_l + e, L) for e in range(1, L)]
    right, left = loop_peers[0], loop_peers[-1]

    barrier = pltpu.get_barrier_semaphore()
    for j in chan_peers:
        pl.semaphore_signal(barrier, inc=1, device_id=(me_l, j), device_id_type=MESH)
    for l in loop_peers:
        pl.semaphore_signal(barrier, inc=1, device_id=(l, me_j), device_id_type=MESH)

    loads = [pltpu.make_async_copy(a, b, load.at[i]) for i, (a, b) in enumerate((
        (x_hbm, xp.at[:, own:own + rows]), (ct_hbm, ctv), (taps_hbm, tapv), (win_hbm, win), (wout_hbm, wout)))]
    for c in loads[:3]:
        c.start()

    half = J // 2
    mine = pl.ds(pl.multiple_of(me_j * cl, cl), cl)

    def col(s, j):
        return lanes((S - 1 - s + (j // half) * (1 + 2 * s)) * B + lax.rem(j, half) * W, W)

    def own_col(s, j):
        return lanes(own + (S - 1 - s + (j // half) * (1 + 2 * s)) * B + lax.rem(j, half) * W, W)

    def block(k):
        return lanes(k * B, B)

    def chan_rows(j):
        return pl.ds(pl.multiple_of(j * cl, cl), cl)

    def ct_copies(s):
        return [rcopy(ct_hbm.at[:, col(s, j)], ctf.at[s, mine, :], ct_s, ct_r + s, me_l, j) for j in chan_peers]

    def f_copies(s):
        return [rcopy(fb.at[:, col(s, j)], fr.at[s, mine, :], f_s, f_r + s, me_l, j) for j in chan_peers]

    def ge_copies(s):
        return [rcopy(geb.at[s, chan_rows(j), :], gep.at[:, own_col(s, me_j)], ge_s, ge_r + s, me_l, j)
                for j in chan_peers]

    def br_copies(s):
        return [rcopy(brb.at[s, chan_rows(j), :], brv.at[:, col(s, me_j)], br_s, br_r + s // (S - 1), me_l, j)
                for j in chan_peers]

    def xh_copies(s):
        return [rcopy(x_hbm.at[:, block(K - 1 - s)], xp.at[:, block(S - 1 - s)], xh_s, xh_r + s, right, me_j),
                rcopy(x_hbm.at[:, block(s)], xp.at[:, block(K + S + s)], xh_s, xh_r + s, left, me_j)]

    def gh_copies(s):
        near, far, into = S - 1 - s, S + s, gh_r + s // (S - 1)
        return [rcopy(gep.at[:, block(far + S)], gep.at[:, block(far - S)], gh_s, into, right, me_j),
                rcopy(gep.at[:, block(near + S)], gep.at[:, block(near + K + S)], gh_s, into, left, me_j)]

    def start(copies):
        for c in copies:
            c.start()

    pl.semaphore_wait(barrier, J - 1 + L - 1)
    start(xh_copies(0))
    start(ct_copies(0))
    for s in range(1, S):
        start(xh_copies(s))
        start(ct_copies(s))
    for c in loads[3:]:
        c.start()
    for c in loads:
        c.wait()
    padded = jnp.concatenate([tapv[...], jnp.zeros((128 - TAPS, cl), f32)], axis=0)
    columns = jnp.concatenate([padded, jnp.zeros((128, 128 - cl), f32)], axis=1).T
    for t in range(TAPS):
        tf[t] = jnp.broadcast_to(columns[0:cl, t:t + 1], (cl, 128))
    wint[...] = win[...].T
    woutt[...] = wout[...].T
    gka[...] = jnp.zeros(gka.shape, f32)
    for s in range(S):
        ctf[s, mine, :] = ctv[:, col(s, me_j)]

    def conv(s):
        near, far = S - 1 - s, S + s

        def part(q, carry):
            done = []
            for g in range(cl // 16):
                ch = slice(g * 16, (g + 1) * 16)
                w = [tf[t, ch, :] for t in range(TAPS)]
                sums = [jnp.zeros((16, 128), f32) for _ in range(2)]
                for b in range(near, far + TAPS):
                    v = xp[ch, lanes(b * B + q * 128, 128)].astype(f32)
                    for i, k in enumerate((near, far)):
                        if 0 <= b - k < TAPS:
                            sums[i] = sums[i] + w[b - k] * v
                done.append([a.astype(bf) for a in sums])
            for g in range(cl // 16):
                for i, k in enumerate((near, far)):
                    fb[g * 16:(g + 1) * 16, lanes(k * B + q * 128, 128)] = done[g][i]
            return carry

        lax.fori_loop(0, B // 128, part, 0)

    for s in range(S):
        got(xp.at[:, 0:2 * B], xh_r + s)
        conv(s)
        start(f_copies(s))
        fr[s, mine, :] = fb[:, col(s, me_j)]

    def mlp_body(s, carry):
        got(ctf.at[s, 0:V, :], ct_r + s)
        got(fr.at[s, 0:V, :], f_r + s)
        here = lanes(s * W, W)
        for b in range(W // 128):
            part = slice(b * 128, (b + 1) * 128)
            v = fr[s, :, part].astype(f32)
            centred = v - jnp.mean(v, axis=0, keepdims=True)
            inv = lax.rsqrt(jnp.mean(centred * centred, axis=0, keepdims=True) + epsilon)
            normed = centred * inv
            nrm[:, part] = normed
            istd[:, part] = inv
            nb[:, lanes(s * W + b * 128, 128)] = normed.astype(bf)
        normed_b = nb[:, here]
        up = ctf[s]
        FC = 256
        for f in range(F // FC):
            part = slice(f * FC, (f + 1) * FC)
            pre = jnp.dot(wint[part, :], normed_b, preferred_element_type=f32)
            ga = jnp.dot(wout[part, :], up, preferred_element_type=f32)
            sq = pre * pre
            tangent = jnp.tanh(pre * (gelu_scale + (gelu_scale * cubic_coef) * sq))
            gate = 0.5 + 0.5 * tangent
            slope = gate + pre * (gate * (1.0 - tangent)) * (gelu_scale + (3.0 * gelu_scale * cubic_coef) * sq)
            act[part, here] = (pre * gate).astype(bf)
            gp[part, here] = (ga * slope).astype(bf)
        gn = jnp.dot(win[...], gp[:, here], preferred_element_type=f32)
        for b in range(W // 128):
            part = slice(b * 128, (b + 1) * 128)
            g, normed = gn[:, part], nrm[:, part]
            out = istd[:, part] * (g - jnp.mean(g, axis=0, keepdims=True)
                                   - normed * jnp.mean(g * normed, axis=0, keepdims=True))
            geb[s, :, part] = out.astype(bf)
        start(ge_copies(s))
        gep[:, own_col(s, me_j)] = geb[s, mine, :]
        brb[s] = jnp.dot(woutt[...], act[:, here], preferred_element_type=f32).astype(bf)
        brv[:, col(s, me_j)] = brb[s, mine, :]

        return carry

    lax.fori_loop(0, S, mlp_body, 0)

    def forward(s):
        got(gep.at[:, 0:(J - 1) * W], ge_r + s)
        start(gh_copies(s))

    def kernel_terms(s):
        near, far = S - 1 - s, S + s
        for g in range(cl // 16):
            ch = slice(g * 16, (g + 1) * 16)
            sums = [gka[t, ch, :] for t in range(TAPS)]
            for q in range(B // 128):
                e = [gep[ch, lanes(own + k * B + q * 128, 128)].astype(f32) for k in (near, far)]
                for b in range(near, far + TAPS):
                    v = xp[ch, lanes(b * B + q * 128, 128)].astype(f32)
                    for i, k in enumerate((near, far)):
                        if 0 <= b - k < TAPS:
                            sums[b - k] = sums[b - k] + e[i] * v
            for t in range(TAPS):
                gka[t, ch, :] = sums[t]

    CR = C // J

    def core_copy(zz):
        return rcopy(gsend.at[1 - core, zz], grecv.at[zz], core_s, core_r + zz, z * 2 + 1 - core, me_j)

    def term_body(e, carry):
        zz = lax.rem(z + 1 + e, Z)
        cols = lanes(zz * 256, 256)
        both = jnp.concatenate([ctf[s] for s in range(S)], axis=1)
        for i, (a, b) in enumerate(((nb[...], gp), (both, act))):
            term = lax.dot_general(a, b[cols, :], (((1,), (1,)), ((), ())), preferred_element_type=f32) * grad_scale
            for h in range(2):
                part = term[:, h * 128:(h + 1) * 128]
                gfull[h, zz, i] = part
                gsend[h, zz, i] = part.astype(bf)
        core_copy(zz).start()

        @pl.when(e == 2)
        def _():
            forward(1)

        @pl.when(e >= 2)
        def _():
            core_sum(e - 2)
        return carry

    def piece(j):
        return pl.ds(pl.multiple_of(j * CR, CR), CR)

    def s1_copies(zz):
        return [rcopy(s1s.at[zz, i], s1r.at[zz, i], s1_s, s1_r + zz, me_l, j) for i, j in enumerate((jx, jy))]

    def s2_copies(zz):
        return [rcopy(s2s.at[zz, i], s2r.at[zz, i], s2_s, s2_r + zz, me_l, j) for i, j in enumerate((jy, jx))]

    def z_copy(e):
        zz = lax.rem(z + 1 + e, Z)
        return rcopy(sb.at[zz], tr.at[z - (z > zz).astype(jnp.int32)], z_s, z_r, zz * 2 + core, me_j)

    def core_sum(e):
        zz = lax.rem(z + 1 + e, Z)
        got(grecv.at[zz], core_r + zz)
        for i, j in enumerate((jx, jy)):
            gfull[core, zz, i] = gfull[core, zz, i] + grecv[zz, i].astype(f32)
            s1s[zz, i, 0] = gfull[core, zz, i, piece(j), :].astype(bf)
            s1s[zz, i, 1] = gfull[core, zz, i, piece(jd), :].astype(bf)
        start(s1_copies(zz))

    def halving(e):
        zz = lax.rem(z + 1 + e, Z)
        got(s1r.at[zz], s1_r + zz)
        for i, j in enumerate((jy, jx)):
            s2s[zz, i] = (gfull[core, zz, i, piece(j), :] + s1r[zz, i, 1].astype(f32)).astype(bf)
            uf[zz, i] = gfull[core, zz, i, piece(me_j), :] + s1r[zz, i, 0].astype(f32)
        start(s2_copies(zz))

    def z_stage(e):
        zz = lax.rem(z + 1 + e, Z)
        got(s2r.at[zz], s2_r + zz)
        total = uf[zz] + s2r[zz].astype(f32)
        uf[zz] = total
        sb[zz] = total.astype(bf)

        if e < Z - 1:
            z_copy(e).start()

    def back(final):
        late = (S - 1, S, S + K - 1, S + K)

        def part(q, carry):
            for g in range(cl // 16):
                ch = slice(g * 16, (g + 1) * 16)
                w = [tf[t, ch, :] for t in range(TAPS)]
                at = [lanes(k * B + q * 128, 128) for k in range(K)]
                sums = [acc_x[ch, a] if final else ctv[ch, a].astype(f32) for a in at]
                for b in range(K + 2 * S):
                    if (b in late) == final:
                        v = gep[ch, lanes(b * B + q * 128, 128)].astype(f32)
                        for t in range(TAPS):
                            k = b - (TAPS - 1 - t)
                            if 0 <= k < K:
                                sums[k] = sums[k] + w[t] * v
                for k in range(K):
                    if final:
                        gx_out[ch, at[k]] = sums[k].astype(bf)
                    else:
                        acc_x[ch, at[k]] = sums[k]
            return carry

        lax.fori_loop(0, B // 128, part, 0)

    forward(0)
    lax.fori_loop(0, Z, term_body, 0)
    core_sum(Z - 2)
    kernel_terms(0)
    core_sum(Z - 1)
    start(br_copies(0))
    kernel_terms(1)
    forward(2)
    kernel_terms(2)
    forward(3)
    halving(0)
    kernel_terms(3)
    halving(1)
    sums = [jnp.sum(gka[t], axis=1, keepdims=True) * grad_scale for t in range(TAPS)]
    total = jnp.concatenate(sums + [jnp.zeros((cl, 128 - TAPS), f32)], axis=1)
    total = jnp.concatenate([total, jnp.zeros((128 - cl, 128), f32)], axis=0).T
    kt[me_l] = total[0:16]
    start([rcopy(kt.at[me_l], kr.at[me_l - (me_l > l).astype(jnp.int32)], kt_s, kt_r, l, me_j) for l in loop_peers])

    halving(2)
    start(br_copies(1))
    start(br_copies(2))
    halving(3)
    start(br_copies(3))
    got(gep.at[:, 0:(S - 1) * 2 * B], gh_r)
    back(False)
    z_stage(0)
    z_stage(1)
    z_stage(2)
    got(gep.at[:, 0:2 * B], gh_r + 1)
    back(True)
    z_stage(3)

    def finish(k, carry):
        bo_out[:, block(k)] = (xp[:, block(k + S)].astype(f32) + brv[:, block(k)].astype(f32)).astype(bf)
        return carry

    got(brv.at[:, 0:(S - 1) * (J - 1) * W], br_r)
    lax.fori_loop(1, K - 1, finish, 0)
    got(kr, kt_r)
    total = kt[me_l]
    for l in range(L - 1):
        total = total + kr[l]
    gk_out[...] = total[0:TAPS, 0:cl]
    got(tr, z_r)
    total = uf[z]
    for e in range(Z - 1):
        total = total + tr[e].astype(f32)
    gw_in_out[...] = total[0]
    gw_out_out[...] = total[1]
    for like, out in ((ctv.at[:, 0:S * (J - 1) * W], ct_s), (fb.at[:, 0:S * (J - 1) * W], f_s), (geb.at[:, 0:V, :], ge_s),
                      (brb.at[:, 0:V, :], br_s), (xp.at[:, 0:2 * S * B], xh_s), (gep.at[:, 0:2 * S * B], gh_s),
                      (gsend.at[0], core_s), (s1s, s1_s), (s2s, s2_s), (sb.at[0:Z - 1], z_s), (kt.at[0:L - 1], kt_s)):
        await_all(like, send.at[out])
    got(brv.at[:, 0:(J - 1) * W], br_r + 1)
    finish(0, 0)
    finish(K - 1, 0)


def flush_kernel(*refs):
    n = len(refs) // 2
    sems = refs[2 * n]
    copies = [pltpu.make_async_copy(refs[i], refs[n + i], sems.at[i]) for i in range(n)]
    for c in copies:
        c.start()
    for c in copies:
        c.wait()


def fits(L, J, rows, cl, F):
    return (cl * 2 == 128 and rows == 2 * MIDDLE * DILATION_STEP and L % 2 == 0 and L > 2 and J == 4
            and F == L * 128 and L == 2 * MIDDLE)


def fused_shards(features, kernel_tap_rows, in_weight, out_weight, cotangent):
    L, J = lax.axis_size("loop"), lax.axis_size("chan")
    rows, cl = features.shape
    C, F = in_weight.shape
    if not fits(L, J, rows, cl, F):
        return shards(features, kernel_tap_rows, in_weight, out_weight, cotangent)
    N = rows // J
    K = rows // DILATION_STEP
    S = K // 2
    W = N // S
    Z = L // 2
    CR = C // J
    bf, f32 = jnp.bfloat16, jnp.float32
    ext = rows + 2 * MIDDLE * DILATION_STEP
    scratch = [
        pltpu.VMEM((cl, ext), bf),
        pltpu.VMEM((cl, rows), bf),
        pltpu.VMEM((TAPS, cl), f32),
        pltpu.VMEM((C, F), bf),
        pltpu.VMEM((F, C), bf),
        pltpu.VMEM((F, C), bf),
        pltpu.VMEM((C, F), bf),
        pltpu.VMEM((TAPS, cl, 128), f32),
        pltpu.VMEM((cl, rows), bf),
        pltpu.VMEM((S, C, W), bf),
        pltpu.VMEM((S, C, W), bf),
        pltpu.VMEM((C, N), bf),
        pltpu.VMEM((C, W), f32),
        pltpu.VMEM((1, W), f32),
        pltpu.VMEM((F, N), bf),
        pltpu.VMEM((F, N), bf),
        pltpu.VMEM((S, C, W), bf),
        pltpu.VMEM((S, C, W), bf),
        pltpu.VMEM((cl, ext), bf),
        pltpu.VMEM((cl, rows), bf),
        pltpu.VMEM((2, Z, 2, C, 128), f32),
        pltpu.VMEM((2, Z, 2, C, 128), bf),
        pltpu.VMEM((Z, 2, C, 128), bf),
        pltpu.VMEM((Z, 2, 2, CR, 128), bf),
        pltpu.VMEM((Z, 2, 2, CR, 128), bf),
        pltpu.VMEM((Z, 2, CR, 128), bf),
        pltpu.VMEM((Z, 2, CR, 128), bf),
        pltpu.VMEM((Z, 2, CR, 128), f32),
        pltpu.VMEM((Z, 2, CR, 128), bf),
        pltpu.VMEM((Z - 1, 2, CR, 128), bf),
        pltpu.VMEM((TAPS, cl, 128), f32),
        pltpu.VMEM((L, 16, 128), f32),
        pltpu.VMEM((L - 1, 16, 128), f32),
        pltpu.VMEM((cl, rows), f32),
    ]
    scratch += [pltpu.SemaphoreType.DMA((5,)), pltpu.SemaphoreType.DMA((11,)), pltpu.SemaphoreType.DMA((7 * S + 6,))]
    vmem = pl.BlockSpec(memory_space=pltpu.VMEM)
    hbm = pl.BlockSpec(memory_space=HBM)
    shapes = (
        jax.ShapeDtypeStruct((cl, rows), bf),
        jax.ShapeDtypeStruct((cl, rows), bf),
        jax.ShapeDtypeStruct((CR, F // L), f32),
        jax.ShapeDtypeStruct((CR, F // L), f32),
        jax.ShapeDtypeStruct((TAPS, cl), f32),
    )
    results = pl.pallas_call(
        functools.partial(fused_kernel, L, J, 1.0 / math.sqrt(rows * L)),
        out_shape=shapes,
        in_specs=[hbm] * 5,
        out_specs=(vmem,) * 5,
        scratch_shapes=scratch,
        compiler_params=pltpu.CompilerParams(
            collective_id=0, has_side_effects=True, vmem_limit_bytes=50 * 1024 * 1024),
        cost_estimate=pl.CostEstimate(flops=12 * N * C * F, bytes_accessed=8 * rows * cl * 2, transcendentals=N * F),
    )(*[pltpu.with_memory_space_constraint(a, HBM)
        for a in (features.T, cotangent.T, kernel_tap_rows, in_weight, out_weight)])
    bo, gx, gw_in, gw_out, gk = pl.pallas_call(
        flush_kernel,
        out_shape=shapes,
        in_specs=[pl.BlockSpec(memory_space=pl.ANY)] * 5,
        out_specs=(hbm,) * 5,
        scratch_shapes=[pltpu.SemaphoreType.DMA((5,))],
        compiler_params=pltpu.CompilerParams(vmem_limit_bytes=1024 * 1024),
    )(*results)
    return bo.T, gx.T, gw_in, gw_out.T, gk


def solution(mesh):
    placed = (P("loop", "chan"), P(None, "chan"), P(), P(), P("loop", "chan"))
    return jax.shard_map(
        fused_shards,
        mesh=mesh,
        in_specs=placed,
        out_specs=(
            P("loop", "chan"),
            P("loop", "chan"),
            P("chan", "loop"),
            P("loop", "chan"),
            P(None, "chan"),
        ),
        check_vma=False,
    )
```

```python
import functools
import math

import jax
import jax.numpy as jnp
from jax import lax
from jax.experimental import pallas as pl
from jax.experimental.pallas import tpu as pltpu
from jax.sharding import PartitionSpec as P

TAPS = 9
DILATION_STEP = 512


gelu_scale = math.sqrt(2.0 / math.pi)
cubic_coef = 0.044715
epsilon = 1e-05


def with_halo(cells, sides, width):
    for axis, dim in sides:
        count = lax.axis_size(axis)
        head = lax.slice_in_dim(cells, 0, width, axis=dim)
        tail = lax.slice_in_dim(cells, cells.shape[dim] - width, cells.shape[dim], axis=dim)
        cells = jnp.concatenate(
            [
                lax.ppermute(tail, axis, [(i, (i + 1) % count) for i in range(count)]),
                cells,
                lax.ppermute(head, axis, [((i + 1) % count, i) for i in range(count)]),
            ],
            axis=dim,
        )
    return cells


def gelu_pair(inputs):
    inner_arg = gelu_scale * (inputs + cubic_coef * inputs * inputs * inputs)
    tangent = jnp.tanh(inner_arg)
    act_value = 0.5 * inputs * (1.0 + tangent)
    act_slope = 0.5 * (1.0 + tangent) + 0.5 * inputs * (1.0 - tangent * tangent) * gelu_scale * (
        1.0 + 3.0 * cubic_coef * inputs * inputs
    )
    return (act_value, act_slope)


def widen_rows(field_rows, reach_positions):
    return with_halo(field_rows, (("loop", 0),), reach_positions)


def shards(features, kernel_tap_rows, in_weight, out_weight, cotangent):
    middle_position = (TAPS - 1) // 2
    reach_positions = middle_position * DILATION_STEP
    loop_size = lax.axis_size("loop")
    chan_size = lax.axis_size("chan")
    rows_here = features.shape[0]
    grad_scale = 1.0 / math.sqrt(rows_here * loop_size)
    padded_in = widen_rows(features, reach_positions)
    blended_sum = jnp.zeros(features.shape, jnp.float32)
    for kernel_tap_index in range(TAPS):
        leading_row = reach_positions + (kernel_tap_index - middle_position) * DILATION_STEP
        blended_sum = blended_sum + kernel_tap_rows[kernel_tap_index] * padded_in[
            leading_row : leading_row + rows_here
        ].astype(jnp.float32)
    filtered = blended_sum.astype(jnp.bfloat16)
    row_block, upstream = (
        lax.all_to_all(filtered, "chan", split_axis=0, concat_axis=1, tiled=True),
        lax.all_to_all(cotangent, "chan", split_axis=0, concat_axis=1, tiled=True),
    )
    values = row_block.astype(jnp.float32)
    mean_value = jnp.mean(values, axis=-1, keepdims=True)
    centred = values - mean_value
    variance = jnp.mean(centred * centred, axis=-1, keepdims=True)
    inv_std = lax.rsqrt(variance + epsilon)
    normed = centred * inv_std
    normed_b = normed.astype(jnp.bfloat16)
    hidden_pre = jnp.dot(normed_b, in_weight, preferred_element_type=jnp.float32)
    act_value, act_slope = gelu_pair(hidden_pre)
    act_b = act_value.astype(jnp.bfloat16)
    branch = jnp.dot(act_b, out_weight, preferred_element_type=jnp.float32).astype(jnp.bfloat16)
    grad_act = jnp.einsum("pc,fc->pf", upstream, out_weight, preferred_element_type=jnp.float32)
    grad_pre = (grad_act * act_slope).astype(jnp.bfloat16)
    grad_normed = jnp.einsum("pf,cf->pc", grad_pre, in_weight, preferred_element_type=jnp.float32)
    grad_filtered = inv_std * (
        grad_normed
        - jnp.mean(grad_normed, axis=-1, keepdims=True)
        - normed * jnp.mean(grad_normed * normed, axis=-1, keepdims=True)
    )
    back_rows = grad_filtered.astype(jnp.bfloat16)
    local_rows = row_block.shape[0]
    width_c = row_block.shape[1]
    width_f = hidden_pre.shape[1]
    chan_part = width_c // chan_size
    loop_part = width_f // loop_size
    normed_parts = normed_b.reshape(local_rows, chan_size, chan_part)
    upstream_parts = upstream.reshape(local_rows, chan_size, chan_part)
    grad_parts = grad_pre.reshape(local_rows, loop_size, loop_part)
    act_parts = act_b.reshape(local_rows, loop_size, loop_part)
    term_in = (
        jnp.einsum("pai,pbj->baij", normed_parts, grad_parts, preferred_element_type=jnp.float32)
        * grad_scale
    )
    term_out = (
        jnp.einsum("pbj,pai->baji", act_parts, upstream_parts, preferred_element_type=jnp.float32)
        * grad_scale
    )
    branch_cols, back_cols = (
        lax.all_to_all(branch, "chan", split_axis=1, concat_axis=0, tiled=True),
        lax.all_to_all(back_rows, "chan", split_axis=1, concat_axis=0, tiled=True),
    )
    block_out = (features.astype(jnp.float32) + branch_cols.astype(jnp.float32)).astype(
        jnp.bfloat16
    )
    first_in, first_out = (
        lax.psum_scatter(
            term_in.astype(jnp.bfloat16), "chan", scatter_dimension=1, tiled=True
        ).astype(jnp.float32),
        lax.psum_scatter(
            term_out.astype(jnp.bfloat16), "chan", scatter_dimension=1, tiled=True
        ).astype(jnp.float32),
    )
    summed_in, summed_out = (
        lax.psum_scatter(first_in, "loop", scatter_dimension=0, tiled=True),
        lax.psum_scatter(first_out, "loop", scatter_dimension=0, tiled=True),
    )
    grad_in_weight = summed_in.reshape(chan_part, loop_part)
    grad_out_weight = summed_out.reshape(loop_part, chan_part)
    padded_back = widen_rows(back_cols, reach_positions)
    grad_sum_rows = cotangent.astype(jnp.float32)
    back_wide = back_cols.astype(jnp.float32)
    kernel_rows = []
    for kernel_tap_index in range(TAPS):
        shift_positions = (kernel_tap_index - middle_position) * DILATION_STEP
        first_back = reach_positions - shift_positions
        grad_sum_rows = grad_sum_rows + kernel_tap_rows[kernel_tap_index] * padded_back[
            first_back : first_back + rows_here
        ].astype(jnp.float32)
        first_in_row = reach_positions + shift_positions
        kernel_rows.append(
            jnp.sum(
                back_wide * padded_in[first_in_row : first_in_row + rows_here].astype(jnp.float32),
                axis=0,
            )
        )
    kernel_terms = jnp.stack(kernel_rows) * grad_scale
    grad_kernel = lax.psum(kernel_terms, "loop")
    return (
        block_out,
        grad_sum_rows.astype(jnp.bfloat16),
        grad_in_weight,
        grad_out_weight,
        grad_kernel,
    )


MESH = pl.DeviceIdType.MESH
MIDDLE = (TAPS - 1) // 2
HBM = pltpu.MemorySpace.HBM


def fused_kernel(
    L, J, grad_scale,
    x_hbm, ct_hbm, taps_hbm, win_hbm, wout_hbm,
    bo_out, gx_out, gw_in_out, gw_out_out, gk_out,
    xp, ctv, tapv, win, wout, wint, woutt, tf, fb, fr, ctf, nb, nrm, istd, act, gp,
    geb, brb, gep, brv, gfull, gsend, grecv, s1s, s1r, s2s, s2r, uf, sb, tr, gka, kt, kr, acc_x,
    load, send, recv,
):
    cl, rows = ctv.shape
    C, F = win.shape
    B = DILATION_STEP
    K = rows // B
    S = K // 2
    W = 2 * B // J
    V = (J - 1) * cl
    Z = L // 2
    own = MIDDLE * B
    bf, f32 = jnp.bfloat16, jnp.float32
    me_l, me_j = lax.axis_index("loop"), lax.axis_index("chan")
    core, z = lax.rem(me_l, 2), me_l // 2
    ct_r, f_r, ge_r, xh_r, core_r, s1_r, s2_r = [S * i for i in range(7)]
    br_r = 7 * S
    gh_r, z_r, kt_r = br_r + 2, br_r + 4, br_r + 5
    ct_s, f_s, ge_s, br_s, xh_s, gh_s, core_s, s1_s, s2_s, z_s, kt_s = range(11)

    def rcopy(src, dst, out, into, l, j):
        return pltpu.make_async_remote_copy(
            src_ref=src, dst_ref=dst, send_sem=send.at[out], recv_sem=recv.at[into],
            device_id=(l, j), device_id_type=MESH)

    def await_all(like, sem):
        pltpu.make_async_copy(like, like, sem).wait()

    def got(like, into):
        await_all(like, recv.at[into])

    def lanes(at, n):
        return pl.ds(pl.multiple_of(at, 128), n)

    jx = me_j + 1 - 2 * lax.rem(me_j, 2)
    jy = lax.rem(me_j + 2, J)
    jd = lax.rem(jx + 2, J)
    chan_peers = [jd, jx, jy]
    loop_peers = [lax.rem(me_l + e, L) for e in range(1, L)]
    right, left = loop_peers[0], loop_peers[-1]

    barrier = pltpu.get_barrier_semaphore()
    for j in chan_peers:
        pl.semaphore_signal(barrier, inc=1, device_id=(me_l, j), device_id_type=MESH)
    for l in loop_peers:
        pl.semaphore_signal(barrier, inc=1, device_id=(l, me_j), device_id_type=MESH)

    loads = [pltpu.make_async_copy(a, b, load.at[i]) for i, (a, b) in enumerate((
        (x_hbm, xp.at[:, own:own + rows]), (ct_hbm, ctv), (taps_hbm, tapv), (win_hbm, win), (wout_hbm, wout)))]
    for c in loads[:3]:
        c.start()

    half = J // 2
    mine = pl.ds(pl.multiple_of(me_j * cl, cl), cl)

    def col(s, j):
        return lanes((S - 1 - s + (j // half) * (1 + 2 * s)) * B + lax.rem(j, half) * W, W)

    def own_col(s, j):
        return lanes(own + (S - 1 - s + (j // half) * (1 + 2 * s)) * B + lax.rem(j, half) * W, W)

    def block(k):
        return lanes(k * B, B)

    def chan_rows(j):
        return pl.ds(pl.multiple_of(j * cl, cl), cl)

    def ct_copies(s):
        return [rcopy(ct_hbm.at[:, col(s, j)], ctf.at[s, mine, :], ct_s, ct_r + s, me_l, j) for j in chan_peers]

    def f_copies(s):
        return [rcopy(fb.at[:, col(s, j)], fr.at[s, mine, :], f_s, f_r + s, me_l, j) for j in chan_peers]

    def ge_copies(s):
        return [rcopy(geb.at[s, chan_rows(j), :], gep.at[:, own_col(s, me_j)], ge_s, ge_r + s, me_l, j)
                for j in chan_peers]

    def br_copies(s):
        return [rcopy(brb.at[s, chan_rows(j), :], brv.at[:, col(s, me_j)], br_s, br_r + s // (S - 1), me_l, j)
                for j in chan_peers]

    def xh_copies(s):
        return [rcopy(x_hbm.at[:, block(K - 1 - s)], xp.at[:, block(S - 1 - s)], xh_s, xh_r + s, right, me_j),
                rcopy(x_hbm.at[:, block(s)], xp.at[:, block(K + S + s)], xh_s, xh_r + s, left, me_j)]

    def gh_copies(s):
        near, far, into = S - 1 - s, S + s, gh_r + s // (S - 1)
        return [rcopy(gep.at[:, block(far + S)], gep.at[:, block(far - S)], gh_s, into, right, me_j),
                rcopy(gep.at[:, block(near + S)], gep.at[:, block(near + K + S)], gh_s, into, left, me_j)]

    def start(copies):
        for c in copies:
            c.start()

    pl.semaphore_wait(barrier, J - 1 + L - 1)
    start(xh_copies(0))
    start(ct_copies(0))
    for s in range(1, S):
        start(xh_copies(s))
        start(ct_copies(s))
    for c in loads[3:]:
        c.start()
    for c in loads:
        c.wait()
    padded = jnp.concatenate([tapv[...], jnp.zeros((128 - TAPS, cl), f32)], axis=0)
    columns = jnp.concatenate([padded, jnp.zeros((128, 128 - cl), f32)], axis=1).T
    for t in range(TAPS):
        tf[t] = jnp.broadcast_to(columns[0:cl, t:t + 1], (cl, 128))
    wint[...] = win[...].T
    woutt[...] = wout[...].T
    gka[...] = jnp.zeros(gka.shape, f32)
    for s in range(S):
        ctf[s, mine, :] = ctv[:, col(s, me_j)]

    def conv(s):
        near, far = S - 1 - s, S + s

        def part(q, carry):
            done = []
            for g in range(cl // 16):
                ch = slice(g * 16, (g + 1) * 16)
                w = [tf[t, ch, :] for t in range(TAPS)]
                sums = [jnp.zeros((16, 128), f32) for _ in range(2)]
                for b in range(near, far + TAPS):
                    v = xp[ch, lanes(b * B + q * 128, 128)].astype(f32)
                    for i, k in enumerate((near, far)):
                        if 0 <= b - k < TAPS:
                            sums[i] = sums[i] + w[b - k] * v
                done.append([a.astype(bf) for a in sums])
            for g in range(cl // 16):
                for i, k in enumerate((near, far)):
                    fb[g * 16:(g + 1) * 16, lanes(k * B + q * 128, 128)] = done[g][i]
            return carry

        lax.fori_loop(0, B // 128, part, 0)

    for s in range(S):
        got(xp.at[:, 0:2 * B], xh_r + s)
        conv(s)
        start(f_copies(s))
        fr[s, mine, :] = fb[:, col(s, me_j)]

    def mlp_body(s, carry):
        got(ctf.at[s, 0:V, :], ct_r + s)
        got(fr.at[s, 0:V, :], f_r + s)
        here = lanes(s * W, W)
        for b in range(W // 128):
            part = slice(b * 128, (b + 1) * 128)
            v = fr[s, :, part].astype(f32)
            centred = v - jnp.mean(v, axis=0, keepdims=True)
            inv = lax.rsqrt(jnp.mean(centred * centred, axis=0, keepdims=True) + epsilon)
            normed = centred * inv
            nrm[:, part] = normed
            istd[:, part] = inv
            nb[:, lanes(s * W + b * 128, 128)] = normed.astype(bf)
        normed_b = nb[:, here]
        up = ctf[s]
        FC = 256
        for f in range(F // FC):
            part = slice(f * FC, (f + 1) * FC)
            pre = jnp.dot(wint[part, :], normed_b, preferred_element_type=f32)
            ga = jnp.dot(wout[part, :], up, preferred_element_type=f32)
            pre, ga = pre.astype(bf), ga.astype(bf)
            sq = pre * pre
            tangent = jnp.tanh(pre * (gelu_scale + (gelu_scale * cubic_coef) * sq))
            gate = 0.5 + 0.5 * tangent
            slope = gate + pre * (gate * (1.0 - tangent)) * (gelu_scale + (3.0 * gelu_scale * cubic_coef) * sq)
            act[part, here] = pre * gate
            gp[part, here] = ga * slope
        gn = jnp.dot(win[...], gp[:, here], preferred_element_type=f32)
        for b in range(W // 128):
            part = slice(b * 128, (b + 1) * 128)
            g, normed = gn[:, part], nrm[:, part]
            out = istd[:, part] * (g - jnp.mean(g, axis=0, keepdims=True)
                                   - normed * jnp.mean(g * normed, axis=0, keepdims=True))
            geb[s, :, part] = out.astype(bf)
        start(ge_copies(s))
        gep[:, own_col(s, me_j)] = geb[s, mine, :]
        brb[s] = jnp.dot(woutt[...], act[:, here], preferred_element_type=f32).astype(bf)
        brv[:, col(s, me_j)] = brb[s, mine, :]

        return carry

    lax.fori_loop(0, S, mlp_body, 0)

    def forward(s):
        got(gep.at[:, 0:(J - 1) * W], ge_r + s)
        start(gh_copies(s))

    def kernel_terms(s):
        near, far = S - 1 - s, S + s
        for g in range(cl // 16):
            ch = slice(g * 16, (g + 1) * 16)
            sums = [gka[t, ch, :] for t in range(TAPS)]
            for q in range(B // 128):
                e = [gep[ch, lanes(own + k * B + q * 128, 128)].astype(f32) for k in (near, far)]
                for b in range(near, far + TAPS):
                    v = xp[ch, lanes(b * B + q * 128, 128)].astype(f32)
                    for i, k in enumerate((near, far)):
                        if 0 <= b - k < TAPS:
                            sums[b - k] = sums[b - k] + e[i] * v
            for t in range(TAPS):
                gka[t, ch, :] = sums[t]

    CR = C // J

    def core_copy(zz):
        return rcopy(gsend.at[1 - core, zz], grecv.at[zz], core_s, core_r + zz, z * 2 + 1 - core, me_j)

    def term_body(e, carry):
        zz = lax.rem(z + 1 + e, Z)
        cols = lanes(zz * 256, 256)
        both = jnp.concatenate([ctf[s] for s in range(S)], axis=1)
        for i, (a, b) in enumerate(((nb[...], gp), (both, act))):
            term = lax.dot_general(a, b[cols, :], (((1,), (1,)), ((), ())), preferred_element_type=f32) * grad_scale
            for h in range(2):
                part = term[:, h * 128:(h + 1) * 128]
                gfull[h, zz, i] = part
                gsend[h, zz, i] = part.astype(bf)
        core_copy(zz).start()

        @pl.when(e == 2)
        def _():
            forward(1)

        @pl.when(e >= 2)
        def _():
            core_sum(e - 2)
        return carry

    def piece(j):
        return pl.ds(pl.multiple_of(j * CR, CR), CR)

    def s1_copies(zz):
        return [rcopy(s1s.at[zz, i], s1r.at[zz, i], s1_s, s1_r + zz, me_l, j) for i, j in enumerate((jx, jy))]

    def s2_copies(zz):
        return [rcopy(s2s.at[zz, i], s2r.at[zz, i], s2_s, s2_r + zz, me_l, j) for i, j in enumerate((jy, jx))]

    def z_copy(e):
        zz = lax.rem(z + 1 + e, Z)
        return rcopy(sb.at[zz], tr.at[z - (z > zz).astype(jnp.int32)], z_s, z_r, zz * 2 + core, me_j)

    def core_sum(e):
        zz = lax.rem(z + 1 + e, Z)
        got(grecv.at[zz], core_r + zz)
        for i, j in enumerate((jx, jy)):
            gfull[core, zz, i] = gfull[core, zz, i] + grecv[zz, i].astype(f32)
            s1s[zz, i, 0] = gfull[core, zz, i, piece(j), :].astype(bf)
            s1s[zz, i, 1] = gfull[core, zz, i, piece(jd), :].astype(bf)
        start(s1_copies(zz))

    def halving(e):
        zz = lax.rem(z + 1 + e, Z)
        got(s1r.at[zz], s1_r + zz)
        for i, j in enumerate((jy, jx)):
            s2s[zz, i] = (gfull[core, zz, i, piece(j), :] + s1r[zz, i, 1].astype(f32)).astype(bf)
            uf[zz, i] = gfull[core, zz, i, piece(me_j), :] + s1r[zz, i, 0].astype(f32)
        start(s2_copies(zz))

    def z_stage(e):
        zz = lax.rem(z + 1 + e, Z)
        got(s2r.at[zz], s2_r + zz)
        total = uf[zz] + s2r[zz].astype(f32)
        uf[zz] = total
        sb[zz] = total.astype(bf)

        if e < Z - 1:
            z_copy(e).start()

    def back(final):
        late = (S - 1, S, S + K - 1, S + K)

        def part(q, carry):
            for g in range(cl // 16):
                ch = slice(g * 16, (g + 1) * 16)
                w = [tf[t, ch, :] for t in range(TAPS)]
                at = [lanes(k * B + q * 128, 128) for k in range(K)]
                sums = [acc_x[ch, a] if final else ctv[ch, a].astype(f32) for a in at]
                for b in range(K + 2 * S):
                    if (b in late) == final:
                        v = gep[ch, lanes(b * B + q * 128, 128)].astype(f32)
                        for t in range(TAPS):
                            k = b - (TAPS - 1 - t)
                            if 0 <= k < K:
                                sums[k] = sums[k] + w[t] * v
                for k in range(K):
                    if final:
                        gx_out[ch, at[k]] = sums[k].astype(bf)
                    else:
                        acc_x[ch, at[k]] = sums[k]
            return carry

        lax.fori_loop(0, B // 128, part, 0)

    forward(0)
    lax.fori_loop(0, Z, term_body, 0)
    core_sum(Z - 2)
    kernel_terms(0)
    core_sum(Z - 1)
    start(br_copies(0))
    kernel_terms(1)
    forward(2)
    kernel_terms(2)
    forward(3)
    halving(0)
    kernel_terms(3)
    halving(1)
    sums = [jnp.sum(gka[t], axis=1, keepdims=True) * grad_scale for t in range(TAPS)]
    total = jnp.concatenate(sums + [jnp.zeros((cl, 128 - TAPS), f32)], axis=1)
    total = jnp.concatenate([total, jnp.zeros((128 - cl, 128), f32)], axis=0).T
    kt[me_l] = total[0:16]
    start([rcopy(kt.at[me_l], kr.at[me_l - (me_l > l).astype(jnp.int32)], kt_s, kt_r, l, me_j) for l in loop_peers])

    start(br_copies(1))
    halving(2)
    start(br_copies(2))
    halving(3)
    start(br_copies(3))
    got(gep.at[:, 0:(S - 1) * 2 * B], gh_r)
    back(False)
    z_stage(0)
    z_stage(1)
    z_stage(2)
    got(gep.at[:, 0:2 * B], gh_r + 1)
    back(True)
    z_stage(3)

    def finish(k, carry):
        bo_out[:, block(k)] = (xp[:, block(k + S)].astype(f32) + brv[:, block(k)].astype(f32)).astype(bf)
        return carry

    got(brv.at[:, 0:(S - 1) * (J - 1) * W], br_r)
    lax.fori_loop(1, K - 1, finish, 0)
    got(kr, kt_r)
    total = kt[me_l]
    for l in range(L - 1):
        total = total + kr[l]
    gk_out[...] = total[0:TAPS, 0:cl]
    got(tr, z_r)
    total = uf[z]
    for e in range(Z - 1):
        total = total + tr[e].astype(f32)
    gw_in_out[...] = total[0]
    gw_out_out[...] = total[1]
    for like, out in ((ctv.at[:, 0:S * (J - 1) * W], ct_s), (fb.at[:, 0:S * (J - 1) * W], f_s), (geb.at[:, 0:V, :], ge_s),
                      (brb.at[:, 0:V, :], br_s), (xp.at[:, 0:2 * S * B], xh_s), (gep.at[:, 0:2 * S * B], gh_s),
                      (gsend.at[0], core_s), (s1s, s1_s), (s2s, s2_s), (sb.at[0:Z - 1], z_s), (kt.at[0:L - 1], kt_s)):
        await_all(like, send.at[out])
    got(brv.at[:, 0:(J - 1) * W], br_r + 1)
    finish(0, 0)
    finish(K - 1, 0)


def flush_kernel(*refs):
    n = len(refs) // 2
    sems = refs[2 * n]
    copies = [pltpu.make_async_copy(refs[i], refs[n + i], sems.at[i]) for i in range(n)]
    for c in copies:
        c.start()
    for c in copies:
        c.wait()


def fits(L, J, rows, cl, F):
    return (cl * 2 == 128 and rows == 2 * MIDDLE * DILATION_STEP and L % 2 == 0 and L > 2 and J == 4
            and F == L * 128 and L == 2 * MIDDLE)


def fused_shards(features, kernel_tap_rows, in_weight, out_weight, cotangent):
    L, J = lax.axis_size("loop"), lax.axis_size("chan")
    rows, cl = features.shape
    C, F = in_weight.shape
    if not fits(L, J, rows, cl, F):
        return shards(features, kernel_tap_rows, in_weight, out_weight, cotangent)
    N = rows // J
    K = rows // DILATION_STEP
    S = K // 2
    W = N // S
    Z = L // 2
    CR = C // J
    bf, f32 = jnp.bfloat16, jnp.float32
    ext = rows + 2 * MIDDLE * DILATION_STEP
    scratch = [
        pltpu.VMEM((cl, ext), bf),
        pltpu.VMEM((cl, rows), bf),
        pltpu.VMEM((TAPS, cl), f32),
        pltpu.VMEM((C, F), bf),
        pltpu.VMEM((F, C), bf),
        pltpu.VMEM((F, C), bf),
        pltpu.VMEM((C, F), bf),
        pltpu.VMEM((TAPS, cl, 128), f32),
        pltpu.VMEM((cl, rows), bf),
        pltpu.VMEM((S, C, W), bf),
        pltpu.VMEM((S, C, W), bf),
        pltpu.VMEM((C, N), bf),
        pltpu.VMEM((C, W), f32),
        pltpu.VMEM((1, W), f32),
        pltpu.VMEM((F, N), bf),
        pltpu.VMEM((F, N), bf),
        pltpu.VMEM((S, C, W), bf),
        pltpu.VMEM((S, C, W), bf),
        pltpu.VMEM((cl, ext), bf),
        pltpu.VMEM((cl, rows), bf),
        pltpu.VMEM((2, Z, 2, C, 128), f32),
        pltpu.VMEM((2, Z, 2, C, 128), bf),
        pltpu.VMEM((Z, 2, C, 128), bf),
        pltpu.VMEM((Z, 2, 2, CR, 128), bf),
        pltpu.VMEM((Z, 2, 2, CR, 128), bf),
        pltpu.VMEM((Z, 2, CR, 128), bf),
        pltpu.VMEM((Z, 2, CR, 128), bf),
        pltpu.VMEM((Z, 2, CR, 128), f32),
        pltpu.VMEM((Z, 2, CR, 128), bf),
        pltpu.VMEM((Z - 1, 2, CR, 128), bf),
        pltpu.VMEM((TAPS, cl, 128), f32),
        pltpu.VMEM((L, 16, 128), f32),
        pltpu.VMEM((L - 1, 16, 128), f32),
        pltpu.VMEM((cl, rows), f32),
    ]
    scratch += [pltpu.SemaphoreType.DMA((5,)), pltpu.SemaphoreType.DMA((11,)), pltpu.SemaphoreType.DMA((7 * S + 6,))]
    vmem = pl.BlockSpec(memory_space=pltpu.VMEM)
    hbm = pl.BlockSpec(memory_space=HBM)
    shapes = (
        jax.ShapeDtypeStruct((cl, rows), bf),
        jax.ShapeDtypeStruct((cl, rows), bf),
        jax.ShapeDtypeStruct((CR, F // L), f32),
        jax.ShapeDtypeStruct((CR, F // L), f32),
        jax.ShapeDtypeStruct((TAPS, cl), f32),
    )
    results = pl.pallas_call(
        functools.partial(fused_kernel, L, J, 1.0 / math.sqrt(rows * L)),
        out_shape=shapes,
        in_specs=[hbm] * 5,
        out_specs=(vmem,) * 5,
        scratch_shapes=scratch,
        compiler_params=pltpu.CompilerParams(
            collective_id=0, has_side_effects=True, vmem_limit_bytes=50 * 1024 * 1024),
        cost_estimate=pl.CostEstimate(flops=12 * N * C * F, bytes_accessed=8 * rows * cl * 2, transcendentals=N * F),
    )(*[pltpu.with_memory_space_constraint(a, HBM)
        for a in (features.T, cotangent.T, kernel_tap_rows, in_weight, out_weight)])
    bo, gx, gw_in, gw_out, gk = pl.pallas_call(
        flush_kernel,
        out_shape=shapes,
        in_specs=[pl.BlockSpec(memory_space=pl.ANY)] * 5,
        out_specs=(hbm,) * 5,
        scratch_shapes=[pltpu.SemaphoreType.DMA((5,))],
        compiler_params=pltpu.CompilerParams(vmem_limit_bytes=1024 * 1024),
    )(*results)
    return bo.T, gx.T, gw_in, gw_out.T, gk


def solution(mesh):
    placed = (P("loop", "chan"), P(None, "chan"), P(), P(), P("loop", "chan"))
    return jax.shard_map(
        fused_shards,
        mesh=mesh,
        in_specs=placed,
        out_specs=(
            P("loop", "chan"),
            P("loop", "chan"),
            P("chan", "loop"),
            P("loop", "chan"),
            P(None, "chan"),
        ),
        check_vma=False,
    )
```

```python
import functools
import math

import jax
import jax.numpy as jnp
from jax import lax
from jax.experimental import pallas as pl
from jax.experimental.pallas import tpu as pltpu
from jax.sharding import PartitionSpec as P

TAPS = 9
DILATION_STEP = 512


gelu_scale = math.sqrt(2.0 / math.pi)
cubic_coef = 0.044715
epsilon = 1e-05


def with_halo(cells, sides, width):
    for axis, dim in sides:
        count = lax.axis_size(axis)
        head = lax.slice_in_dim(cells, 0, width, axis=dim)
        tail = lax.slice_in_dim(cells, cells.shape[dim] - width, cells.shape[dim], axis=dim)
        cells = jnp.concatenate(
            [
                lax.ppermute(tail, axis, [(i, (i + 1) % count) for i in range(count)]),
                cells,
                lax.ppermute(head, axis, [((i + 1) % count, i) for i in range(count)]),
            ],
            axis=dim,
        )
    return cells


def gelu_pair(inputs):
    inner_arg = gelu_scale * (inputs + cubic_coef * inputs * inputs * inputs)
    tangent = jnp.tanh(inner_arg)
    act_value = 0.5 * inputs * (1.0 + tangent)
    act_slope = 0.5 * (1.0 + tangent) + 0.5 * inputs * (1.0 - tangent * tangent) * gelu_scale * (
        1.0 + 3.0 * cubic_coef * inputs * inputs
    )
    return (act_value, act_slope)


def widen_rows(field_rows, reach_positions):
    return with_halo(field_rows, (("loop", 0),), reach_positions)


def shards(features, kernel_tap_rows, in_weight, out_weight, cotangent):
    middle_position = (TAPS - 1) // 2
    reach_positions = middle_position * DILATION_STEP
    loop_size = lax.axis_size("loop")
    chan_size = lax.axis_size("chan")
    rows_here = features.shape[0]
    grad_scale = 1.0 / math.sqrt(rows_here * loop_size)
    padded_in = widen_rows(features, reach_positions)
    blended_sum = jnp.zeros(features.shape, jnp.float32)
    for kernel_tap_index in range(TAPS):
        leading_row = reach_positions + (kernel_tap_index - middle_position) * DILATION_STEP
        blended_sum = blended_sum + kernel_tap_rows[kernel_tap_index] * padded_in[
            leading_row : leading_row + rows_here
        ].astype(jnp.float32)
    filtered = blended_sum.astype(jnp.bfloat16)
    row_block, upstream = (
        lax.all_to_all(filtered, "chan", split_axis=0, concat_axis=1, tiled=True),
        lax.all_to_all(cotangent, "chan", split_axis=0, concat_axis=1, tiled=True),
    )
    values = row_block.astype(jnp.float32)
    mean_value = jnp.mean(values, axis=-1, keepdims=True)
    centred = values - mean_value
    variance = jnp.mean(centred * centred, axis=-1, keepdims=True)
    inv_std = lax.rsqrt(variance + epsilon)
    normed = centred * inv_std
    normed_b = normed.astype(jnp.bfloat16)
    hidden_pre = jnp.dot(normed_b, in_weight, preferred_element_type=jnp.float32)
    act_value, act_slope = gelu_pair(hidden_pre)
    act_b = act_value.astype(jnp.bfloat16)
    branch = jnp.dot(act_b, out_weight, preferred_element_type=jnp.float32).astype(jnp.bfloat16)
    grad_act = jnp.einsum("pc,fc->pf", upstream, out_weight, preferred_element_type=jnp.float32)
    grad_pre = (grad_act * act_slope).astype(jnp.bfloat16)
    grad_normed = jnp.einsum("pf,cf->pc", grad_pre, in_weight, preferred_element_type=jnp.float32)
    grad_filtered = inv_std * (
        grad_normed
        - jnp.mean(grad_normed, axis=-1, keepdims=True)
        - normed * jnp.mean(grad_normed * normed, axis=-1, keepdims=True)
    )
    back_rows = grad_filtered.astype(jnp.bfloat16)
    local_rows = row_block.shape[0]
    width_c = row_block.shape[1]
    width_f = hidden_pre.shape[1]
    chan_part = width_c // chan_size
    loop_part = width_f // loop_size
    normed_parts = normed_b.reshape(local_rows, chan_size, chan_part)
    upstream_parts = upstream.reshape(local_rows, chan_size, chan_part)
    grad_parts = grad_pre.reshape(local_rows, loop_size, loop_part)
    act_parts = act_b.reshape(local_rows, loop_size, loop_part)
    term_in = (
        jnp.einsum("pai,pbj->baij", normed_parts, grad_parts, preferred_element_type=jnp.float32)
        * grad_scale
    )
    term_out = (
        jnp.einsum("pbj,pai->baji", act_parts, upstream_parts, preferred_element_type=jnp.float32)
        * grad_scale
    )
    branch_cols, back_cols = (
        lax.all_to_all(branch, "chan", split_axis=1, concat_axis=0, tiled=True),
        lax.all_to_all(back_rows, "chan", split_axis=1, concat_axis=0, tiled=True),
    )
    block_out = (features.astype(jnp.float32) + branch_cols.astype(jnp.float32)).astype(
        jnp.bfloat16
    )
    first_in, first_out = (
        lax.psum_scatter(
            term_in.astype(jnp.bfloat16), "chan", scatter_dimension=1, tiled=True
        ).astype(jnp.float32),
        lax.psum_scatter(
            term_out.astype(jnp.bfloat16), "chan", scatter_dimension=1, tiled=True
        ).astype(jnp.float32),
    )
    summed_in, summed_out = (
        lax.psum_scatter(first_in, "loop", scatter_dimension=0, tiled=True),
        lax.psum_scatter(first_out, "loop", scatter_dimension=0, tiled=True),
    )
    grad_in_weight = summed_in.reshape(chan_part, loop_part)
    grad_out_weight = summed_out.reshape(loop_part, chan_part)
    padded_back = widen_rows(back_cols, reach_positions)
    grad_sum_rows = cotangent.astype(jnp.float32)
    back_wide = back_cols.astype(jnp.float32)
    kernel_rows = []
    for kernel_tap_index in range(TAPS):
        shift_positions = (kernel_tap_index - middle_position) * DILATION_STEP
        first_back = reach_positions - shift_positions
        grad_sum_rows = grad_sum_rows + kernel_tap_rows[kernel_tap_index] * padded_back[
            first_back : first_back + rows_here
        ].astype(jnp.float32)
        first_in_row = reach_positions + shift_positions
        kernel_rows.append(
            jnp.sum(
                back_wide * padded_in[first_in_row : first_in_row + rows_here].astype(jnp.float32),
                axis=0,
            )
        )
    kernel_terms = jnp.stack(kernel_rows) * grad_scale
    grad_kernel = lax.psum(kernel_terms, "loop")
    return (
        block_out,
        grad_sum_rows.astype(jnp.bfloat16),
        grad_in_weight,
        grad_out_weight,
        grad_kernel,
    )


MESH = pl.DeviceIdType.MESH
MIDDLE = (TAPS - 1) // 2
HBM = pltpu.MemorySpace.HBM


def fused_kernel(
    L, J, grad_scale,
    x_hbm, ct_hbm, taps_hbm, win_hbm, wout_hbm,
    bo_out, gx_out, gw_in_out, gw_out_out, gk_out,
    xp, ctv, tapv, win, wout, wint, woutt, tf, fb, fr, ctf, nb, nrm, istd, act, gp,
    geb, brb, gep, brv, gfull, gsend, grecv, s1s, s1r, s2s, s2r, uf, sb, tr, gka, kt, kr, acc_x,
    load, send, recv,
):
    cl, rows = ctv.shape
    C, F = win.shape
    B = DILATION_STEP
    K = rows // B
    S = K // 2
    W = 2 * B // J
    V = (J - 1) * cl
    Z = L // 2
    own = MIDDLE * B
    bf, f32 = jnp.bfloat16, jnp.float32
    me_l, me_j = lax.axis_index("loop"), lax.axis_index("chan")
    core, z = lax.rem(me_l, 2), me_l // 2
    ct_r, f_r, ge_r, xh_r, core_r, s1_r, s2_r = [S * i for i in range(7)]
    br_r = 7 * S
    gh_r, z_r, kt_r = br_r + 2, br_r + 4, br_r + 5
    ct_s, f_s, ge_s, br_s, xh_s, gh_s, core_s, s1_s, s2_s, z_s, kt_s = range(11)

    def rcopy(src, dst, out, into, l, j):
        return pltpu.make_async_remote_copy(
            src_ref=src, dst_ref=dst, send_sem=send.at[out], recv_sem=recv.at[into],
            device_id=(l, j), device_id_type=MESH)

    def await_all(like, sem):
        pltpu.make_async_copy(like, like, sem).wait()

    def got(like, into):
        await_all(like, recv.at[into])

    def lanes(at, n):
        return pl.ds(pl.multiple_of(at, 128), n)

    jx = me_j + 1 - 2 * lax.rem(me_j, 2)
    jy = lax.rem(me_j + 2, J)
    jd = lax.rem(jx + 2, J)
    chan_peers = [jd, jx, jy]
    loop_peers = [lax.rem(me_l + e, L) for e in range(1, L)]
    right, left = loop_peers[0], loop_peers[-1]

    barrier = pltpu.get_barrier_semaphore()
    for j in chan_peers:
        pl.semaphore_signal(barrier, inc=1, device_id=(me_l, j), device_id_type=MESH)
    for l in loop_peers:
        pl.semaphore_signal(barrier, inc=1, device_id=(l, me_j), device_id_type=MESH)

    loads = [pltpu.make_async_copy(a, b, load.at[i]) for i, (a, b) in enumerate((
        (x_hbm, xp.at[:, own:own + rows]), (ct_hbm, ctv), (taps_hbm, tapv), (win_hbm, win), (wout_hbm, wout)))]
    for c in loads[:3]:
        c.start()

    half = J // 2
    mine = pl.ds(pl.multiple_of(me_j * cl, cl), cl)

    def col(s, j):
        return lanes((S - 1 - s + (j // half) * (1 + 2 * s)) * B + lax.rem(j, half) * W, W)

    def own_col(s, j):
        return lanes(own + (S - 1 - s + (j // half) * (1 + 2 * s)) * B + lax.rem(j, half) * W, W)

    def block(k):
        return lanes(k * B, B)

    def chan_rows(j):
        return pl.ds(pl.multiple_of(j * cl, cl), cl)

    def ct_copies(s):
        return [rcopy(ct_hbm.at[:, col(s, j)], ctf.at[s, mine, :], ct_s, ct_r + s, me_l, j) for j in chan_peers]

    def f_copies(s):
        return [rcopy(fb.at[:, col(s, j)], fr.at[s, mine, :], f_s, f_r + s, me_l, j) for j in chan_peers]

    def ge_copies(s):
        return [rcopy(geb.at[s, chan_rows(j), :], gep.at[:, own_col(s, me_j)], ge_s, ge_r + s, me_l, j)
                for j in chan_peers]

    def br_copies(s):
        return [rcopy(brb.at[s, chan_rows(j), :], brv.at[:, col(s, me_j)], br_s, br_r + s // (S - 1), me_l, j)
                for j in chan_peers]

    def xh_copies(s):
        return [rcopy(x_hbm.at[:, block(K - 1 - s)], xp.at[:, block(S - 1 - s)], xh_s, xh_r + s, right, me_j),
                rcopy(x_hbm.at[:, block(s)], xp.at[:, block(K + S + s)], xh_s, xh_r + s, left, me_j)]

    def gh_copies(s):
        near, far, into = S - 1 - s, S + s, gh_r + s // (S - 1)
        return [rcopy(gep.at[:, block(far + S)], gep.at[:, block(far - S)], gh_s, into, right, me_j),
                rcopy(gep.at[:, block(near + S)], gep.at[:, block(near + K + S)], gh_s, into, left, me_j)]

    def start(copies):
        for c in copies:
            c.start()

    pl.semaphore_wait(barrier, J - 1 + L - 1)
    start(xh_copies(0))
    start(ct_copies(0))
    for s in range(1, S):
        start(xh_copies(s))
        start(ct_copies(s))
    for c in loads[3:]:
        c.start()
    for c in loads:
        c.wait()
    padded = jnp.concatenate([tapv[...], jnp.zeros((128 - TAPS, cl), f32)], axis=0)
    columns = jnp.concatenate([padded, jnp.zeros((128, 128 - cl), f32)], axis=1).T
    for t in range(TAPS):
        tf[t] = jnp.broadcast_to(columns[0:cl, t:t + 1], (cl, 128))
    wint[...] = win[...].T
    woutt[...] = wout[...].T
    gka[...] = jnp.zeros(gka.shape, f32)
    for s in range(S):
        ctf[s, mine, :] = ctv[:, col(s, me_j)]

    def conv(s):
        near, far = S - 1 - s, S + s

        def part(q, carry):
            done = []
            for g in range(cl // 16):
                ch = slice(g * 16, (g + 1) * 16)
                w = [tf[t, ch, :] for t in range(TAPS)]
                sums = [jnp.zeros((16, 128), f32) for _ in range(2)]
                for b in range(near, far + TAPS):
                    v = xp[ch, lanes(b * B + q * 128, 128)].astype(f32)
                    for i, k in enumerate((near, far)):
                        if 0 <= b - k < TAPS:
                            sums[i] = sums[i] + w[b - k] * v
                done.append([a.astype(bf) for a in sums])
            for g in range(cl // 16):
                for i, k in enumerate((near, far)):
                    fb[g * 16:(g + 1) * 16, lanes(k * B + q * 128, 128)] = done[g][i]
            return carry

        lax.fori_loop(0, B // 128, part, 0)

    for s in range(S):
        got(xp.at[:, 0:2 * B], xh_r + s)
        conv(s)
        start(f_copies(s))
        fr[s, mine, :] = fb[:, col(s, me_j)]

    def mlp_body(s, carry):
        got(ctf.at[s, 0:V, :], ct_r + s)
        got(fr.at[s, 0:V, :], f_r + s)
        here = lanes(s * W, W)
        for b in range(W // 128):
            part = slice(b * 128, (b + 1) * 128)
            v = fr[s, :, part].astype(f32)
            centred = v - jnp.mean(v, axis=0, keepdims=True)
            inv = lax.rsqrt(jnp.mean(centred * centred, axis=0, keepdims=True) + epsilon)
            normed = centred * inv
            nrm[:, part] = normed
            istd[:, part] = inv
            nb[:, lanes(s * W + b * 128, 128)] = normed.astype(bf)
        normed_b = nb[:, here]
        up = ctf[s]
        FC = 256
        for f in range(F // FC):
            part = slice(f * FC, (f + 1) * FC)
            pre = jnp.dot(wint[part, :], normed_b, preferred_element_type=f32)
            ga = jnp.dot(wout[part, :], up, preferred_element_type=f32)
            pre, ga = pre.astype(bf), ga.astype(bf)
            sq = pre * pre
            tangent = jnp.tanh(pre * (gelu_scale + (gelu_scale * cubic_coef) * sq))
            gate = 0.5 + 0.5 * tangent
            slope = gate + pre * (gate * (1.0 - tangent)) * (gelu_scale + (3.0 * gelu_scale * cubic_coef) * sq)
            act[part, here] = pre * gate
            gp[part, here] = ga * slope
        gn = jnp.dot(win[...], gp[:, here], preferred_element_type=f32)
        for b in range(W // 128):
            part = slice(b * 128, (b + 1) * 128)
            g, normed = gn[:, part], nrm[:, part]
            out = istd[:, part] * (g - jnp.mean(g, axis=0, keepdims=True)
                                   - normed * jnp.mean(g * normed, axis=0, keepdims=True))
            geb[s, :, part] = out.astype(bf)
        start(ge_copies(s))
        gep[:, own_col(s, me_j)] = geb[s, mine, :]

        return carry

    lax.fori_loop(0, S, mlp_body, 0)

    def send_branch(s, carry):
        brb[s] = jnp.dot(woutt[...], act[:, lanes(s * W, W)], preferred_element_type=f32).astype(bf)
        brv[:, col(s, me_j)] = brb[s, mine, :]
        start(br_copies(s))
        return carry

    def forward(s):
        got(gep.at[:, 0:(J - 1) * W], ge_r + s)
        start(gh_copies(s))

    def kernel_terms(s):
        near, far = S - 1 - s, S + s
        for g in range(cl // 16):
            ch = slice(g * 16, (g + 1) * 16)
            sums = [gka[t, ch, :] for t in range(TAPS)]
            for q in range(B // 128):
                e = [gep[ch, lanes(own + k * B + q * 128, 128)].astype(f32) for k in (near, far)]
                for b in range(near, far + TAPS):
                    v = xp[ch, lanes(b * B + q * 128, 128)].astype(f32)
                    for i, k in enumerate((near, far)):
                        if 0 <= b - k < TAPS:
                            sums[b - k] = sums[b - k] + e[i] * v
            for t in range(TAPS):
                gka[t, ch, :] = sums[t]

    CR = C // J

    def core_copy(zz):
        return rcopy(gsend.at[1 - core, zz], grecv.at[zz], core_s, core_r + zz, z * 2 + 1 - core, me_j)

    def term_body(e, carry):
        zz = lax.rem(z + 1 + e, Z)
        cols = lanes(zz * 256, 256)
        both = jnp.concatenate([ctf[s] for s in range(S)], axis=1)
        for i, (a, b) in enumerate(((nb[...], gp), (both, act))):
            term = lax.dot_general(a, b[cols, :], (((1,), (1,)), ((), ())), preferred_element_type=f32) * grad_scale
            for h in range(2):
                part = term[:, h * 128:(h + 1) * 128]
                gfull[h, zz, i] = part
                gsend[h, zz, i] = part.astype(bf)
        core_copy(zz).start()

        @pl.when(e == 2)
        def _():
            forward(0)

        @pl.when(e >= 2)
        def _():
            core_sum(e - 2)
        return carry

    def piece(j):
        return pl.ds(pl.multiple_of(j * CR, CR), CR)

    def s1_copies(zz):
        return [rcopy(s1s.at[zz, i], s1r.at[zz, i], s1_s, s1_r + zz, me_l, j) for i, j in enumerate((jx, jy))]

    def s2_copies(zz):
        return [rcopy(s2s.at[zz, i], s2r.at[zz, i], s2_s, s2_r + zz, me_l, j) for i, j in enumerate((jy, jx))]

    def z_copy(e):
        zz = lax.rem(z + 1 + e, Z)
        return rcopy(sb.at[zz], tr.at[z - (z > zz).astype(jnp.int32)], z_s, z_r, zz * 2 + core, me_j)

    def core_sum(e):
        zz = lax.rem(z + 1 + e, Z)
        got(grecv.at[zz], core_r + zz)
        for i, j in enumerate((jx, jy)):
            gfull[core, zz, i] = gfull[core, zz, i] + grecv[zz, i].astype(f32)
            s1s[zz, i, 0] = gfull[core, zz, i, piece(j), :].astype(bf)
            s1s[zz, i, 1] = gfull[core, zz, i, piece(jd), :].astype(bf)
        start(s1_copies(zz))

    def halving(e):
        zz = lax.rem(z + 1 + e, Z)
        got(s1r.at[zz], s1_r + zz)
        for i, j in enumerate((jy, jx)):
            s2s[zz, i] = (gfull[core, zz, i, piece(j), :] + s1r[zz, i, 1].astype(f32)).astype(bf)
            uf[zz, i] = gfull[core, zz, i, piece(me_j), :] + s1r[zz, i, 0].astype(f32)
        start(s2_copies(zz))

    def z_stage(e):
        zz = lax.rem(z + 1 + e, Z)
        got(s2r.at[zz], s2_r + zz)
        total = uf[zz] + s2r[zz].astype(f32)
        uf[zz] = total
        sb[zz] = total.astype(bf)

        if e < Z - 1:
            z_copy(e).start()

    def back(final):
        late = (S - 1, S, S + K - 1, S + K)

        def part(q, carry):
            for g in range(cl // 16):
                ch = slice(g * 16, (g + 1) * 16)
                w = [tf[t, ch, :] for t in range(TAPS)]
                at = [lanes(k * B + q * 128, 128) for k in range(K)]
                sums = [acc_x[ch, a] if final else ctv[ch, a].astype(f32) for a in at]
                for b in range(K + 2 * S):
                    if (b in late) == final:
                        v = gep[ch, lanes(b * B + q * 128, 128)].astype(f32)
                        for t in range(TAPS):
                            k = b - (TAPS - 1 - t)
                            if 0 <= k < K:
                                sums[k] = sums[k] + w[t] * v
                for k in range(K):
                    if final:
                        gx_out[ch, at[k]] = sums[k].astype(bf)
                    else:
                        acc_x[ch, at[k]] = sums[k]
            return carry

        lax.fori_loop(0, B // 128, part, 0)

    lax.fori_loop(0, Z, term_body, 0)
    core_sum(Z - 2)
    core_sum(Z - 1)
    forward(1)
    kernel_terms(0)
    send_branch(0, 0)
    kernel_terms(1)
    forward(2)
    kernel_terms(2)
    forward(3)
    halving(0)
    kernel_terms(3)
    halving(1)
    sums = [jnp.sum(gka[t], axis=1, keepdims=True) * grad_scale for t in range(TAPS)]
    total = jnp.concatenate(sums + [jnp.zeros((cl, 128 - TAPS), f32)], axis=1)
    total = jnp.concatenate([total, jnp.zeros((128 - cl, 128), f32)], axis=0).T
    kt[me_l] = total[0:16]
    start([rcopy(kt.at[me_l], kr.at[me_l - (me_l > l).astype(jnp.int32)], kt_s, kt_r, l, me_j) for l in loop_peers])

    send_branch(1, 0)
    halving(2)
    send_branch(2, 0)
    halving(3)
    send_branch(3, 0)
    got(gep.at[:, 0:(S - 1) * 2 * B], gh_r)
    back(False)
    z_stage(0)
    z_stage(1)
    z_stage(2)
    got(gep.at[:, 0:2 * B], gh_r + 1)
    back(True)
    z_stage(3)

    def finish(k, carry):
        bo_out[:, block(k)] = (xp[:, block(k + S)].astype(f32) + brv[:, block(k)].astype(f32)).astype(bf)
        return carry

    got(brv.at[:, 0:(S - 1) * (J - 1) * W], br_r)
    lax.fori_loop(1, K - 1, finish, 0)
    got(kr, kt_r)
    total = kt[me_l]
    for l in range(L - 1):
        total = total + kr[l]
    gk_out[...] = total[0:TAPS, 0:cl]
    got(tr, z_r)
    total = uf[z]
    for e in range(Z - 1):
        total = total + tr[e].astype(f32)
    gw_in_out[...] = total[0]
    gw_out_out[...] = total[1]
    for like, out in ((ctv.at[:, 0:S * (J - 1) * W], ct_s), (fb.at[:, 0:S * (J - 1) * W], f_s), (geb.at[:, 0:V, :], ge_s),
                      (brb.at[:, 0:V, :], br_s), (xp.at[:, 0:2 * S * B], xh_s), (gep.at[:, 0:2 * S * B], gh_s),
                      (gsend.at[0], core_s), (s1s, s1_s), (s2s, s2_s), (sb.at[0:Z - 1], z_s), (kt.at[0:L - 1], kt_s)):
        await_all(like, send.at[out])
    got(brv.at[:, 0:(J - 1) * W], br_r + 1)
    finish(0, 0)
    finish(K - 1, 0)


def flush_kernel(*refs):
    n = len(refs) // 2
    sems = refs[2 * n]
    copies = [pltpu.make_async_copy(refs[i], refs[n + i], sems.at[i]) for i in range(n)]
    for c in copies:
        c.start()
    for c in copies:
        c.wait()


def fits(L, J, rows, cl, F):
    return (cl * 2 == 128 and rows == 2 * MIDDLE * DILATION_STEP and L % 2 == 0 and L > 2 and J == 4
            and F == L * 128 and L == 2 * MIDDLE)


def fused_shards(features, kernel_tap_rows, in_weight, out_weight, cotangent):
    L, J = lax.axis_size("loop"), lax.axis_size("chan")
    rows, cl = features.shape
    C, F = in_weight.shape
    if not fits(L, J, rows, cl, F):
        return shards(features, kernel_tap_rows, in_weight, out_weight, cotangent)
    N = rows // J
    K = rows // DILATION_STEP
    S = K // 2
    W = N // S
    Z = L // 2
    CR = C // J
    bf, f32 = jnp.bfloat16, jnp.float32
    ext = rows + 2 * MIDDLE * DILATION_STEP
    scratch = [
        pltpu.VMEM((cl, ext), bf),
        pltpu.VMEM((cl, rows), bf),
        pltpu.VMEM((TAPS, cl), f32),
        pltpu.VMEM((C, F), bf),
        pltpu.VMEM((F, C), bf),
        pltpu.VMEM((F, C), bf),
        pltpu.VMEM((C, F), bf),
        pltpu.VMEM((TAPS, cl, 128), f32),
        pltpu.VMEM((cl, rows), bf),
        pltpu.VMEM((S, C, W), bf),
        pltpu.VMEM((S, C, W), bf),
        pltpu.VMEM((C, N), bf),
        pltpu.VMEM((C, W), f32),
        pltpu.VMEM((1, W), f32),
        pltpu.VMEM((F, N), bf),
        pltpu.VMEM((F, N), bf),
        pltpu.VMEM((S, C, W), bf),
        pltpu.VMEM((S, C, W), bf),
        pltpu.VMEM((cl, ext), bf),
        pltpu.VMEM((cl, rows), bf),
        pltpu.VMEM((2, Z, 2, C, 128), f32),
        pltpu.VMEM((2, Z, 2, C, 128), bf),
        pltpu.VMEM((Z, 2, C, 128), bf),
        pltpu.VMEM((Z, 2, 2, CR, 128), bf),
        pltpu.VMEM((Z, 2, 2, CR, 128), bf),
        pltpu.VMEM((Z, 2, CR, 128), bf),
        pltpu.VMEM((Z, 2, CR, 128), bf),
        pltpu.VMEM((Z, 2, CR, 128), f32),
        pltpu.VMEM((Z, 2, CR, 128), bf),
        pltpu.VMEM((Z - 1, 2, CR, 128), bf),
        pltpu.VMEM((TAPS, cl, 128), f32),
        pltpu.VMEM((L, 16, 128), f32),
        pltpu.VMEM((L - 1, 16, 128), f32),
        pltpu.VMEM((cl, rows), f32),
    ]
    scratch += [pltpu.SemaphoreType.DMA((5,)), pltpu.SemaphoreType.DMA((11,)), pltpu.SemaphoreType.DMA((7 * S + 6,))]
    vmem = pl.BlockSpec(memory_space=pltpu.VMEM)
    hbm = pl.BlockSpec(memory_space=HBM)
    shapes = (
        jax.ShapeDtypeStruct((cl, rows), bf),
        jax.ShapeDtypeStruct((cl, rows), bf),
        jax.ShapeDtypeStruct((CR, F // L), f32),
        jax.ShapeDtypeStruct((CR, F // L), f32),
        jax.ShapeDtypeStruct((TAPS, cl), f32),
    )
    results = pl.pallas_call(
        functools.partial(fused_kernel, L, J, 1.0 / math.sqrt(rows * L)),
        out_shape=shapes,
        in_specs=[hbm] * 5,
        out_specs=(vmem,) * 5,
        scratch_shapes=scratch,
        compiler_params=pltpu.CompilerParams(
            collective_id=0, has_side_effects=True, vmem_limit_bytes=50 * 1024 * 1024),
        cost_estimate=pl.CostEstimate(flops=12 * N * C * F, bytes_accessed=8 * rows * cl * 2, transcendentals=N * F),
    )(*[pltpu.with_memory_space_constraint(a, HBM)
        for a in (features.T, cotangent.T, kernel_tap_rows, in_weight, out_weight)])
    bo, gx, gw_in, gw_out, gk = pl.pallas_call(
        flush_kernel,
        out_shape=shapes,
        in_specs=[pl.BlockSpec(memory_space=pl.ANY)] * 5,
        out_specs=(hbm,) * 5,
        scratch_shapes=[pltpu.SemaphoreType.DMA((5,))],
        compiler_params=pltpu.CompilerParams(vmem_limit_bytes=1024 * 1024),
    )(*results)
    return bo.T, gx.T, gw_in, gw_out.T, gk


def solution(mesh):
    placed = (P("loop", "chan"), P(None, "chan"), P(), P(), P("loop", "chan"))
    return jax.shard_map(
        fused_shards,
        mesh=mesh,
        in_specs=placed,
        out_specs=(
            P("loop", "chan"),
            P("loop", "chan"),
            P("chan", "loop"),
            P("loop", "chan"),
            P(None, "chan"),
        ),
        check_vma=False,
    )
```

```python
import functools
import math

import jax
import jax.numpy as jnp
from jax import lax
from jax.experimental import pallas as pl
from jax.experimental.pallas import tpu as pltpu
from jax.sharding import PartitionSpec as P

TAPS = 9
DILATION_STEP = 512


gelu_scale = math.sqrt(2.0 / math.pi)
cubic_coef = 0.044715
epsilon = 1e-05


def with_halo(cells, sides, width):
    for axis, dim in sides:
        count = lax.axis_size(axis)
        head = lax.slice_in_dim(cells, 0, width, axis=dim)
        tail = lax.slice_in_dim(cells, cells.shape[dim] - width, cells.shape[dim], axis=dim)
        cells = jnp.concatenate(
            [
                lax.ppermute(tail, axis, [(i, (i + 1) % count) for i in range(count)]),
                cells,
                lax.ppermute(head, axis, [((i + 1) % count, i) for i in range(count)]),
            ],
            axis=dim,
        )
    return cells


def gelu_pair(inputs):
    inner_arg = gelu_scale * (inputs + cubic_coef * inputs * inputs * inputs)
    tangent = jnp.tanh(inner_arg)
    act_value = 0.5 * inputs * (1.0 + tangent)
    act_slope = 0.5 * (1.0 + tangent) + 0.5 * inputs * (1.0 - tangent * tangent) * gelu_scale * (
        1.0 + 3.0 * cubic_coef * inputs * inputs
    )
    return (act_value, act_slope)


def widen_rows(field_rows, reach_positions):
    return with_halo(field_rows, (("loop", 0),), reach_positions)


def shards(features, kernel_tap_rows, in_weight, out_weight, cotangent):
    middle_position = (TAPS - 1) // 2
    reach_positions = middle_position * DILATION_STEP
    loop_size = lax.axis_size("loop")
    chan_size = lax.axis_size("chan")
    rows_here = features.shape[0]
    grad_scale = 1.0 / math.sqrt(rows_here * loop_size)
    padded_in = widen_rows(features, reach_positions)
    blended_sum = jnp.zeros(features.shape, jnp.float32)
    for kernel_tap_index in range(TAPS):
        leading_row = reach_positions + (kernel_tap_index - middle_position) * DILATION_STEP
        blended_sum = blended_sum + kernel_tap_rows[kernel_tap_index] * padded_in[
            leading_row : leading_row + rows_here
        ].astype(jnp.float32)
    filtered = blended_sum.astype(jnp.bfloat16)
    row_block, upstream = (
        lax.all_to_all(filtered, "chan", split_axis=0, concat_axis=1, tiled=True),
        lax.all_to_all(cotangent, "chan", split_axis=0, concat_axis=1, tiled=True),
    )
    values = row_block.astype(jnp.float32)
    mean_value = jnp.mean(values, axis=-1, keepdims=True)
    centred = values - mean_value
    variance = jnp.mean(centred * centred, axis=-1, keepdims=True)
    inv_std = lax.rsqrt(variance + epsilon)
    normed = centred * inv_std
    normed_b = normed.astype(jnp.bfloat16)
    hidden_pre = jnp.dot(normed_b, in_weight, preferred_element_type=jnp.float32)
    act_value, act_slope = gelu_pair(hidden_pre)
    act_b = act_value.astype(jnp.bfloat16)
    branch = jnp.dot(act_b, out_weight, preferred_element_type=jnp.float32).astype(jnp.bfloat16)
    grad_act = jnp.einsum("pc,fc->pf", upstream, out_weight, preferred_element_type=jnp.float32)
    grad_pre = (grad_act * act_slope).astype(jnp.bfloat16)
    grad_normed = jnp.einsum("pf,cf->pc", grad_pre, in_weight, preferred_element_type=jnp.float32)
    grad_filtered = inv_std * (
        grad_normed
        - jnp.mean(grad_normed, axis=-1, keepdims=True)
        - normed * jnp.mean(grad_normed * normed, axis=-1, keepdims=True)
    )
    back_rows = grad_filtered.astype(jnp.bfloat16)
    local_rows = row_block.shape[0]
    width_c = row_block.shape[1]
    width_f = hidden_pre.shape[1]
    chan_part = width_c // chan_size
    loop_part = width_f // loop_size
    normed_parts = normed_b.reshape(local_rows, chan_size, chan_part)
    upstream_parts = upstream.reshape(local_rows, chan_size, chan_part)
    grad_parts = grad_pre.reshape(local_rows, loop_size, loop_part)
    act_parts = act_b.reshape(local_rows, loop_size, loop_part)
    term_in = (
        jnp.einsum("pai,pbj->baij", normed_parts, grad_parts, preferred_element_type=jnp.float32)
        * grad_scale
    )
    term_out = (
        jnp.einsum("pbj,pai->baji", act_parts, upstream_parts, preferred_element_type=jnp.float32)
        * grad_scale
    )
    branch_cols, back_cols = (
        lax.all_to_all(branch, "chan", split_axis=1, concat_axis=0, tiled=True),
        lax.all_to_all(back_rows, "chan", split_axis=1, concat_axis=0, tiled=True),
    )
    block_out = (features.astype(jnp.float32) + branch_cols.astype(jnp.float32)).astype(
        jnp.bfloat16
    )
    first_in, first_out = (
        lax.psum_scatter(
            term_in.astype(jnp.bfloat16), "chan", scatter_dimension=1, tiled=True
        ).astype(jnp.float32),
        lax.psum_scatter(
            term_out.astype(jnp.bfloat16), "chan", scatter_dimension=1, tiled=True
        ).astype(jnp.float32),
    )
    summed_in, summed_out = (
        lax.psum_scatter(first_in, "loop", scatter_dimension=0, tiled=True),
        lax.psum_scatter(first_out, "loop", scatter_dimension=0, tiled=True),
    )
    grad_in_weight = summed_in.reshape(chan_part, loop_part)
    grad_out_weight = summed_out.reshape(loop_part, chan_part)
    padded_back = widen_rows(back_cols, reach_positions)
    grad_sum_rows = cotangent.astype(jnp.float32)
    back_wide = back_cols.astype(jnp.float32)
    kernel_rows = []
    for kernel_tap_index in range(TAPS):
        shift_positions = (kernel_tap_index - middle_position) * DILATION_STEP
        first_back = reach_positions - shift_positions
        grad_sum_rows = grad_sum_rows + kernel_tap_rows[kernel_tap_index] * padded_back[
            first_back : first_back + rows_here
        ].astype(jnp.float32)
        first_in_row = reach_positions + shift_positions
        kernel_rows.append(
            jnp.sum(
                back_wide * padded_in[first_in_row : first_in_row + rows_here].astype(jnp.float32),
                axis=0,
            )
        )
    kernel_terms = jnp.stack(kernel_rows) * grad_scale
    grad_kernel = lax.psum(kernel_terms, "loop")
    return (
        block_out,
        grad_sum_rows.astype(jnp.bfloat16),
        grad_in_weight,
        grad_out_weight,
        grad_kernel,
    )


MESH = pl.DeviceIdType.MESH
MIDDLE = (TAPS - 1) // 2
HBM = pltpu.MemorySpace.HBM


def fused_kernel(
    L, J, grad_scale,
    x_hbm, ct_hbm, taps_hbm, win_hbm, wout_hbm,
    bo_out, gx_out, gw_in_out, gw_out_out, gk_out,
    xp, ctv, tapv, win, wout, wint, woutt, tf, fb, fr, ctf, nb, nrm, istd, act, gp,
    geb, brb, gep, brv, gfull, gsend, grecv, s1s, s1r, s2s, s2r, uf, sb, tr, gka, kt, kr, acc_x, gab,
    load, send, recv,
):
    cl, rows = ctv.shape
    C, F = win.shape
    B = DILATION_STEP
    K = rows // B
    S = K // 2
    W = 2 * B // J
    V = (J - 1) * cl
    Z = L // 2
    own = MIDDLE * B
    bf, f32 = jnp.bfloat16, jnp.float32
    me_l, me_j = lax.axis_index("loop"), lax.axis_index("chan")
    core, z = lax.rem(me_l, 2), me_l // 2
    ct_r, f_r, ge_r, xh_r, core_r, s1_r, s2_r = [S * i for i in range(7)]
    br_r = 7 * S
    gh_r, z_r, kt_r = br_r + 2, br_r + 4, br_r + 5
    ct_s, f_s, ge_s, br_s, xh_s, gh_s, core_s, s1_s, s2_s, z_s, kt_s = range(11)

    def rcopy(src, dst, out, into, l, j):
        return pltpu.make_async_remote_copy(
            src_ref=src, dst_ref=dst, send_sem=send.at[out], recv_sem=recv.at[into],
            device_id=(l, j), device_id_type=MESH)

    def await_all(like, sem):
        pltpu.make_async_copy(like, like, sem).wait()

    def got(like, into):
        await_all(like, recv.at[into])

    def lanes(at, n):
        return pl.ds(pl.multiple_of(at, 128), n)

    jx = me_j + 1 - 2 * lax.rem(me_j, 2)
    jy = lax.rem(me_j + 2, J)
    jd = lax.rem(jx + 2, J)
    chan_peers = [jd, jx, jy]
    loop_peers = [lax.rem(me_l + e, L) for e in range(1, L)]
    right, left = loop_peers[0], loop_peers[-1]

    barrier = pltpu.get_barrier_semaphore()
    for j in chan_peers:
        pl.semaphore_signal(barrier, inc=1, device_id=(me_l, j), device_id_type=MESH)
    for l in loop_peers:
        pl.semaphore_signal(barrier, inc=1, device_id=(l, me_j), device_id_type=MESH)

    loads = [pltpu.make_async_copy(a, b, load.at[i]) for i, (a, b) in enumerate((
        (x_hbm, xp.at[:, own:own + rows]), (ct_hbm, ctv), (taps_hbm, tapv), (win_hbm, win), (wout_hbm, wout)))]
    for c in loads[:3]:
        c.start()

    half = J // 2
    mine = pl.ds(pl.multiple_of(me_j * cl, cl), cl)

    def col(s, j):
        return lanes((S - 1 - s + (j // half) * (1 + 2 * s)) * B + lax.rem(j, half) * W, W)

    def own_col(s, j):
        return lanes(own + (S - 1 - s + (j // half) * (1 + 2 * s)) * B + lax.rem(j, half) * W, W)

    def block(k):
        return lanes(k * B, B)

    def chan_rows(j):
        return pl.ds(pl.multiple_of(j * cl, cl), cl)

    def ct_copies(s):
        return [rcopy(ct_hbm.at[:, col(s, j)], ctf.at[s, mine, :], ct_s, ct_r + s, me_l, j) for j in chan_peers]

    def f_copies(s):
        return [rcopy(fb.at[:, col(s, j)], fr.at[s, mine, :], f_s, f_r + s, me_l, j) for j in chan_peers]

    def ge_copies(s):
        return [rcopy(geb.at[s, chan_rows(j), :], gep.at[:, own_col(s, me_j)], ge_s, ge_r + s, me_l, j)
                for j in chan_peers]

    def br_copies(s):
        return [rcopy(brb.at[s, chan_rows(j), :], brv.at[:, col(s, me_j)], br_s, br_r + s // (S - 1), me_l, j)
                for j in chan_peers]

    def xh_copies(s):
        return [rcopy(x_hbm.at[:, block(K - 1 - s)], xp.at[:, block(S - 1 - s)], xh_s, xh_r + s, right, me_j),
                rcopy(x_hbm.at[:, block(s)], xp.at[:, block(K + S + s)], xh_s, xh_r + s, left, me_j)]

    def gh_copies(s):
        near, far, into = S - 1 - s, S + s, gh_r + s // (S - 1)
        return [rcopy(gep.at[:, block(far + S)], gep.at[:, block(far - S)], gh_s, into, right, me_j),
                rcopy(gep.at[:, block(near + S)], gep.at[:, block(near + K + S)], gh_s, into, left, me_j)]

    def start(copies):
        for c in copies:
            c.start()

    pl.semaphore_wait(barrier, J - 1 + L - 1)
    start(xh_copies(0))
    start(ct_copies(0))
    for s in range(1, S):
        start(xh_copies(s))
        start(ct_copies(s))
    for c in loads[3:]:
        c.start()
    for c in loads:
        c.wait()
    padded = jnp.concatenate([tapv[...], jnp.zeros((128 - TAPS, cl), f32)], axis=0)
    columns = jnp.concatenate([padded, jnp.zeros((128, 128 - cl), f32)], axis=1).T
    for t in range(TAPS):
        tf[t] = jnp.broadcast_to(columns[0:cl, t:t + 1], (cl, 128))
    wint[...] = win[...].T
    woutt[...] = wout[...].T
    gka[...] = jnp.zeros(gka.shape, f32)
    for s in range(S):
        ctf[s, mine, :] = ctv[:, col(s, me_j)]

    def conv(s):
        near, far = S - 1 - s, S + s

        def part(q, carry):
            done = []
            for g in range(cl // 16):
                ch = slice(g * 16, (g + 1) * 16)
                w = [tf[t, ch, :] for t in range(TAPS)]
                sums = [jnp.zeros((16, 128), f32) for _ in range(2)]
                for b in range(near, far + TAPS):
                    v = xp[ch, lanes(b * B + q * 128, 128)].astype(f32)
                    for i, k in enumerate((near, far)):
                        if 0 <= b - k < TAPS:
                            sums[i] = sums[i] + w[b - k] * v
                done.append([a.astype(bf) for a in sums])
            for g in range(cl // 16):
                for i, k in enumerate((near, far)):
                    fb[g * 16:(g + 1) * 16, lanes(k * B + q * 128, 128)] = done[g][i]
            return carry

        lax.fori_loop(0, B // 128, part, 0)

    for s in range(S):
        got(xp.at[:, 0:2 * B], xh_r + s)
        conv(s)
        start(f_copies(s))
        fr[s, mine, :] = fb[:, col(s, me_j)]

    def mlp_body(s, carry):
        got(ctf.at[s, 0:V, :], ct_r + s)
        gab[...] = jnp.dot(wout[...], ctf[s], preferred_element_type=f32).astype(bf)
        got(fr.at[s, 0:V, :], f_r + s)
        here = lanes(s * W, W)
        for b in range(W // 128):
            part = slice(b * 128, (b + 1) * 128)
            v = fr[s, :, part].astype(f32)
            centred = v - jnp.mean(v, axis=0, keepdims=True)
            inv = lax.rsqrt(jnp.mean(centred * centred, axis=0, keepdims=True) + epsilon)
            normed = centred * inv
            nrm[:, part] = normed
            istd[:, part] = inv
            nb[:, lanes(s * W + b * 128, 128)] = normed.astype(bf)
        normed_b = nb[:, here]
        FC = 256
        for f in range(F // FC):
            part = slice(f * FC, (f + 1) * FC)
            pre = jnp.dot(wint[part, :], normed_b, preferred_element_type=f32)
            pre, ga = pre.astype(bf), gab[part, :]
            sq = pre * pre
            tangent = jnp.tanh(pre * (gelu_scale + (gelu_scale * cubic_coef) * sq))
            gate = 0.5 + 0.5 * tangent
            slope = gate + pre * (gate * (1.0 - tangent)) * (gelu_scale + (3.0 * gelu_scale * cubic_coef) * sq)
            act[part, here] = pre * gate
            gp[part, here] = ga * slope
        gn = jnp.dot(win[...], gp[:, here], preferred_element_type=f32)
        for b in range(W // 128):
            part = slice(b * 128, (b + 1) * 128)
            g, normed = gn[:, part], nrm[:, part]
            out = istd[:, part] * (g - jnp.mean(g, axis=0, keepdims=True)
                                   - normed * jnp.mean(g * normed, axis=0, keepdims=True))
            geb[s, :, part] = out.astype(bf)
        start(ge_copies(s))
        gep[:, own_col(s, me_j)] = geb[s, mine, :]

        return carry

    lax.fori_loop(0, S, mlp_body, 0)

    def send_branch(s, carry):
        brb[s] = jnp.dot(woutt[...], act[:, lanes(s * W, W)], preferred_element_type=f32).astype(bf)
        brv[:, col(s, me_j)] = brb[s, mine, :]
        start(br_copies(s))
        return carry

    def forward(s):
        got(gep.at[:, 0:(J - 1) * W], ge_r + s)
        start(gh_copies(s))

    def kernel_terms(s):
        near, far = S - 1 - s, S + s
        for g in range(cl // 16):
            ch = slice(g * 16, (g + 1) * 16)
            sums = [gka[t, ch, :] for t in range(TAPS)]
            for q in range(B // 128):
                e = [gep[ch, lanes(own + k * B + q * 128, 128)].astype(f32) for k in (near, far)]
                for b in range(near, far + TAPS):
                    v = xp[ch, lanes(b * B + q * 128, 128)].astype(f32)
                    for i, k in enumerate((near, far)):
                        if 0 <= b - k < TAPS:
                            sums[b - k] = sums[b - k] + e[i] * v
            for t in range(TAPS):
                gka[t, ch, :] = sums[t]

    CR = C // J

    def core_copy(zz):
        return rcopy(gsend.at[1 - core, zz], grecv.at[zz], core_s, core_r + zz, z * 2 + 1 - core, me_j)

    def term_body(e, carry):
        zz = lax.rem(z + 1 + e, Z)
        cols = lanes(zz * 256, 256)
        both = jnp.concatenate([ctf[s] for s in range(S)], axis=1)
        for i, (a, b) in enumerate(((nb[...], gp), (both, act))):
            term = lax.dot_general(a, b[cols, :], (((1,), (1,)), ((), ())), preferred_element_type=f32) * grad_scale
            for h in range(2):
                part = term[:, h * 128:(h + 1) * 128]
                gfull[h, zz, i] = part
                gsend[h, zz, i] = part.astype(bf)
        core_copy(zz).start()

        @pl.when(e == 2)
        def _():
            forward(0)

        @pl.when(e >= 2)
        def _():
            core_sum(e - 2)
        return carry

    def piece(j):
        return pl.ds(pl.multiple_of(j * CR, CR), CR)

    def s1_copies(zz):
        return [rcopy(s1s.at[zz, i], s1r.at[zz, i], s1_s, s1_r + zz, me_l, j) for i, j in enumerate((jx, jy))]

    def s2_copies(zz):
        return [rcopy(s2s.at[zz, i], s2r.at[zz, i], s2_s, s2_r + zz, me_l, j) for i, j in enumerate((jy, jx))]

    def z_copy(e):
        zz = lax.rem(z + 1 + e, Z)
        return rcopy(sb.at[zz], tr.at[z - (z > zz).astype(jnp.int32)], z_s, z_r, zz * 2 + core, me_j)

    def core_sum(e):
        zz = lax.rem(z + 1 + e, Z)
        got(grecv.at[zz], core_r + zz)
        for i, j in enumerate((jx, jy)):
            gfull[core, zz, i] = gfull[core, zz, i] + grecv[zz, i].astype(f32)
            s1s[zz, i, 0] = gfull[core, zz, i, piece(j), :].astype(bf)
            s1s[zz, i, 1] = gfull[core, zz, i, piece(jd), :].astype(bf)
        start(s1_copies(zz))

    def halving(e):
        zz = lax.rem(z + 1 + e, Z)
        got(s1r.at[zz], s1_r + zz)
        for i, j in enumerate((jy, jx)):
            s2s[zz, i] = (gfull[core, zz, i, piece(j), :] + s1r[zz, i, 1].astype(f32)).astype(bf)
            uf[zz, i] = gfull[core, zz, i, piece(me_j), :] + s1r[zz, i, 0].astype(f32)
        start(s2_copies(zz))

    def z_stage(e):
        zz = lax.rem(z + 1 + e, Z)
        got(s2r.at[zz], s2_r + zz)
        total = uf[zz] + s2r[zz].astype(f32)
        uf[zz] = total
        sb[zz] = total.astype(bf)

        if e < Z - 1:
            z_copy(e).start()

    def back(final):
        late = (S - 1, S, S + K - 1, S + K)

        def part(q, carry):
            for g in range(cl // 16):
                ch = slice(g * 16, (g + 1) * 16)
                w = [tf[t, ch, :] for t in range(TAPS)]
                at = [lanes(k * B + q * 128, 128) for k in range(K)]
                sums = [acc_x[ch, a] if final else ctv[ch, a].astype(f32) for a in at]
                for b in range(K + 2 * S):
                    if (b in late) == final:
                        v = gep[ch, lanes(b * B + q * 128, 128)].astype(f32)
                        for t in range(TAPS):
                            k = b - (TAPS - 1 - t)
                            if 0 <= k < K:
                                sums[k] = sums[k] + w[t] * v
                for k in range(K):
                    if final:
                        gx_out[ch, at[k]] = sums[k].astype(bf)
                    else:
                        acc_x[ch, at[k]] = sums[k]
            return carry

        lax.fori_loop(0, B // 128, part, 0)

    lax.fori_loop(0, Z, term_body, 0)
    core_sum(Z - 2)
    core_sum(Z - 1)
    forward(1)
    kernel_terms(0)
    send_branch(0, 0)
    kernel_terms(1)
    forward(2)
    kernel_terms(2)
    forward(3)
    halving(0)
    kernel_terms(3)
    halving(1)
    sums = [jnp.sum(gka[t], axis=1, keepdims=True) * grad_scale for t in range(TAPS)]
    total = jnp.concatenate(sums + [jnp.zeros((cl, 128 - TAPS), f32)], axis=1)
    total = jnp.concatenate([total, jnp.zeros((128 - cl, 128), f32)], axis=0).T
    kt[me_l] = total[0:16]
    start([rcopy(kt.at[me_l], kr.at[me_l - (me_l > l).astype(jnp.int32)], kt_s, kt_r, l, me_j) for l in loop_peers])

    send_branch(1, 0)
    halving(2)
    send_branch(2, 0)
    halving(3)
    send_branch(3, 0)
    got(gep.at[:, 0:(S - 1) * 2 * B], gh_r)
    back(False)
    z_stage(0)
    z_stage(1)
    z_stage(2)
    got(gep.at[:, 0:2 * B], gh_r + 1)
    back(True)
    z_stage(3)

    def finish(k, carry):
        bo_out[:, block(k)] = (xp[:, block(k + S)].astype(f32) + brv[:, block(k)].astype(f32)).astype(bf)
        return carry

    got(brv.at[:, 0:(S - 1) * (J - 1) * W], br_r)
    lax.fori_loop(1, K - 1, finish, 0)
    got(kr, kt_r)
    total = kt[me_l]
    for l in range(L - 1):
        total = total + kr[l]
    gk_out[...] = total[0:TAPS, 0:cl]
    got(tr, z_r)
    total = uf[z]
    for e in range(Z - 1):
        total = total + tr[e].astype(f32)
    gw_in_out[...] = total[0]
    gw_out_out[...] = total[1]
    for like, out in ((ctv.at[:, 0:S * (J - 1) * W], ct_s), (fb.at[:, 0:S * (J - 1) * W], f_s), (geb.at[:, 0:V, :], ge_s),
                      (brb.at[:, 0:V, :], br_s), (xp.at[:, 0:2 * S * B], xh_s), (gep.at[:, 0:2 * S * B], gh_s),
                      (gsend.at[0], core_s), (s1s, s1_s), (s2s, s2_s), (sb.at[0:Z - 1], z_s), (kt.at[0:L - 1], kt_s)):
        await_all(like, send.at[out])
    got(brv.at[:, 0:(J - 1) * W], br_r + 1)
    finish(0, 0)
    finish(K - 1, 0)


def flush_kernel(*refs):
    n = len(refs) // 2
    sems = refs[2 * n]
    copies = [pltpu.make_async_copy(refs[i], refs[n + i], sems.at[i]) for i in range(n)]
    for c in copies:
        c.start()
    for c in copies:
        c.wait()


def fits(L, J, rows, cl, F):
    return (cl * 2 == 128 and rows == 2 * MIDDLE * DILATION_STEP and L % 2 == 0 and L > 2 and J == 4
            and F == L * 128 and L == 2 * MIDDLE)


def fused_shards(features, kernel_tap_rows, in_weight, out_weight, cotangent):
    L, J = lax.axis_size("loop"), lax.axis_size("chan")
    rows, cl = features.shape
    C, F = in_weight.shape
    if not fits(L, J, rows, cl, F):
        return shards(features, kernel_tap_rows, in_weight, out_weight, cotangent)
    N = rows // J
    K = rows // DILATION_STEP
    S = K // 2
    W = N // S
    Z = L // 2
    CR = C // J
    bf, f32 = jnp.bfloat16, jnp.float32
    ext = rows + 2 * MIDDLE * DILATION_STEP
    scratch = [
        pltpu.VMEM((cl, ext), bf),
        pltpu.VMEM((cl, rows), bf),
        pltpu.VMEM((TAPS, cl), f32),
        pltpu.VMEM((C, F), bf),
        pltpu.VMEM((F, C), bf),
        pltpu.VMEM((F, C), bf),
        pltpu.VMEM((C, F), bf),
        pltpu.VMEM((TAPS, cl, 128), f32),
        pltpu.VMEM((cl, rows), bf),
        pltpu.VMEM((S, C, W), bf),
        pltpu.VMEM((S, C, W), bf),
        pltpu.VMEM((C, N), bf),
        pltpu.VMEM((C, W), f32),
        pltpu.VMEM((1, W), f32),
        pltpu.VMEM((F, N), bf),
        pltpu.VMEM((F, N), bf),
        pltpu.VMEM((S, C, W), bf),
        pltpu.VMEM((S, C, W), bf),
        pltpu.VMEM((cl, ext), bf),
        pltpu.VMEM((cl, rows), bf),
        pltpu.VMEM((2, Z, 2, C, 128), f32),
        pltpu.VMEM((2, Z, 2, C, 128), bf),
        pltpu.VMEM((Z, 2, C, 128), bf),
        pltpu.VMEM((Z, 2, 2, CR, 128), bf),
        pltpu.VMEM((Z, 2, 2, CR, 128), bf),
        pltpu.VMEM((Z, 2, CR, 128), bf),
        pltpu.VMEM((Z, 2, CR, 128), bf),
        pltpu.VMEM((Z, 2, CR, 128), f32),
        pltpu.VMEM((Z, 2, CR, 128), bf),
        pltpu.VMEM((Z - 1, 2, CR, 128), bf),
        pltpu.VMEM((TAPS, cl, 128), f32),
        pltpu.VMEM((L, 16, 128), f32),
        pltpu.VMEM((L - 1, 16, 128), f32),
        pltpu.VMEM((cl, rows), f32),
        pltpu.VMEM((F, W), bf),
    ]
    scratch += [pltpu.SemaphoreType.DMA((5,)), pltpu.SemaphoreType.DMA((11,)), pltpu.SemaphoreType.DMA((7 * S + 6,))]
    vmem = pl.BlockSpec(memory_space=pltpu.VMEM)
    hbm = pl.BlockSpec(memory_space=HBM)
    shapes = (
        jax.ShapeDtypeStruct((cl, rows), bf),
        jax.ShapeDtypeStruct((cl, rows), bf),
        jax.ShapeDtypeStruct((CR, F // L), f32),
        jax.ShapeDtypeStruct((CR, F // L), f32),
        jax.ShapeDtypeStruct((TAPS, cl), f32),
    )
    results = pl.pallas_call(
        functools.partial(fused_kernel, L, J, 1.0 / math.sqrt(rows * L)),
        out_shape=shapes,
        in_specs=[hbm] * 5,
        out_specs=(vmem,) * 5,
        scratch_shapes=scratch,
        compiler_params=pltpu.CompilerParams(
            collective_id=0, has_side_effects=True, vmem_limit_bytes=50 * 1024 * 1024),
        cost_estimate=pl.CostEstimate(flops=12 * N * C * F, bytes_accessed=8 * rows * cl * 2, transcendentals=N * F),
    )(*[pltpu.with_memory_space_constraint(a, HBM)
        for a in (features.T, cotangent.T, kernel_tap_rows, in_weight, out_weight)])
    bo, gx, gw_in, gw_out, gk = pl.pallas_call(
        flush_kernel,
        out_shape=shapes,
        in_specs=[pl.BlockSpec(memory_space=pl.ANY)] * 5,
        out_specs=(hbm,) * 5,
        scratch_shapes=[pltpu.SemaphoreType.DMA((5,))],
        compiler_params=pltpu.CompilerParams(vmem_limit_bytes=1024 * 1024),
    )(*results)
    return bo.T, gx.T, gw_in, gw_out.T, gk


def solution(mesh):
    placed = (P("loop", "chan"), P(None, "chan"), P(), P(), P("loop", "chan"))
    return jax.shard_map(
        fused_shards,
        mesh=mesh,
        in_specs=placed,
        out_specs=(
            P("loop", "chan"),
            P("loop", "chan"),
            P("chan", "loop"),
            P("loop", "chan"),
            P(None, "chan"),
        ),
        check_vma=False,
    )
```

```python
import functools
import math

import jax
import jax.numpy as jnp
from jax import lax
from jax.experimental import pallas as pl
from jax.experimental.pallas import tpu as pltpu
from jax.sharding import PartitionSpec as P

TAPS = 9
DILATION_STEP = 512


gelu_scale = math.sqrt(2.0 / math.pi)
cubic_coef = 0.044715
epsilon = 1e-05


def with_halo(cells, sides, width):
    for axis, dim in sides:
        count = lax.axis_size(axis)
        head = lax.slice_in_dim(cells, 0, width, axis=dim)
        tail = lax.slice_in_dim(cells, cells.shape[dim] - width, cells.shape[dim], axis=dim)
        cells = jnp.concatenate(
            [
                lax.ppermute(tail, axis, [(i, (i + 1) % count) for i in range(count)]),
                cells,
                lax.ppermute(head, axis, [((i + 1) % count, i) for i in range(count)]),
            ],
            axis=dim,
        )
    return cells


def gelu_pair(inputs):
    inner_arg = gelu_scale * (inputs + cubic_coef * inputs * inputs * inputs)
    tangent = jnp.tanh(inner_arg)
    act_value = 0.5 * inputs * (1.0 + tangent)
    act_slope = 0.5 * (1.0 + tangent) + 0.5 * inputs * (1.0 - tangent * tangent) * gelu_scale * (
        1.0 + 3.0 * cubic_coef * inputs * inputs
    )
    return (act_value, act_slope)


def widen_rows(field_rows, reach_positions):
    return with_halo(field_rows, (("loop", 0),), reach_positions)


def shards(features, kernel_tap_rows, in_weight, out_weight, cotangent):
    middle_position = (TAPS - 1) // 2
    reach_positions = middle_position * DILATION_STEP
    loop_size = lax.axis_size("loop")
    chan_size = lax.axis_size("chan")
    rows_here = features.shape[0]
    grad_scale = 1.0 / math.sqrt(rows_here * loop_size)
    padded_in = widen_rows(features, reach_positions)
    blended_sum = jnp.zeros(features.shape, jnp.float32)
    for kernel_tap_index in range(TAPS):
        leading_row = reach_positions + (kernel_tap_index - middle_position) * DILATION_STEP
        blended_sum = blended_sum + kernel_tap_rows[kernel_tap_index] * padded_in[
            leading_row : leading_row + rows_here
        ].astype(jnp.float32)
    filtered = blended_sum.astype(jnp.bfloat16)
    row_block, upstream = (
        lax.all_to_all(filtered, "chan", split_axis=0, concat_axis=1, tiled=True),
        lax.all_to_all(cotangent, "chan", split_axis=0, concat_axis=1, tiled=True),
    )
    values = row_block.astype(jnp.float32)
    mean_value = jnp.mean(values, axis=-1, keepdims=True)
    centred = values - mean_value
    variance = jnp.mean(centred * centred, axis=-1, keepdims=True)
    inv_std = lax.rsqrt(variance + epsilon)
    normed = centred * inv_std
    normed_b = normed.astype(jnp.bfloat16)
    hidden_pre = jnp.dot(normed_b, in_weight, preferred_element_type=jnp.float32)
    act_value, act_slope = gelu_pair(hidden_pre)
    act_b = act_value.astype(jnp.bfloat16)
    branch = jnp.dot(act_b, out_weight, preferred_element_type=jnp.float32).astype(jnp.bfloat16)
    grad_act = jnp.einsum("pc,fc->pf", upstream, out_weight, preferred_element_type=jnp.float32)
    grad_pre = (grad_act * act_slope).astype(jnp.bfloat16)
    grad_normed = jnp.einsum("pf,cf->pc", grad_pre, in_weight, preferred_element_type=jnp.float32)
    grad_filtered = inv_std * (
        grad_normed
        - jnp.mean(grad_normed, axis=-1, keepdims=True)
        - normed * jnp.mean(grad_normed * normed, axis=-1, keepdims=True)
    )
    back_rows = grad_filtered.astype(jnp.bfloat16)
    local_rows = row_block.shape[0]
    width_c = row_block.shape[1]
    width_f = hidden_pre.shape[1]
    chan_part = width_c // chan_size
    loop_part = width_f // loop_size
    normed_parts = normed_b.reshape(local_rows, chan_size, chan_part)
    upstream_parts = upstream.reshape(local_rows, chan_size, chan_part)
    grad_parts = grad_pre.reshape(local_rows, loop_size, loop_part)
    act_parts = act_b.reshape(local_rows, loop_size, loop_part)
    term_in = (
        jnp.einsum("pai,pbj->baij", normed_parts, grad_parts, preferred_element_type=jnp.float32)
        * grad_scale
    )
    term_out = (
        jnp.einsum("pbj,pai->baji", act_parts, upstream_parts, preferred_element_type=jnp.float32)
        * grad_scale
    )
    branch_cols, back_cols = (
        lax.all_to_all(branch, "chan", split_axis=1, concat_axis=0, tiled=True),
        lax.all_to_all(back_rows, "chan", split_axis=1, concat_axis=0, tiled=True),
    )
    block_out = (features.astype(jnp.float32) + branch_cols.astype(jnp.float32)).astype(
        jnp.bfloat16
    )
    first_in, first_out = (
        lax.psum_scatter(
            term_in.astype(jnp.bfloat16), "chan", scatter_dimension=1, tiled=True
        ).astype(jnp.float32),
        lax.psum_scatter(
            term_out.astype(jnp.bfloat16), "chan", scatter_dimension=1, tiled=True
        ).astype(jnp.float32),
    )
    summed_in, summed_out = (
        lax.psum_scatter(first_in, "loop", scatter_dimension=0, tiled=True),
        lax.psum_scatter(first_out, "loop", scatter_dimension=0, tiled=True),
    )
    grad_in_weight = summed_in.reshape(chan_part, loop_part)
    grad_out_weight = summed_out.reshape(loop_part, chan_part)
    padded_back = widen_rows(back_cols, reach_positions)
    grad_sum_rows = cotangent.astype(jnp.float32)
    back_wide = back_cols.astype(jnp.float32)
    kernel_rows = []
    for kernel_tap_index in range(TAPS):
        shift_positions = (kernel_tap_index - middle_position) * DILATION_STEP
        first_back = reach_positions - shift_positions
        grad_sum_rows = grad_sum_rows + kernel_tap_rows[kernel_tap_index] * padded_back[
            first_back : first_back + rows_here
        ].astype(jnp.float32)
        first_in_row = reach_positions + shift_positions
        kernel_rows.append(
            jnp.sum(
                back_wide * padded_in[first_in_row : first_in_row + rows_here].astype(jnp.float32),
                axis=0,
            )
        )
    kernel_terms = jnp.stack(kernel_rows) * grad_scale
    grad_kernel = lax.psum(kernel_terms, "loop")
    return (
        block_out,
        grad_sum_rows.astype(jnp.bfloat16),
        grad_in_weight,
        grad_out_weight,
        grad_kernel,
    )


MESH = pl.DeviceIdType.MESH
MIDDLE = (TAPS - 1) // 2
HBM = pltpu.MemorySpace.HBM


def fused_kernel(
    L, J, grad_scale,
    x_hbm, ct_hbm, taps_hbm, win_hbm, wout_hbm,
    bo_out, gx_out, gw_in_out, gw_out_out, gk_out,
    xp, ctv, tapv, win, wout, wint, woutt, tf, fb, fr, ctf, nb, nrm, istd, act, gp,
    geb, brb, gep, brv, gfull, gsend, grecv, s1s, s1r, s2s, s2r, uf, sb, tr, gka, kt, kr, acc_x, gab,
    load, send, recv,
):
    cl, rows = ctv.shape
    C, F = win.shape
    B = DILATION_STEP
    K = rows // B
    S = K // 2
    W = 2 * B // J
    V = (J - 1) * cl
    Z = L // 2
    own = MIDDLE * B
    bf, f32 = jnp.bfloat16, jnp.float32
    me_l, me_j = lax.axis_index("loop"), lax.axis_index("chan")
    core, z = lax.rem(me_l, 2), me_l // 2
    ct_r, f_r, ge_r, xh_r, core_r, s1_r, s2_r = [S * i for i in range(7)]
    br_r = 7 * S
    gh_r, z_r, kt_r = br_r + 2, br_r + 4, br_r + 5
    ct_s, f_s, ge_s, br_s, xh_s, gh_s, core_s, s1_s, s2_s, z_s, kt_s = range(11)

    def rcopy(src, dst, out, into, l, j):
        return pltpu.make_async_remote_copy(
            src_ref=src, dst_ref=dst, send_sem=send.at[out], recv_sem=recv.at[into],
            device_id=(l, j), device_id_type=MESH)

    def await_all(like, sem):
        pltpu.make_async_copy(like, like, sem).wait()

    def got(like, into):
        await_all(like, recv.at[into])

    def lanes(at, n):
        return pl.ds(pl.multiple_of(at, 128), n)

    jx = me_j + 1 - 2 * lax.rem(me_j, 2)
    jy = lax.rem(me_j + 2, J)
    jd = lax.rem(jx + 2, J)
    chan_peers = [jd, jx, jy]
    loop_peers = [lax.rem(me_l + e, L) for e in range(1, L)]
    right, left = loop_peers[0], loop_peers[-1]

    barrier = pltpu.get_barrier_semaphore()
    for j in chan_peers:
        pl.semaphore_signal(barrier, inc=1, device_id=(me_l, j), device_id_type=MESH)
    for l in loop_peers:
        pl.semaphore_signal(barrier, inc=1, device_id=(l, me_j), device_id_type=MESH)

    loads = [pltpu.make_async_copy(a, b, load.at[i]) for i, (a, b) in enumerate((
        (x_hbm, xp.at[:, own:own + rows]), (ct_hbm, ctv), (taps_hbm, tapv), (win_hbm, win), (wout_hbm, wout)))]
    for c in loads[:3]:
        c.start()

    half = J // 2
    mine = pl.ds(pl.multiple_of(me_j * cl, cl), cl)

    def col(s, j):
        return lanes((S - 1 - s + (j // half) * (1 + 2 * s)) * B + lax.rem(j, half) * W, W)

    def own_col(s, j):
        return lanes(own + (S - 1 - s + (j // half) * (1 + 2 * s)) * B + lax.rem(j, half) * W, W)

    def block(k):
        return lanes(k * B, B)

    def chan_rows(j):
        return pl.ds(pl.multiple_of(j * cl, cl), cl)

    def ct_copies(s):
        return [rcopy(ct_hbm.at[:, col(s, j)], ctf.at[s, mine, :], ct_s, ct_r + s, me_l, j) for j in chan_peers]

    def f_copies(s):
        return [rcopy(fb.at[:, col(s, j)], fr.at[s, mine, :], f_s, f_r + s, me_l, j) for j in chan_peers]

    def ge_copies(s):
        return [rcopy(geb.at[s, chan_rows(j), :], gep.at[:, own_col(s, me_j)], ge_s, ge_r + s, me_l, j)
                for j in chan_peers]

    def br_copies(s):
        return [rcopy(brb.at[s, chan_rows(j), :], brv.at[:, col(s, me_j)], br_s, br_r + s // (S - 1), me_l, j)
                for j in chan_peers]

    def xh_copies(s):
        return [rcopy(x_hbm.at[:, block(K - 1 - s)], xp.at[:, block(S - 1 - s)], xh_s, xh_r + s, right, me_j),
                rcopy(x_hbm.at[:, block(s)], xp.at[:, block(K + S + s)], xh_s, xh_r + s, left, me_j)]

    def gh_copies(s):
        near, far, into = S - 1 - s, S + s, gh_r + s // (S - 1)
        return [rcopy(gep.at[:, block(far + S)], gep.at[:, block(far - S)], gh_s, into, right, me_j),
                rcopy(gep.at[:, block(near + S)], gep.at[:, block(near + K + S)], gh_s, into, left, me_j)]

    def start(copies):
        for c in copies:
            c.start()

    pl.semaphore_wait(barrier, J - 1 + L - 1)
    start(xh_copies(0))
    start(ct_copies(0))
    for s in range(1, S):
        start(xh_copies(s))
        start(ct_copies(s))
    for c in loads[3:]:
        c.start()
    for c in loads:
        c.wait()
    padded = jnp.concatenate([tapv[...], jnp.zeros((128 - TAPS, cl), f32)], axis=0)
    columns = jnp.concatenate([padded, jnp.zeros((128, 128 - cl), f32)], axis=1).T
    for t in range(TAPS):
        tf[t] = jnp.broadcast_to(columns[0:cl, t:t + 1], (cl, 128))
    wint[...] = win[...].T
    woutt[...] = wout[...].T
    gka[...] = jnp.zeros(gka.shape, f32)
    for s in range(S):
        ctf[s, mine, :] = ctv[:, col(s, me_j)]

    def conv(s):
        near, far = S - 1 - s, S + s

        def part(q, carry):
            done = []
            for g in range(cl // 16):
                ch = slice(g * 16, (g + 1) * 16)
                w = [tf[t, ch, :] for t in range(TAPS)]
                sums = [jnp.zeros((16, 128), f32) for _ in range(2)]
                for b in range(near, far + TAPS):
                    v = xp[ch, lanes(b * B + q * 128, 128)].astype(f32)
                    for i, k in enumerate((near, far)):
                        if 0 <= b - k < TAPS:
                            sums[i] = sums[i] + w[b - k] * v
                done.append([a.astype(bf) for a in sums])
            for g in range(cl // 16):
                for i, k in enumerate((near, far)):
                    fb[g * 16:(g + 1) * 16, lanes(k * B + q * 128, 128)] = done[g][i]
            return carry

        lax.fori_loop(0, B // 128, part, 0)

    for s in range(S):
        got(xp.at[:, 0:2 * B], xh_r + s)
        conv(s)
        start(f_copies(s))
        fr[s, mine, :] = fb[:, col(s, me_j)]

    def mlp_body(s, carry):
        got(ctf.at[s, 0:V, :], ct_r + s)
        gab[...] = jnp.dot(wout[...], ctf[s], preferred_element_type=f32).astype(bf)
        got(fr.at[s, 0:V, :], f_r + s)
        here = lanes(s * W, W)
        for b in range(W // 128):
            part = slice(b * 128, (b + 1) * 128)
            v = fr[s, :, part].astype(f32)
            centred = v - jnp.mean(v, axis=0, keepdims=True)
            inv = lax.rsqrt(jnp.mean(centred * centred, axis=0, keepdims=True) + epsilon)
            normed = centred * inv
            nrm[:, part] = normed
            istd[:, part] = inv
            nb[:, lanes(s * W + b * 128, 128)] = normed.astype(bf)
        normed_b = nb[:, here]
        FC = 512
        for f in range(F // FC):
            part = slice(f * FC, (f + 1) * FC)
            pre = jnp.dot(wint[part, :], normed_b, preferred_element_type=f32)
            pre, ga = pre.astype(bf), gab[part, :]
            sq = pre * pre
            tangent = jnp.tanh(pre * (gelu_scale + (gelu_scale * cubic_coef) * sq))
            gate = 0.5 + 0.5 * tangent
            slope = gate + pre * (gate * (1.0 - tangent)) * (gelu_scale + (3.0 * gelu_scale * cubic_coef) * sq)
            act[part, here] = pre * gate
            gp[part, here] = ga * slope
        gn = jnp.dot(win[...], gp[:, here], preferred_element_type=f32)
        for b in range(W // 128):
            part = slice(b * 128, (b + 1) * 128)
            g, normed = gn[:, part], nrm[:, part]
            out = istd[:, part] * (g - jnp.mean(g, axis=0, keepdims=True)
                                   - normed * jnp.mean(g * normed, axis=0, keepdims=True))
            geb[s, :, part] = out.astype(bf)
        start(ge_copies(s))
        gep[:, own_col(s, me_j)] = geb[s, mine, :]

        return carry

    lax.fori_loop(0, S, mlp_body, 0)

    def send_branch(s, carry):
        brb[s] = jnp.dot(woutt[...], act[:, lanes(s * W, W)], preferred_element_type=f32).astype(bf)
        brv[:, col(s, me_j)] = brb[s, mine, :]
        start(br_copies(s))
        return carry

    def forward(s):
        got(gep.at[:, 0:(J - 1) * W], ge_r + s)
        start(gh_copies(s))

    def kernel_terms(s):
        near, far = S - 1 - s, S + s
        for g in range(cl // 16):
            ch = slice(g * 16, (g + 1) * 16)
            sums = [gka[t, ch, :] for t in range(TAPS)]
            for q in range(B // 128):
                e = [gep[ch, lanes(own + k * B + q * 128, 128)].astype(f32) for k in (near, far)]
                for b in range(near, far + TAPS):
                    v = xp[ch, lanes(b * B + q * 128, 128)].astype(f32)
                    for i, k in enumerate((near, far)):
                        if 0 <= b - k < TAPS:
                            sums[b - k] = sums[b - k] + e[i] * v
            for t in range(TAPS):
                gka[t, ch, :] = sums[t]

    CR = C // J

    def core_copy(zz):
        return rcopy(gsend.at[1 - core, zz], grecv.at[zz], core_s, core_r + zz, z * 2 + 1 - core, me_j)

    def term_body(e, carry):
        zz = lax.rem(z + 1 + e, Z)
        cols = lanes(zz * 256, 256)
        both = jnp.concatenate([ctf[s] for s in range(S)], axis=1)
        for i, (a, b) in enumerate(((nb[...], gp), (both, act))):
            term = lax.dot_general(a, b[cols, :], (((1,), (1,)), ((), ())), preferred_element_type=f32) * grad_scale
            for h in range(2):
                part = term[:, h * 128:(h + 1) * 128]
                gfull[h, zz, i] = part
                gsend[h, zz, i] = part.astype(bf)
        core_copy(zz).start()

        @pl.when(e == 2)
        def _():
            forward(0)

        @pl.when(e >= 2)
        def _():
            core_sum(e - 2)
        return carry

    def piece(j):
        return pl.ds(pl.multiple_of(j * CR, CR), CR)

    def s1_copies(zz):
        return [rcopy(s1s.at[zz, i], s1r.at[zz, i], s1_s, s1_r + zz, me_l, j) for i, j in enumerate((jx, jy))]

    def s2_copies(zz):
        return [rcopy(s2s.at[zz, i], s2r.at[zz, i], s2_s, s2_r + zz, me_l, j) for i, j in enumerate((jy, jx))]

    def z_copy(e):
        zz = lax.rem(z + 1 + e, Z)
        return rcopy(sb.at[zz], tr.at[z - (z > zz).astype(jnp.int32)], z_s, z_r, zz * 2 + core, me_j)

    def core_sum(e):
        zz = lax.rem(z + 1 + e, Z)
        got(grecv.at[zz], core_r + zz)
        for i, j in enumerate((jx, jy)):
            gfull[core, zz, i] = gfull[core, zz, i] + grecv[zz, i].astype(f32)
            s1s[zz, i, 0] = gfull[core, zz, i, piece(j), :].astype(bf)
            s1s[zz, i, 1] = gfull[core, zz, i, piece(jd), :].astype(bf)
        start(s1_copies(zz))

    def halving(e):
        zz = lax.rem(z + 1 + e, Z)
        got(s1r.at[zz], s1_r + zz)
        for i, j in enumerate((jy, jx)):
            s2s[zz, i] = (gfull[core, zz, i, piece(j), :] + s1r[zz, i, 1].astype(f32)).astype(bf)
            uf[zz, i] = gfull[core, zz, i, piece(me_j), :] + s1r[zz, i, 0].astype(f32)
        start(s2_copies(zz))

    def z_stage(e):
        zz = lax.rem(z + 1 + e, Z)
        got(s2r.at[zz], s2_r + zz)
        total = uf[zz] + s2r[zz].astype(f32)
        uf[zz] = total
        sb[zz] = total.astype(bf)

        if e < Z - 1:
            z_copy(e).start()

    def back(final):
        late = (S - 1, S, S + K - 1, S + K)

        def part(q, carry):
            for g in range(cl // 16):
                ch = slice(g * 16, (g + 1) * 16)
                w = [tf[t, ch, :] for t in range(TAPS)]
                at = [lanes(k * B + q * 128, 128) for k in range(K)]
                sums = [acc_x[ch, a] if final else ctv[ch, a].astype(f32) for a in at]
                for b in range(K + 2 * S):
                    if (b in late) == final:
                        v = gep[ch, lanes(b * B + q * 128, 128)].astype(f32)
                        for t in range(TAPS):
                            k = b - (TAPS - 1 - t)
                            if 0 <= k < K:
                                sums[k] = sums[k] + w[t] * v
                for k in range(K):
                    if final:
                        gx_out[ch, at[k]] = sums[k].astype(bf)
                    else:
                        acc_x[ch, at[k]] = sums[k]
            return carry

        lax.fori_loop(0, B // 128, part, 0)

    lax.fori_loop(0, Z, term_body, 0)
    core_sum(Z - 2)
    core_sum(Z - 1)
    forward(1)
    kernel_terms(0)
    send_branch(0, 0)
    kernel_terms(1)
    forward(2)
    kernel_terms(2)
    forward(3)
    halving(0)
    kernel_terms(3)
    halving(1)
    sums = [jnp.sum(gka[t], axis=1, keepdims=True) * grad_scale for t in range(TAPS)]
    total = jnp.concatenate(sums + [jnp.zeros((cl, 128 - TAPS), f32)], axis=1)
    total = jnp.concatenate([total, jnp.zeros((128 - cl, 128), f32)], axis=0).T
    kt[me_l] = total[0:16]
    start([rcopy(kt.at[me_l], kr.at[me_l - (me_l > l).astype(jnp.int32)], kt_s, kt_r, l, me_j) for l in loop_peers])

    send_branch(1, 0)
    halving(2)
    send_branch(2, 0)
    halving(3)
    send_branch(3, 0)
    got(gep.at[:, 0:(S - 1) * 2 * B], gh_r)
    back(False)
    z_stage(0)
    z_stage(1)
    z_stage(2)
    got(gep.at[:, 0:2 * B], gh_r + 1)
    back(True)
    z_stage(3)

    def finish(k, carry):
        bo_out[:, block(k)] = (xp[:, block(k + S)].astype(f32) + brv[:, block(k)].astype(f32)).astype(bf)
        return carry

    got(brv.at[:, 0:(S - 1) * (J - 1) * W], br_r)
    lax.fori_loop(1, K - 1, finish, 0)
    got(kr, kt_r)
    total = kt[me_l]
    for l in range(L - 1):
        total = total + kr[l]
    gk_out[...] = total[0:TAPS, 0:cl]
    got(tr, z_r)
    total = uf[z]
    for e in range(Z - 1):
        total = total + tr[e].astype(f32)
    gw_in_out[...] = total[0]
    gw_out_out[...] = total[1]
    for like, out in ((ctv.at[:, 0:S * (J - 1) * W], ct_s), (fb.at[:, 0:S * (J - 1) * W], f_s), (geb.at[:, 0:V, :], ge_s),
                      (brb.at[:, 0:V, :], br_s), (xp.at[:, 0:2 * S * B], xh_s), (gep.at[:, 0:2 * S * B], gh_s),
                      (gsend.at[0], core_s), (s1s, s1_s), (s2s, s2_s), (sb.at[0:Z - 1], z_s), (kt.at[0:L - 1], kt_s)):
        await_all(like, send.at[out])
    got(brv.at[:, 0:(J - 1) * W], br_r + 1)
    finish(0, 0)
    finish(K - 1, 0)


def flush_kernel(*refs):
    n = len(refs) // 2
    sems = refs[2 * n]
    copies = [pltpu.make_async_copy(refs[i], refs[n + i], sems.at[i]) for i in range(n)]
    for c in copies:
        c.start()
    for c in copies:
        c.wait()


def fits(L, J, rows, cl, F):
    return (cl * 2 == 128 and rows == 2 * MIDDLE * DILATION_STEP and L % 2 == 0 and L > 2 and J == 4
            and F == L * 128 and L == 2 * MIDDLE)


def fused_shards(features, kernel_tap_rows, in_weight, out_weight, cotangent):
    L, J = lax.axis_size("loop"), lax.axis_size("chan")
    rows, cl = features.shape
    C, F = in_weight.shape
    if not fits(L, J, rows, cl, F):
        return shards(features, kernel_tap_rows, in_weight, out_weight, cotangent)
    N = rows // J
    K = rows // DILATION_STEP
    S = K // 2
    W = N // S
    Z = L // 2
    CR = C // J
    bf, f32 = jnp.bfloat16, jnp.float32
    ext = rows + 2 * MIDDLE * DILATION_STEP
    scratch = [
        pltpu.VMEM((cl, ext), bf),
        pltpu.VMEM((cl, rows), bf),
        pltpu.VMEM((TAPS, cl), f32),
        pltpu.VMEM((C, F), bf),
        pltpu.VMEM((F, C), bf),
        pltpu.VMEM((F, C), bf),
        pltpu.VMEM((C, F), bf),
        pltpu.VMEM((TAPS, cl, 128), f32),
        pltpu.VMEM((cl, rows), bf),
        pltpu.VMEM((S, C, W), bf),
        pltpu.VMEM((S, C, W), bf),
        pltpu.VMEM((C, N), bf),
        pltpu.VMEM((C, W), f32),
        pltpu.VMEM((1, W), f32),
        pltpu.VMEM((F, N), bf),
        pltpu.VMEM((F, N), bf),
        pltpu.VMEM((S, C, W), bf),
        pltpu.VMEM((S, C, W), bf),
        pltpu.VMEM((cl, ext), bf),
        pltpu.VMEM((cl, rows), bf),
        pltpu.VMEM((2, Z, 2, C, 128), f32),
        pltpu.VMEM((2, Z, 2, C, 128), bf),
        pltpu.VMEM((Z, 2, C, 128), bf),
        pltpu.VMEM((Z, 2, 2, CR, 128), bf),
        pltpu.VMEM((Z, 2, 2, CR, 128), bf),
        pltpu.VMEM((Z, 2, CR, 128), bf),
        pltpu.VMEM((Z, 2, CR, 128), bf),
        pltpu.VMEM((Z, 2, CR, 128), f32),
        pltpu.VMEM((Z, 2, CR, 128), bf),
        pltpu.VMEM((Z - 1, 2, CR, 128), bf),
        pltpu.VMEM((TAPS, cl, 128), f32),
        pltpu.VMEM((L, 16, 128), f32),
        pltpu.VMEM((L - 1, 16, 128), f32),
        pltpu.VMEM((cl, rows), f32),
        pltpu.VMEM((F, W), bf),
    ]
    scratch += [pltpu.SemaphoreType.DMA((5,)), pltpu.SemaphoreType.DMA((11,)), pltpu.SemaphoreType.DMA((7 * S + 6,))]
    vmem = pl.BlockSpec(memory_space=pltpu.VMEM)
    hbm = pl.BlockSpec(memory_space=HBM)
    shapes = (
        jax.ShapeDtypeStruct((cl, rows), bf),
        jax.ShapeDtypeStruct((cl, rows), bf),
        jax.ShapeDtypeStruct((CR, F // L), f32),
        jax.ShapeDtypeStruct((CR, F // L), f32),
        jax.ShapeDtypeStruct((TAPS, cl), f32),
    )
    results = pl.pallas_call(
        functools.partial(fused_kernel, L, J, 1.0 / math.sqrt(rows * L)),
        out_shape=shapes,
        in_specs=[hbm] * 5,
        out_specs=(vmem,) * 5,
        scratch_shapes=scratch,
        compiler_params=pltpu.CompilerParams(
            collective_id=0, has_side_effects=True, vmem_limit_bytes=50 * 1024 * 1024),
        cost_estimate=pl.CostEstimate(flops=12 * N * C * F, bytes_accessed=8 * rows * cl * 2, transcendentals=N * F),
    )(*[pltpu.with_memory_space_constraint(a, HBM)
        for a in (features.T, cotangent.T, kernel_tap_rows, in_weight, out_weight)])
    bo, gx, gw_in, gw_out, gk = pl.pallas_call(
        flush_kernel,
        out_shape=shapes,
        in_specs=[pl.BlockSpec(memory_space=pl.ANY)] * 5,
        out_specs=(hbm,) * 5,
        scratch_shapes=[pltpu.SemaphoreType.DMA((5,))],
        compiler_params=pltpu.CompilerParams(vmem_limit_bytes=1024 * 1024),
    )(*results)
    return bo.T, gx.T, gw_in, gw_out.T, gk


def solution(mesh):
    placed = (P("loop", "chan"), P(None, "chan"), P(), P(), P("loop", "chan"))
    return jax.shard_map(
        fused_shards,
        mesh=mesh,
        in_specs=placed,
        out_specs=(
            P("loop", "chan"),
            P("loop", "chan"),
            P("chan", "loop"),
            P("loop", "chan"),
            P(None, "chan"),
        ),
        check_vma=False,
    )
```
